32 devices in a mesh: dp: 16 (over z, y, x), fsdp: 2 (over core).
Axes of the slice: x: 2, y: 2, z: 4, core: 2. Of those that a mesh axis runs over, the one named last changes fastest.
Arguments:
- tokens: bfloat16 [32768, 1024], P(('dp', 'fsdp')), may hold values from -6 to 6
- cotangent: bfloat16 [32768, 1024], P(('dp', 'fsdp')), may hold values from -6 to 6
- lengths: int32 [2], replicated, may hold values from 2048 to 16384, as said below
- norm_gain: bfloat16 [1024], P(('dp', 'fsdp')), may hold values from 0.5 to 1.5
- norm_bias: bfloat16 [1024], P(('dp', 'fsdp')), may hold values from -1.25 to 1.25
- w_one: bfloat16 [1024, 3072], P(('dp', 'fsdp')), may hold values from -0.1875 to 0.1875
- b_one: bfloat16 [3072], P(('dp', 'fsdp')), may hold values from -1.25 to 1.25
- w_two: bfloat16 [1024, 512], P(('dp', 'fsdp')), may hold values from -0.1875 to 0.1875
- b_two: bfloat16 [512], P(('dp', 'fsdp')), may hold values from -1.25 to 1.25
- w_three: bfloat16 [512, 3072], P(('dp', 'fsdp')), may hold values from -0.25 to 0.25
- b_three: bfloat16 [3072], P(('dp', 'fsdp')), may hold values from -1.25 to 1.25
- w_four: bfloat16 [3072, 1024], P(('dp', 'fsdp')), may hold values from -0.109375 to 0.109375
- b_four: bfloat16 [1024], P(('dp', 'fsdp')), may hold values from -1.25 to 1.25
- log_rate: float32 [512, 512], P(('dp', 'fsdp')), may hold values from -9 to -3
- ssm_coeff: float32 [512, 512], P(('dp', 'fsdp')), may hold values from -0.009765625 to 0.009765625
- ssm_skip: float32 [512], P(('dp', 'fsdp')), may hold values from 0.5 to 1.5
Outputs:
- mixed: bfloat16 [32768, 1024], P(('dp', 'fsdp'))
- input_grad: bfloat16 [32768, 1024], P(('dp', 'fsdp'))
- grad_norm_gain: float32 [1024], P(('dp', 'fsdp'))
- grad_norm_bias: float32 [1024], P(('dp', 'fsdp'))
- grad_w_one: float32 [1024, 3072], P(('dp', 'fsdp'))
- grad_b_one: float32 [3072], P(('dp', 'fsdp'))
- grad_w_two: float32 [1024, 512], P(('dp', 'fsdp'))
- grad_b_two: float32 [512], P(('dp', 'fsdp'))
- grad_w_three: float32 [512, 3072], P(('dp', 'fsdp'))
- grad_b_three: float32 [3072], P(('dp', 'fsdp'))
- grad_w_four: float32 [3072, 1024], P(('dp', 'fsdp'))
- grad_b_four: float32 [1024], P(('dp', 'fsdp'))
- grad_log_rate: float32 [512, 512], P(('dp', 'fsdp'))
- grad_ssm_coeff: float32 [512, 512], P(('dp', 'fsdp'))
- grad_ssm_skip: float32 [512], P(('dp', 'fsdp'))
The draws below stay inside these ranges and needn't reach their ends.
Inputs may be any that keep to these rules, and one draw needn't show every extreme that they name: `lengths`: every bucket's length is at least 2048; one bucket in every draw holds a full sequence of 16384 tokens.
All inputs are finite; a program needn't handle non-finite values.
Results may differ from the reference program's by a relative error of at most 0.0071.
Values may be sent and summed in bfloat16 or wider, within the bound.
No kernel may reach another device: no remote copies, remote signals or barrier semaphores. Data moves between devices by JAX's collectives and lax.ppermute only.
A program may use at most 192 MiB of HBM per device.

```python
import jax
import jax.numpy as jnp
from jax import lax

E = 1024
F = 3072
H = 512
NSTATE = 512
SEQ = 16384
QBLK = 256
TOKENS = 32768


def draw_lengths(key, part):
    key = jax.random.fold_in(key, 7)
    key_level, key_extra, key_full = jax.random.split(key, 3)
    count = TOKENS // SEQ
    level = jnp.maximum(jax.random.randint(key_level, (count,), 0, 4) - 1, 0)
    base = jnp.right_shift(jnp.full((count,), SEQ, jnp.int32), level + 1)
    extra = jax.random.randint(key_extra, (count,), 0, SEQ + 1) % (base + 1)
    chosen = jax.random.randint(key_full, (), 0, count)
    lengths = jnp.where(jnp.arange(count) == chosen, SEQ, base + extra)
    return lengths.astype(jnp.int32)


def block_levels(key, shape, cuts, smallest, high):
    gain = 1.0
    for axis_at, shards_of in cuts:
        draws = jax.random.uniform(jax.random.fold_in(jax.random.fold_in(key, 6), axis_at), (shards_of,), jnp.float32, smallest / len(cuts), high / len(cuts))
        gain = gain * jnp.repeat(jnp.exp(draws), shape[axis_at] // shards_of).reshape((-1,) + (1,) * (len(shape) - 1 - axis_at))
    return gain


def normal_values(key, dims, scale, limit, cuts=(), held_as=jnp.bfloat16):
    drawn = scale * jax.random.normal(key, dims, jnp.float32)
    if cuts:
        drawn = drawn * block_levels(key, dims, cuts, -0.22, 0.18)
    return jnp.clip(drawn, -limit, limit).astype(held_as)


def setup_inputs(seed: int = 0) -> dict:
    key_of = jax.random.split(jax.random.key(seed), 17)
    tokens = normal_values(key_of[0], (TOKENS, E), 1.0, 6.0, ((0, 32),))
    cotangent = normal_values(key_of[1], (TOKENS, E), 1.0, 6.0, ((0, 32),))
    lengths = draw_lengths(jax.random.fold_in(key_of[16], 71), 0)
    norm_gain = jnp.clip(1.0 + 0.1 * jax.random.normal(key_of[3], (E,), jnp.float32), 0.5, 1.5).astype(jnp.bfloat16)
    norm_bias = normal_values(key_of[4], (E,), 0.2, 1.25, ((0, 32),))
    w_one = normal_values(key_of[5], (E, F), E ** -0.5, 0.1875, ((0, 32),))
    b_one = normal_values(key_of[6], (F,), 0.2, 1.25, ((0, 32),))
    w_two = normal_values(key_of[7], (E, H), E ** -0.5, 0.1875, ((0, 32),))
    b_two = normal_values(key_of[8], (H,), 0.2, 1.25, ((0, 32),))
    w_three = normal_values(key_of[9], (H, F), H ** -0.5, 0.25, ((0, 32),))
    b_three = normal_values(key_of[10], (F,), 0.2, 1.25, ((0, 32),))
    w_four = normal_values(key_of[11], (F, E), F ** -0.5, 0.109375, ((0, 32),))
    b_four = normal_values(key_of[12], (E,), 0.2, 1.25, ((0, 32),))
    log_rate = jnp.clip(-9.0 + 6.0 * jax.random.uniform(key_of[13], (H, NSTATE), jnp.float32) ** block_levels(key_of[13], (H, NSTATE), ((0, 32),), -0.2, 0.2), -9.0, -3.0)
    ssm_coeff = normal_values(key_of[14], (H, NSTATE), (0.04 / NSTATE ** 0.5), 0.009765625, ((0, 32),), jnp.float32)
    ssm_skip = jnp.clip(1.0 + 0.1 * jax.random.normal(key_of[15], (H,), jnp.float32), 0.5, 1.5)
    return dict(tokens=tokens, cotangent=cotangent, lengths=lengths, norm_gain=norm_gain, norm_bias=norm_bias, w_one=w_one, b_one=b_one, w_two=w_two, b_two=b_two, w_three=w_three, b_three=b_three, w_four=w_four, b_four=b_four, log_rate=log_rate, ssm_coeff=ssm_coeff, ssm_skip=ssm_skip)


@jax.custom_vjp
def low(v):
    return lax.optimization_barrier(v.astype(jnp.bfloat16)).astype(jnp.float32)

@jax.custom_vjp
def low_back(v):
    return v

def low_keep(v):
    return (low(v), None)

def low_pass(kept, grad):
    return (grad,)

def back_keep(v):
    return (v, None)

def back_low(kept, grad):
    return (low(grad),)
low.defvjp(low_keep, low_pass)
low_back.defvjp(back_keep, back_low)
HIGH = lax.Precision.HIGHEST

def state_mix(values, log_rate, ssm_coeff, ssm_skip, seq_len, block_len):
    chans, total = values.shape
    nstates = log_rate.shape[1]
    buckets = total // seq_len
    per_seq = seq_len // block_len
    all_blocks = total // block_len
    decay_rate = jnp.exp(log_rate)
    offsets = jnp.arange(block_len, dtype=jnp.int32)
    offsets_f = offsets.astype(jnp.float32)
    decay = jnp.exp(-decay_rate[:, :, None] * offsets_f[None, None, :])
    growth = jnp.exp(decay_rate[:, :, None] * offsets_f[None, None, :])
    weighted = ssm_coeff[:, :, None] * decay
    full_mat = jnp.einsum('hnt,hns->hts', weighted, growth, precision=HIGH)
    lower = offsets[:, None] >= offsets[None, :]
    toeplitz = jnp.where(lower[None], full_mat, 0.0)
    blocks = values.reshape(chans, all_blocks, block_len)
    inner_part = jnp.einsum('hts,hks->hkt', toeplitz, blocks, precision=HIGH)
    block_ends = jnp.einsum('hks,hns->hkn', blocks, decay[:, :, ::-1], precision=HIGH)
    block_ends = jnp.moveaxis(block_ends.reshape(chans, buckets, per_seq, nstates), 2, 0)
    carry_decay = jnp.exp(-decay_rate * block_len)[:, None, :]

    def advance(state_in, contrib):
        return (state_in * carry_decay + contrib, state_in)
    start = jnp.zeros((chans, buckets, nstates), jnp.float32)
    final_state, entering = lax.scan(advance, start, block_ends)
    entering = jnp.moveaxis(entering, 0, 2).reshape(chans, all_blocks, nstates)
    reach = weighted * jnp.exp(-decay_rate)[:, :, None]
    outer_part = jnp.einsum('hkn,hnt->hkt', entering, reach, precision=HIGH)
    mixed_out = (inner_part + outer_part).reshape(chans, total)
    return mixed_out + ssm_skip[:, None] * values

def matmul(left, right):
    return jnp.dot(left, right, precision=HIGH)

def forward(inputs, live, params):
    norm_gain, norm_bias, w_one, b_one, w_two, b_two, w_three, b_three, w_four, b_four, log_rate, ssm_coeff, ssm_skip = params
    center = lax.optimization_barrier(jnp.mean(inputs, axis=-1, keepdims=True))
    centered = inputs - center
    spread = lax.optimization_barrier(jnp.mean(centered * centered, axis=-1, keepdims=True))
    normed = centered * lax.rsqrt(spread + 1e-05) * norm_gain + norm_bias
    normed_bf = low(normed)
    hidden_one = low_back(matmul(normed_bf, w_one) + b_one)
    act_one = jax.nn.gelu(hidden_one, approximate=False)
    hidden_two = low_back(matmul(normed_bf, w_two) + b_two)
    reduced = low_back(low(jax.nn.gelu(hidden_two, approximate=False)))
    mixer_out = state_mix(reduced.T, log_rate, ssm_coeff, ssm_skip, SEQ, QBLK).T
    mixer_bf = low_back(low(mixer_out))
    gate = low_back(matmul(mixer_bf, w_three) + b_three)
    product = low(act_one * gate)
    branch = matmul(product, w_four) + b_four
    return live[:, None] * (inputs + branch)

def reference(tokens, cotangent, lengths, norm_gain, norm_bias, w_one, b_one, w_two, b_two, w_three, b_three, w_four, b_four, log_rate, ssm_coeff, ssm_skip):
    params = (norm_gain.astype(jnp.float32), norm_bias.astype(jnp.float32), w_one.astype(jnp.float32), b_one.astype(jnp.float32), w_two.astype(jnp.float32), b_two.astype(jnp.float32), w_three.astype(jnp.float32), b_three.astype(jnp.float32), w_four.astype(jnp.float32), b_four.astype(jnp.float32), log_rate, ssm_coeff, ssm_skip)
    count = TOKENS // SEQ
    inputs = tokens.astype(jnp.float32).reshape(count, SEQ, E)
    cotans = cotangent.astype(jnp.float32).reshape(count, SEQ, E)
    lives = (jnp.arange(SEQ, dtype=jnp.int32)[None, :] < lengths[:, None]).astype(jnp.float32)

    def one_bucket(totals, item):
        inputs_b, cotan_b, live_b = item
        result, pullback = jax.vjp(lambda xin, prm: forward(xin, live_b, prm), inputs_b, params)
        grad_in, grad_params = pullback(cotan_b)
        totals = jax.tree.map(jnp.add, totals, grad_params)
        return (totals, (result, grad_in))
    zeros = jax.tree.map(jnp.zeros_like, params)
    grads, (results, grad_ins) = lax.scan(one_bucket, zeros, (inputs, cotans, lives))
    mixed = results.reshape(TOKENS, E).astype(jnp.bfloat16)
    input_grad = grad_ins.reshape(TOKENS, E).astype(jnp.bfloat16)
    return (mixed, input_grad, grads[0], grads[1], grads[2], grads[3], grads[4], grads[5], grads[6], grads[7], grads[8], grads[9], grads[10], grads[11], grads[12])
```

```python
import functools

import jax
import jax.numpy as jnp
from jax import lax
from jax.experimental import pallas as pl
from jax.experimental.pallas import tpu as pltpu
from jax.sharding import PartitionSpec as P

SEQ = 16384
QBLK = 256
F32 = jnp.float32
BF = jnp.bfloat16
SWAP = [(0, 1), (1, 0)]


def mm(left, right, left_dim, right_dim):
    return lax.dot_general(
        left, right, (((left_dim,), (right_dim,)), ((), ())), preferred_element_type=F32
    )


def split(value):
    high = value.astype(BF)
    return high, (value - high.astype(F32)).astype(BF)


def decay_table(rate):
    row = lax.broadcasted_iota(jnp.int32, (8, rate.shape[1]), 0).astype(F32)
    table = jnp.exp(-rate * row)
    step = 8
    while step < QBLK:
        table = jnp.concatenate([table, table * jnp.exp(-rate * float(step))], axis=0)
        step *= 2
    return table


def shift_down(x, k):
    if k % 8 == 0:
        return jnp.concatenate([jnp.zeros((k, x.shape[1]), x.dtype), x[:-k]], axis=0)
    row = lax.broadcasted_iota(jnp.int32, x.shape, 0)
    return jnp.where(row >= k, pltpu.roll(x, k, 0), 0.0)


def shift_up(x, k):
    n = x.shape[0]
    if k % 8 == 0:
        return jnp.concatenate([x[k:], jnp.zeros((k, x.shape[1]), x.dtype)], axis=0)
    row = lax.broadcasted_iota(jnp.int32, x.shape, 0)
    return jnp.where(row < n - k, pltpu.roll(x, n - k, 0), 0.0)


def states(x, rate, shift):
    k = 1
    while k < x.shape[0]:
        x = x + shift(x, k) * jnp.exp(-rate * float(QBLK * k))
        k *= 2
    return shift(x, 1)


def flip_matrix():
    i = lax.broadcasted_iota(jnp.int32, (QBLK, QBLK), 0)
    j = lax.broadcasted_iota(jnp.int32, (QBLK, QBLK), 1)
    return jnp.where(i + j == QBLK - 1, 1.0, 0.0).astype(BF)


def toeplitz(kern, skip):
    rolled = pltpu.roll(jnp.broadcast_to(kern, (QBLK, QBLK)), 0, 1, stride=1, stride_axis=0)
    i = lax.broadcasted_iota(jnp.int32, (QBLK, QBLK), 0)
    j = lax.broadcasted_iota(jnp.int32, (QBLK, QBLK), 1)
    return jnp.where(j >= i, rolled, 0.0) + jnp.where(i == j, skip, 0.0)


def far_rows(entering, coeff, d_high, d_low):
    rows = entering.shape[0] + 8
    high, low = split(
        jnp.concatenate([entering, jnp.broadcast_to(coeff, (8, coeff.shape[1]))], axis=0)
    )
    both = mm(jnp.concatenate([high, low], axis=0), d_high, 1, 1)
    return both[:rows] + both[rows:] + mm(high, d_low, 1, 1)


def forward_channel(v, log_rate, coeff, skip, flip):
    count = v.shape[0]
    rate = jnp.exp(log_rate)
    d_high, d_low = split(decay_table(rate))
    v_flip = mm(v, flip, 1, 0).astype(BF)
    ends = mm(v_flip, d_high, 1, 0) + mm(v_flip, d_low, 1, 0)
    entering = states(ends, rate, shift_down)
    far = far_rows(entering * (coeff * jnp.exp(-rate)), coeff, d_high, d_low)
    t_high, t_low = split(toeplitz(far[count : count + 1], skip))
    return far[:count] + mm(v, t_high, 1, 0) + mm(v, t_low, 1, 0)


def forward_kernel(v_ref, lr_ref, co_ref, sk_ref, y_ref):
    flip = flip_matrix()
    for c in range(v_ref.shape[0]):
        y_ref[c] = forward_channel(
            v_ref[c], lr_ref[c], co_ref[c], sk_ref[c][:, :1], flip
        ).astype(BF)


def backward_channel(v, dy, log_rate, coeff, skip, flip):
    count = v.shape[0]
    rate = jnp.exp(log_rate)
    d_high, d_low = split(decay_table(rate))
    flipped = mm(jnp.concatenate([v, dy], axis=0), flip, 1, 0)
    v_flip, dy_flip = flipped[:count].astype(BF), flipped[count:].astype(BF)
    pair = jnp.concatenate([v_flip, dy], axis=0)
    lane = lax.broadcasted_iota(jnp.int32, (count, QBLK), 1).astype(F32)
    v_lag = (flipped[:count] * lane).astype(BF)
    dy_lag = (dy.astype(F32) * lane).astype(BF)
    sums = mm(jnp.concatenate([pair, v_lag, dy_lag], axis=0), d_high, 1, 0)
    lows = mm(pair, d_low, 1, 0)
    ends = sums[:count] + lows[:count]
    starts = sums[count : 2 * count] + lows[count:]
    ends_lag, starts_lag = sums[2 * count : 3 * count], sums[3 * count :]
    entering = states(ends, rate, shift_down)
    leaving = states(starts, rate, shift_up)
    one = jnp.exp(-rate)
    far = far_rows(leaving * (coeff * one), coeff, d_high, d_low)
    t_high, t_low = split(toeplitz(far[count : count + 1], skip))
    dv_flip = far[:count] + mm(dy_flip, t_high, 1, 0) + mm(dy_flip, t_low, 1, 0)
    dv = mm(dv_flip.astype(BF), flip, 1, 0)
    pairs = pltpu.roll(mm(v_flip, dy, 0, 0), 1, 1, stride=1, stride_axis=0)
    i = lax.broadcasted_iota(jnp.int32, (QBLK, QBLK), 0)
    j = lax.broadcasted_iota(jnp.int32, (QBLK, QBLK), 1)
    near = jnp.sum(jnp.where(j <= i, pairs, 0.0), axis=0, keepdims=True)
    lag = lax.broadcasted_iota(jnp.int32, (1, QBLK), 1).astype(F32)
    n_high, n_low = split(
        jnp.concatenate(
            [jnp.broadcast_to(near, (8, QBLK)), jnp.broadcast_to(near * lag, (8, QBLK))], axis=0
        )
    )
    both = mm(jnp.concatenate([n_high, n_low], axis=0), d_high, 1, 0)
    inner = both[:16] + both[16:] + mm(n_high, d_low, 1, 0)
    whole = jnp.exp(-rate * float(QBLK))
    outer = jnp.sum(entering * starts, axis=0, keepdims=True)
    moment = jnp.sum(
        ends_lag * leaving + entering * starts_lag + (float(QBLK) * whole) * (entering * leaving),
        axis=0,
        keepdims=True,
    )
    grad_coeff = inner[0:1] + one * outer
    grad_rate = -(coeff * rate) * (inner[8:9] + one * (moment + outer))
    return dv, grad_rate, grad_coeff, near[:, :1]


def backward_kernel(v_ref, dy_ref, lr_ref, co_ref, sk_ref, dv_ref, gr_ref, gc_ref, gs_ref):
    flip = flip_matrix()
    for c in range(v_ref.shape[0]):
        dv, grad_rate, grad_coeff, grad_skip = backward_channel(
            v_ref[c], dy_ref[c], lr_ref[c], co_ref[c], sk_ref[c][:, :1], flip
        )
        dv_ref[c] = dv.astype(BF)
        gr_ref[c] = grad_rate
        gc_ref[c] = grad_coeff
        gs_ref[c] = jnp.broadcast_to(grad_skip, (1, 128))


def mixer_call(kernel, tokens_in, params, token_outs, grads, name):
    chans, count, _ = tokens_in[0].shape
    per = 4
    n = params[0].shape[2]
    wide = pl.BlockSpec((per, count, QBLK), lambda i: (i, 0, 0))
    row = pl.BlockSpec((per, 1, n), lambda i: (i, 0, 0))
    lane = pl.BlockSpec((per, 1, 128), lambda i: (i, 0, 0))
    out_specs = [wide] * token_outs
    out_shape = [jax.ShapeDtypeStruct((chans, count, QBLK), BF)] * token_outs
    if grads:
        out_specs += [row, row, lane]
        out_shape += [jax.ShapeDtypeStruct((chans, 1, n), F32)] * 2
        out_shape += [jax.ShapeDtypeStruct((chans, 1, 128), F32)]
    return pl.pallas_call(
        kernel,
        grid=(chans // per,),
        in_specs=[wide] * len(tokens_in) + [row, row, lane],
        out_specs=out_specs,
        out_shape=out_shape,
        compiler_params=pltpu.CompilerParams(vmem_limit_bytes=48 * 2**20),
        name=name,
    )(*tokens_in, *params)


def swap_cores(x):
    return lax.ppermute(x, "fsdp", SWAP)


def across(x, size, bit):
    return lax.ppermute(x, "dp", [(i, i ^ (1 << bit)) for i in range(size)])


def bit_of(bit):
    return (lax.axis_index("dp") >> bit) & 1


def gather_bits(x, size, order, layout):
    have = []
    for bit in order:
        other = across(x, size, bit)
        mine = bit_of(bit) == 1
        have = [b for b in layout if b in have or b == bit]
        x = jnp.stack(
            [jnp.where(mine, other, x), jnp.where(mine, x, other)], axis=have.index(bit)
        )
    return x


def scatter_bits(x, size, order, layout, send_type):
    have = list(layout)
    for bit in order:
        axis = have.index(bit)
        mine = bit_of(bit)
        theirs = lax.dynamic_index_in_dim(x, 1 - mine, axis, keepdims=False)
        kept = lax.dynamic_index_in_dim(x, mine, axis, keepdims=False)
        x = kept + across(theirs.astype(send_type), size, bit).astype(F32)
        have.remove(bit)
    return x


def gelu_slope(hidden):
    return (
        0.5 * (1.0 + lax.erf(hidden * 0.7071067811865476))
        + hidden * jnp.exp(-0.5 * hidden * hidden) * 0.3989422804014327
    )


def per_device(
    size,
    tokens,
    cotangent,
    lengths,
    norm_gain,
    norm_bias,
    w_one,
    b_one,
    w_two,
    b_two,
    w_three,
    b_three,
    w_four,
    b_four,
    log_rate,
    ssm_coeff,
    ssm_skip,
):
    bits = size.bit_length() - 1
    tok_dev, width = tokens.shape
    rows_e = w_one.shape[0]
    rows_f = w_four.shape[0]
    rows_h = w_three.shape[0]
    f_half = size * rows_f
    h_half = size * rows_h
    buckets = lengths.shape[0]
    group = size // buckets
    group_bits = group.bit_length() - 1
    natural = list(range(bits))[::-1]
    by_owner = natural[bits - group_bits :] + natural[: bits - group_bits]
    top = natural[: bits - group_bits]
    order_a = list(range(2, bits)) + [0, 1]
    order_b = list(range(2, bits)) + [1, 0]
    core = lax.axis_index("fsdp")
    first = core == 0
    chip = lax.axis_index("dp")

    def natural_pair(mine, other, axis=0):
        return jnp.stack(
            [jnp.where(first, mine, other), jnp.where(first, other, mine)], axis=axis
        )

    def halves_f(x):
        parts = x.reshape(x.shape[:-1] + (size, 2, rows_f))
        a, b = parts[..., 0, :], parts[..., 1, :]
        shape = x.shape[:-1] + (f_half,)
        return (
            jnp.where(first, a, b).reshape(shape),
            jnp.where(first, b, a).reshape(shape),
        )

    def halves_h(x):
        parts = x.reshape(x.shape[:-1] + (buckets, group, 2, rows_h))
        parts = jnp.moveaxis(parts, -4, -3)
        a, b = parts[..., 0, :], parts[..., 1, :]
        shape = x.shape[:-1] + (h_half,)
        return (
            jnp.where(first, a, b).reshape(shape),
            jnp.where(first, b, a).reshape(shape),
        )

    tok_pair = jnp.concatenate([tokens, swap_cores(tokens)], axis=0)
    cot_pair = jnp.concatenate([cotangent, swap_cores(cotangent)], axis=0)

    two_mine, two_other = halves_h(w_two)
    vec = jnp.concatenate([norm_gain, norm_bias, b_four, b_one, b_three, b_two])
    vec_len = vec.shape[0]
    vec_rows = -(-2 * vec_len // h_half)
    two_got, vec_got = swap_cores(two_other), swap_cores(vec)
    two_rows = natural_pair(two_mine, two_got).reshape(2 * rows_e, h_half)
    vec_both = jnp.pad(
        natural_pair(vec, vec_got).reshape(-1), (0, vec_rows * h_half - 2 * vec_len)
    ).reshape(vec_rows, h_half)
    small = gather_bits(
        jnp.concatenate([two_rows, vec_both], axis=0), size, order_a, natural
    ).reshape(size, 2 * rows_e + vec_rows, h_half)
    two_half = small[:, : 2 * rows_e].reshape(width, h_half)
    vecs = (
        small[:, 2 * rows_e :]
        .reshape(size, -1)[:, : 2 * vec_len]
        .reshape(size, 2, vec_len)
        .astype(F32)
    )
    gain_f = vecs[:, :, :rows_e].reshape(1, width)
    nbias_f = vecs[:, :, rows_e : 2 * rows_e].reshape(1, width)
    bfour_f = vecs[:, :, 2 * rows_e : 3 * rows_e].reshape(1, width)
    own_vecs = jnp.where(first, vecs[:, 0], vecs[:, 1])
    bone_f = own_vecs[:, 3 * rows_e : 3 * rows_e + rows_f].reshape(1, f_half)
    bthree_f = own_vecs[:, 3 * rows_e + rows_f : 3 * rows_e + 2 * rows_f].reshape(1, f_half)
    btwo_f = (
        own_vecs[:, 3 * rows_e + 2 * rows_f :]
        .reshape(buckets, group, rows_h)
        .swapaxes(0, 1)
        .reshape(h_half, 1)
    )

    one_mine, one_other = halves_f(w_one)
    three_mine, three_other = halves_f(w_three)
    one_got, three_got = swap_cores(one_other), swap_cores(three_other)
    one_rows = natural_pair(one_mine, one_got)
    one_half = jnp.stack(
        [
            gather_bits(one_rows[0], size, order_a, natural),
            gather_bits(one_rows[1], size, order_b, natural),
        ],
        axis=bits,
    ).reshape(width, f_half)
    three_half = jnp.stack(
        [
            gather_bits(three_mine, size, order_a, by_owner),
            gather_bits(three_got, size, order_b, by_owner),
        ]
    ).reshape(2 * h_half, f_half)
    four_rows = w_four.reshape(2, rows_f // 2, width)
    four_half = jnp.stack(
        [
            gather_bits(four_rows[0], size, order_a, natural),
            gather_bits(four_rows[1], size, order_b, natural),
        ],
        axis=bits,
    ).reshape(f_half, width)

    def shared(x):
        return gather_bits(x, size, sorted(top), top).reshape((buckets * rows_h,) + x.shape[1:])

    params = shared(
        jnp.concatenate(
            [log_rate, ssm_coeff, jnp.broadcast_to(ssm_skip[:, None], (rows_h, 128))], axis=1
        )
    )[:, None]
    nstate = log_rate.shape[1]
    mix_params = (
        params[..., :nstate],
        params[..., nstate : 2 * nstate],
        params[..., 2 * nstate :],
    )
    chans = buckets * rows_h
    tok_chip = 2 * tok_dev
    per_dev = tok_dev // QBLK
    groups = [[b * group + j for j in range(group)] for b in range(buckets)]

    def exchange(x):
        return lax.all_to_all(x, "dp", split_axis=0, concat_axis=0, axis_index_groups=groups)

    def to_owner(x):
        got = exchange(x.reshape(group, chans, tok_chip)).reshape(
            group, chans, 2, per_dev, QBLK
        )
        got = jnp.where(first, got, got[:, :, ::-1])
        return got.swapaxes(0, 1).reshape(chans, group * 2 * per_dev, QBLK)

    def from_owner(x):
        parts = x.reshape(chans, group, 2, per_dev, QBLK).swapaxes(0, 1)
        parts = jnp.where(first, parts, parts[:, :, ::-1])
        return exchange(parts.reshape(group, chans, tok_chip)).reshape(h_half, tok_chip)

    def swap_turned(x):
        got = swap_cores(x)
        return jnp.concatenate([got[:, tok_dev:], got[:, :tok_dev]], axis=1)

    device = 2 * chip + core
    place_own = device * tok_dev + jnp.arange(tok_dev, dtype=jnp.int32)
    place_other = (device ^ 1) * tok_dev + jnp.arange(tok_dev, dtype=jnp.int32)
    place = jnp.concatenate([place_own, place_other])
    bucket_range = jnp.arange(buckets, dtype=jnp.int32)
    limit = jnp.sum(
        jnp.where((place // SEQ)[:, None] == bucket_range[None, :], lengths[None, :], 0), axis=1
    )
    live = (place % SEQ < limit).astype(F32)[:, None]

    inputs = tok_pair.astype(F32)
    centered = inputs - jnp.mean(inputs, axis=-1, keepdims=True)
    inv_std = lax.rsqrt(jnp.mean(centered * centered, axis=-1, keepdims=True) + 1e-05)
    normal_hat = centered * inv_std
    normed = (normal_hat * gain_f + nbias_f).astype(BF)
    out_grad = (live * cot_pair.astype(F32)).astype(BF)
    hidden_two_t = mm(two_half, normed, 0, 1) + btwo_f
    reduced_t = jax.nn.gelu(hidden_two_t, approximate=False).astype(BF)
    v_seq = to_owner(reduced_t)
    (y_seq,) = mixer_call(forward_kernel, [v_seq], mix_params, 1, False, "mixer_forward")
    y_own = from_owner(y_seq)
    y_t = jnp.concatenate([y_own, swap_turned(y_own)], axis=0)

    hidden_one = jnp.dot(normed, one_half, preferred_element_type=F32) + bone_f
    act_one = jax.nn.gelu(hidden_one, approximate=False)
    gate = mm(y_t, three_half, 0, 0) + bthree_f
    product = (act_one * gate).astype(BF)
    grad_four = mm(product, out_grad, 0, 0)
    branch = jnp.dot(product, four_half, preferred_element_type=F32)
    branch_own = branch[:tok_dev] + swap_cores(branch[tok_dev:].astype(BF)).astype(F32)
    mixed = (live[:tok_dev] * (inputs[:tok_dev] + branch_own + bfour_f)).astype(BF)

    prod_grad = mm(out_grad, four_half, 1, 1)
    gate_grad = (prod_grad * act_one).astype(BF)
    dy_part = mm(three_half, gate_grad, 1, 1)
    dy_own = (
        dy_part[:h_half] + swap_turned(dy_part[h_half:].astype(BF)).astype(F32)
    ).astype(BF)
    dy_seq = to_owner(dy_own)
    dv_seq, grad_rate, grad_coeff, grad_skip = mixer_call(
        backward_kernel, [v_seq, dy_seq], mix_params, 1, True, "mixer_backward"
    )
    dv_own = from_owner(dv_seq)
    mix_grads = jnp.concatenate([grad_rate[:, 0], grad_coeff[:, 0], grad_skip[:, 0]], axis=1)
    mix_grads = scatter_bits(
        mix_grads.reshape((2,) * len(top) + (rows_h, -1)), size, sorted(top)[::-1], top, F32
    )

    act_grad = prod_grad * gate
    one_grad = (act_grad * gelu_slope(hidden_one)).astype(BF)
    two_grad_t = (dv_own.astype(F32) * gelu_slope(hidden_two_t)).astype(BF)
    grad_three = mm(y_t, gate_grad, 1, 0)
    grad_one = mm(normed, one_grad, 0, 0)
    grad_two = mm(normed, two_grad_t, 0, 1)
    normed_part = mm(one_grad, one_half, 1, 1) + mm(two_grad_t, two_half, 0, 1)
    normed_grad = normed_part[:tok_dev] + swap_cores(normed_part[tok_dev:].astype(BF)).astype(
        F32
    )
    hat = normal_hat[:tok_dev]
    hat_grad = normed_grad * gain_f
    input_grad = (
        out_grad[:tok_dev].astype(F32)
        + inv_std[:tok_dev]
        * (
            hat_grad
            - jnp.mean(hat_grad, axis=-1, keepdims=True)
            - hat * jnp.mean(hat_grad * hat, axis=-1, keepdims=True)
        )
    ).astype(BF)

    shape_bits = (2,) * bits
    back_a, back_b = order_a[::-1], order_b[::-1]

    def merge_f(mine, other):
        rows = mine.shape[0]
        parts = (mine.reshape(rows, size, rows_f), other.reshape(rows, size, rows_f))
        return natural_pair(*parts, axis=2).reshape(rows, 2 * f_half)

    four_parts = grad_four.reshape(shape_bits + (2, rows_f // 2, width))
    four_a, four_b = four_parts[..., 0, :, :], four_parts[..., 1, :, :]
    sum_four = jnp.concatenate(
        [
            scatter_bits(four_a, size, back_a, natural, BF),
            scatter_bits(four_b, size, back_b, natural, BF),
        ],
        axis=0,
    )
    three_parts = grad_three.reshape((2,) + shape_bits + (rows_h, f_half))
    three_own = scatter_bits(three_parts[0], size, back_a, by_owner, BF)
    three_for = scatter_bits(three_parts[1], size, back_b, by_owner, BF)
    sum_three = merge_f(three_own, swap_cores(three_for))
    one_parts = grad_one.reshape(shape_bits + (2, rows_e, f_half))
    one_a = scatter_bits(one_parts[..., 0, :, :], size, back_a, natural, BF)
    one_b = scatter_bits(one_parts[..., 1, :, :], size, back_b, natural, BF)
    sum_one = merge_f(
        jnp.where(first, one_a, one_b), swap_cores(jnp.where(first, one_b, one_a))
    )

    def chipwise(x):
        return x.reshape(size, -1)

    grad_btwo = (
        jnp.sum(two_grad_t.astype(F32), axis=1)
        .reshape(group, buckets, rows_h)
        .swapaxes(0, 1)
    )
    both_cores = jnp.concatenate(
        [
            chipwise(jnp.sum(normed_grad * hat, axis=0)),
            chipwise(jnp.sum(normed_grad, axis=0)),
            chipwise(jnp.sum(out_grad[:tok_dev].astype(F32), axis=0)),
        ],
        axis=1,
    )
    one_core = jnp.concatenate(
        [
            chipwise(jnp.sum(one_grad.astype(F32), axis=0)),
            chipwise(jnp.sum(gate_grad.astype(F32), axis=0)),
            chipwise(grad_btwo),
        ],
        axis=1,
    )
    vec_grads = jnp.concatenate([both_cores, one_core], axis=1)
    grad_rows = -(-vec_grads.shape[1] // h_half)
    vec_grads = jnp.pad(vec_grads, ((0, 0), (0, grad_rows * h_half - vec_grads.shape[1])))
    small_grads = jnp.concatenate(
        [grad_two.reshape(size, 2 * rows_e, h_half), vec_grads.reshape(size, grad_rows, h_half)],
        axis=1,
    ).reshape(shape_bits + (2 * rows_e + grad_rows, h_half))
    small_sum = scatter_bits(small_grads, size, back_a, natural, BF)
    two_a, two_b = small_sum[:rows_e], small_sum[rows_e : 2 * rows_e]
    vec_sum = small_sum[2 * rows_e :].reshape(-1)
    shared_sum = vec_sum[: 6 * rows_e].reshape(3, 2, rows_e)
    for_me = jnp.where(first, shared_sum[:, 0], shared_sum[:, 1])
    for_other = jnp.where(first, shared_sum[:, 1], shared_sum[:, 0])
    for_me = for_me + swap_cores(for_other)
    own_sum = vec_sum[6 * rows_e :]
    two_mine_sum = jnp.where(first, two_a, two_b)
    two_other_sum = swap_cores(jnp.where(first, two_b, two_a))
    parts = (
        two_mine_sum.reshape(rows_e, group, buckets, rows_h),
        two_other_sum.reshape(rows_e, group, buckets, rows_h),
    )
    sum_two = natural_pair(*parts, axis=3).swapaxes(1, 2).reshape(rows_e, 2 * h_half)

    return (
        mixed,
        input_grad,
        for_me[0],
        for_me[1],
        sum_one,
        own_sum[:rows_f],
        sum_two,
        own_sum[2 * rows_f : 2 * rows_f + rows_h],
        sum_three,
        own_sum[rows_f : 2 * rows_f],
        sum_four,
        for_me[2],
        mix_grads[:, :nstate],
        mix_grads[:, nstate : 2 * nstate],
        mix_grads[:, 2 * nstate],
    )


def solution(mesh):
    both = ("dp", "fsdp")
    rows, vector = P(both, None), P(both)
    in_specs = (
        rows, rows, P(), vector, vector, rows, vector, rows, vector, rows, vector, rows, vector,
        rows, rows, vector,
    )
    out_specs = (
        rows, rows, vector, vector, rows, vector, rows, vector, rows, vector, rows, vector,
        rows, rows, vector,
    )
    return jax.shard_map(
        functools.partial(per_device, mesh.shape["dp"]),
        mesh=mesh,
        in_specs=in_specs,
        out_specs=out_specs,
        check_vma=False,
    )
```

```python
import functools

import jax
import jax.numpy as jnp
from jax import lax
from jax.experimental import pallas as pl
from jax.experimental.pallas import tpu as pltpu
from jax.sharding import PartitionSpec as P

SEQ = 16384
QBLK = 256
F32 = jnp.float32
BF = jnp.bfloat16
SWAP = [(0, 1), (1, 0)]


def mm(left, right, left_dim, right_dim):
    return lax.dot_general(
        left, right, (((left_dim,), (right_dim,)), ((), ())), preferred_element_type=F32
    )


def split(value):
    high = value.astype(BF)
    return high, (value - high.astype(F32)).astype(BF)


def iotas(rows, cols):
    return (
        lax.broadcasted_iota(jnp.int32, (rows, cols), 0),
        lax.broadcasted_iota(jnp.int32, (rows, cols), 1),
    )


def shift_rows(x, k, backward):
    n = x.shape[0]
    row = iotas(*x.shape)[0]
    if backward:
        return jnp.where(row < n - k, pltpu.roll(x, n - k, 0), 0.0)
    return jnp.where(row >= k, pltpu.roll(x, k, 0), 0.0)


def states(x, rate, group, backward):
    blocks = x.shape[0] // group
    order = list(range(blocks))[:: -1 if backward else 1]
    decay = jnp.exp(-rate * float(QBLK))
    local, state = {}, None
    for b in order:
        local[b] = state
        here = x[b * group : (b + 1) * group]
        state = here if state is None else state * decay + here
    k = 1
    while k < group:
        state = state + shift_rows(state, k, backward) * jnp.exp(-rate * float(QBLK * blocks * k))
        k *= 2
    carry = shift_rows(state, 1, backward)
    out = {}
    for step, b in enumerate(order):
        far = carry * jnp.exp(-rate * float(QBLK * step)) if step else carry
        out[b] = far if local[b] is None else far + local[b]
    return jnp.concatenate([out[b] for b in range(blocks)], axis=0)


def flip_matrix():
    i, j = iotas(QBLK, QBLK)
    return jnp.where(i + j == QBLK - 1, 1.0, 0.0).astype(BF)


def base_of(rate):
    return jnp.where(rate * float(QBLK) < 1.0, 1.0, 0.0)


def row_sums(x):
    return jnp.sum(x.astype(F32), axis=1, keepdims=True)


def through(rows, table, base):
    return mm(rows, table, 1, 0) + row_sums(rows) * base


def table_kernel(lr_ref, co_ref, d_ref, dt_ref, t_ref):
    i, j = iotas(QBLK, QBLK)
    for c in range(lr_ref.shape[0]):
        rate, coeff = jnp.exp(lr_ref[c]), co_ref[c]
        row = lax.broadcasted_iota(jnp.int32, (8, rate.shape[1]), 0).astype(F32)
        table = jnp.exp(-rate * row)
        step = 8
        while step < QBLK:
            table = jnp.concatenate([table, table * jnp.exp(-rate * float(step))], axis=0)
            step *= 2
        lowered = table - base_of(rate)
        d_ref[c] = lowered.astype(BF)
        turned = lowered.T
        dt_ref[c] = turned.astype(BF)
        high, low = split(jnp.broadcast_to(coeff, (8, coeff.shape[1])))
        t_high, t_low = split(turned)
        kern = (
            mm(high, t_high, 1, 0) + mm(low, t_high, 1, 0) + mm(high, t_low, 1, 0)
        )[0:1] + row_sums(coeff * base_of(rate))
        rolled = pltpu.roll(jnp.broadcast_to(kern, (QBLK, QBLK)), 0, 1, stride=1, stride_axis=0)
        t_ref[c] = jnp.where(j >= i, rolled, 0.0).astype(BF)


def far_rows(entering, scale, turned, base):
    rows = entering.shape[0]
    scaled = entering * scale
    both = mm(jnp.concatenate(split(scaled), axis=0), turned, 1, 0)
    return both[:rows] + both[rows:] + row_sums(scaled * base)


def lanes_of(b, turn, total):
    start = b * QBLK + turn * (total // 2)
    start = jnp.where(start >= total, start - total, start)
    return pl.ds(pl.multiple_of(start, QBLK), QBLK)


def take_rows(x_ref, rows_ref, turn):
    group, _, total = x_ref.shape
    for b in range(0, total // QBLK, 2):
        pair = [
            jnp.swapaxes(x_ref[:, :, lanes_of(b + k, turn, total)].astype(F32), 0, 1)
            for k in range(2)
        ]
        rows_ref[:, b * group : (b + 2) * group, :] = jnp.concatenate(pair, axis=1).astype(BF)


def give_rows(rows_ref, x_ref, turn):
    group, _, total = x_ref.shape
    for b in range(0, total // QBLK, 2):
        pair = rows_ref[:, b * group : (b + 2) * group, :].astype(F32)
        for k in range(2):
            x_ref[:, :, lanes_of(b + k, turn, total)] = jnp.swapaxes(
                pair[:, k * group : (k + 1) * group], 0, 1
            ).astype(BF)


def forward_kernel(turn_ref, v_ref, d_ref, dt_ref, t_ref, lr_ref, co_ref, sk_ref, y_ref, en_ref, rows_ref, back_ref):
    per, group, turn = d_ref.shape[0], v_ref.shape[0], turn_ref[0]
    part, parts = pl.program_id(1), pl.num_programs(1)
    count = rows_ref.shape[1]

    @pl.when(part == 0)
    def _():
        take_rows(v_ref, rows_ref, turn)

    mine = rows_ref[pl.ds(part * per, per)]
    flipped = mm(mine.reshape(per * count, QBLK), flip_matrix(), 1, 0).astype(BF)
    for c in range(per):
        v = mine[c]
        rate = jnp.exp(lr_ref[c])
        base = base_of(rate)
        ends = through(flipped[c * count : (c + 1) * count], d_ref[c], base)
        entering = states(ends, rate, group, False)
        en_ref[c] = entering
        far = far_rows(entering, co_ref[c] * jnp.exp(-rate), dt_ref[c], base)
        back_ref[part * per + c] = (
            far + mm(v, t_ref[c], 1, 0) + sk_ref[c][:, :1] * v.astype(F32)
        ).astype(BF)

    @pl.when(part == parts - 1)
    def _():
        give_rows(back_ref, y_ref, turn)


def backward_kernel(
    turn_ref, v_ref, dy_ref, en_ref, d_ref, dt_ref, t_ref, lr_ref, co_ref, sk_ref,
    dv_ref, gr_ref, gc_ref, gs_ref, v_rows_ref, dy_rows_ref, back_ref,
):
    per, group, turn = d_ref.shape[0], v_ref.shape[0], turn_ref[0]
    part, parts = pl.program_id(1), pl.num_programs(1)
    count = v_rows_ref.shape[1]
    rows = per * count

    @pl.when(part == 0)
    def _():
        take_rows(v_ref, v_rows_ref, turn)
        take_rows(dy_ref, dy_rows_ref, turn)

    flip = flip_matrix()
    v_all = v_rows_ref[pl.ds(part * per, per)].reshape(rows, QBLK)
    dy_all = dy_rows_ref[pl.ds(part * per, per)].reshape(rows, QBLK)
    flipped = mm(jnp.concatenate([v_all, dy_all], axis=0), flip, 1, 0)
    lane = lax.broadcasted_iota(jnp.int32, (rows, QBLK), 1).astype(F32)
    v_lag = (flipped[:rows] * lane).astype(BF)
    dy_lag = (dy_all.astype(F32) * lane).astype(BF)
    flipped = flipped.astype(BF)
    i, j = iotas(QBLK, QBLK)
    lag = lax.broadcasted_iota(jnp.int32, (1, QBLK), 1).astype(F32)
    back = []
    for c in range(per):
        here = slice(c * count, (c + 1) * count)
        dy = dy_all[here]
        v_flip, dy_flip = flipped[here], flipped[rows + c * count : rows + (c + 1) * count]
        rate, coeff = jnp.exp(lr_ref[c]), co_ref[c]
        base = base_of(rate)
        pairs = pltpu.roll(mm(v_flip, dy, 0, 0), 1, 1, stride=1, stride_axis=0)
        near = jnp.sum(jnp.where(j <= i, pairs, 0.0), axis=0, keepdims=True)
        near_rows = jnp.concatenate(
            split(
                jnp.concatenate(
                    [jnp.broadcast_to(near, (8, QBLK)), jnp.broadcast_to(near * lag, (8, QBLK))],
                    axis=0,
                )
            ),
            axis=0,
        )
        sums = through(
            jnp.concatenate([dy, dy_lag[here], v_lag[here], near_rows], axis=0), d_ref[c], base
        )
        starts, starts_lag, ends_lag = (sums[k * count : (k + 1) * count] for k in range(3))
        inner = sums[3 * count : 3 * count + 16] + sums[3 * count + 16 :]
        leaving = states(starts, rate, group, True)
        entering = en_ref[c]
        one = jnp.exp(-rate)
        far = far_rows(leaving, coeff * one, dt_ref[c], base)
        back.append(
            (
                far + mm(dy_flip, t_ref[c], 1, 0) + sk_ref[c][:, :1] * dy_flip.astype(F32)
            ).astype(BF)
        )
        whole = jnp.exp(-rate * float(QBLK))
        outer = jnp.sum(entering * starts, axis=0, keepdims=True)
        moment = jnp.sum(
            ends_lag * leaving + entering * (starts_lag + (float(QBLK) * whole) * leaving),
            axis=0,
            keepdims=True,
        )
        gc_ref[c] = inner[0:1] + one * outer
        gr_ref[c] = -(coeff * rate) * (inner[8:9] + one * (moment + outer))
        gs_ref[c] = jnp.broadcast_to(near[:, :1], (1, 128))
    turned = mm(jnp.concatenate(back, axis=0), flip, 1, 0).astype(BF)
    back_ref[pl.ds(part * per, per)] = turned.reshape(per, count, QBLK)

    @pl.when(part == parts - 1)
    def _():
        give_rows(back_ref, dv_ref, turn)


def mixer_tables(log_rate, coeff):
    chans, _, n = log_rate.shape
    per = 4

    def spec(rows, cols):
        return pl.BlockSpec((per, rows, cols), lambda i: (i, 0, 0))

    shapes = [(QBLK, n), (n, QBLK), (QBLK, QBLK)]
    return pl.pallas_call(
        table_kernel,
        grid=(chans // per,),
        in_specs=[spec(1, n)] * 2,
        out_specs=[spec(*shape) for shape in shapes],
        out_shape=[jax.ShapeDtypeStruct((chans,) + shape, BF) for shape in shapes],
        compiler_params=pltpu.CompilerParams(vmem_limit_bytes=32 * 2**20),
        name="mixer_tables",
    )(log_rate, coeff)


def mixer_call(kernel, turn, tokens_in, by_channel, outs, name):
    group, chans, total = tokens_in[0].shape
    tall, per = 16, 8
    parts = tall // per
    count = group * (total // QBLK)

    def spec(shape):
        return pl.BlockSpec((per,) + tuple(shape[1:]), lambda i, j, *_: (i * parts + j, 0, 0))

    wide = pl.BlockSpec((group, tall, total), lambda i, j, *_: (0, i, 0))
    return pl.pallas_call(
        kernel,
        grid_spec=pltpu.PrefetchScalarGridSpec(
            num_scalar_prefetch=1,
            grid=(chans // tall, parts),
            in_specs=[wide] * len(tokens_in) + [spec(x.shape) for x in by_channel],
            out_specs=[wide] + [spec(shape) for shape, _ in outs],
            scratch_shapes=[pltpu.VMEM((tall, count, QBLK), BF)] * (len(tokens_in) + 1),
        ),
        out_shape=[jax.ShapeDtypeStruct((group, chans, total), BF)]
        + [jax.ShapeDtypeStruct(shape, kind) for shape, kind in outs],
        compiler_params=pltpu.CompilerParams(vmem_limit_bytes=40 * 2**20),
        name=name,
    )(turn, *tokens_in, *by_channel)


def mixer_forward(turn, v, tables, params):
    group, chans, total = v.shape
    n = params[0].shape[2]
    states_of = (chans, group * (total // QBLK), n)
    return mixer_call(
        forward_kernel, turn, [v], [*tables, *params], [(states_of, F32)], "mixer_forward"
    )


def mixer_backward(turn, v, dy, entering, tables, params):
    chans, n = v.shape[1], params[0].shape[2]
    return mixer_call(
        backward_kernel,
        turn,
        [v, dy],
        [entering, *tables, *params],
        [((chans, 1, n), F32), ((chans, 1, n), F32), ((chans, 1, 128), F32)],
        "mixer_backward",
    )


TILE = 512


def call(kernel, grid, core, ins, outs, name, room=24):
    return pl.pallas_call(
        kernel,
        grid_spec=pltpu.PrefetchScalarGridSpec(
            num_scalar_prefetch=1,
            grid=(grid,),
            in_specs=[
                pl.BlockSpec(block, index, pipeline_mode=None if index in MOVING else pl.Buffered(1))
                for _, block, index in ins
            ],
            out_specs=[pl.BlockSpec(block, index) for _, _, block, index in outs],
        ),
        out_shape=[jax.ShapeDtypeStruct(shape, kind) for shape, kind, _, _ in outs],
        compiler_params=pltpu.CompilerParams(vmem_limit_bytes=room * 2**20),
        cost_estimate=pl.CostEstimate(flops=0, bytes_accessed=0, transcendentals=0),
        name=name,
    )(core, *[array for array, _, _ in ins])


def row_tile(m, _):
    return (m, 0)


def col_tile(m, _):
    return (0, m)


def turned_tile(m, _):
    half = pl.num_programs(0) // 2
    return (0, jnp.where(m < half, m + half, m - half))


def fixed(m, _):
    return (0, 0)


MOVING = (row_tile, col_tile, turned_tile)


def first_rows(m, _):
    return (jnp.minimum(m, pl.num_programs(0) // 2 - 1), 0)


def last_rows(m, _):
    return (jnp.maximum(m - pl.num_programs(0) // 2, 0), 0)


def strips_of(start, stop, strip):
    while start < stop:
        k = start // strip
        end = min(stop, (k + 1) * strip)
        yield k, slice(start - k * strip, end - k * strip)
        start = end


def strip_columns(ref, strips, start, stop, order):
    rows = ref.shape[2] // strips
    return jnp.concatenate(
        [
            jnp.concatenate(
                [
                    ref[chip, core, k * rows : (k + 1) * rows, lanes]
                    for chip in order
                    for core in range(ref.shape[1])
                ],
                axis=0,
            )
            for k, lanes in strips_of(start, stop, ref.shape[3])
        ],
        axis=1,
    )


def strip_rows(ref, strips, start, stop):
    rows = ref.shape[2] // strips
    return jnp.concatenate(
        [
            jnp.concatenate(
                [
                    ref[chip, 0, k * rows + part.start : k * rows + part.stop, :]
                    for chip, part in strips_of(start, stop, rows)
                ],
                axis=0,
            )
            for k in range(strips)
        ],
        axis=1,
    )


def col_sum(x):
    return jnp.sum(x.astype(F32), axis=0, keepdims=True)


def hat_of(x):
    x = x.astype(F32)
    centered = x - jnp.mean(x, axis=-1, keepdims=True)
    inv_std = lax.rsqrt(jnp.mean(centered * centered, axis=-1, keepdims=True) + 1e-05)
    return centered * inv_std, inv_std


def slope_and_gelu(h):
    phi = 0.5 + 0.5 * lax.erf(h * 0.7071067811865476)
    return h * phi, phi + h * jnp.exp(-0.5 * h * h) * 0.3989422804014327


def norm_kernel(
    _, tok_ref, cot_ref, live_ref, gain_ref, bias_ref, w_ref, b_ref, n_ref, g_ref, v_ref, s_ref, sum_ref
):
    m = pl.program_id(0)

    @pl.when(m == 0)
    def _():
        sum_ref[...] = jnp.zeros_like(sum_ref)

    hat, _ = hat_of(tok_ref[...])
    normed = (hat * gain_ref[...] + bias_ref[...]).astype(BF)
    n_ref[...] = normed
    g = jnp.where(live_ref[...][:, :1] > 0.0, cot_ref[...], jnp.zeros((), BF))
    g_ref[...] = g

    @pl.when(m < pl.num_programs(0) // 2)
    def _():
        sum_ref[...] += col_sum(g)

    v, s = slope_and_gelu(mm(w_ref[...], normed, 1, 1) + b_ref[...][:, :1])
    v_ref[...] = v.astype(BF)
    s_ref[...] = s.astype(BF)


def norm_call(core, tok, cot, live, gain, bias, w_turned, b):
    tokens, width = tok.shape
    chans = w_turned.shape[0]
    rows, cols = (TILE, width), (chans, TILE)
    return call(
        norm_kernel,
        tokens // TILE,
        core,
        [
            (tok, rows, row_tile),
            (cot, rows, row_tile),
            (live, (TILE, 128), row_tile),
            (gain, (1, width), fixed),
            (bias, (1, width), fixed),
            (w_turned, (chans, width), fixed),
            (b, (chans, 128), fixed),
        ],
        [((tokens, width), BF, rows, row_tile)] * 2
        + [((chans, tokens), BF, cols, col_tile)] * 2
        + [((1, width), F32, (1, width), fixed)],
        "norm",
    )


def early_kernel(
    _, x_ref, g_ref, b1_ref, w1_ref, w4_ref, w3m_ref, w3o_ref,
    u_ref, dzs_ref, dgate_ref, mine_ref, other_ref, sum_ref, *, order,
):
    total = u_ref.shape[1]
    cols, strips = 384, total // w1_ref.shape[3]
    chips = range(w1_ref.shape[0])
    e_strips = g_ref.shape[1] // w4_ref.shape[3]

    @pl.when(pl.program_id(0) == 0)
    def _():
        sum_ref[...] = jnp.zeros_like(sum_ref)

    for n in range(total // cols):
        at = slice(n * cols, (n + 1) * cols)
        w1 = strip_columns(w1_ref, strips, at.start, at.stop, chips)
        u, s = slope_and_gelu(mm(x_ref[...], w1, 1, 0) + b1_ref[:, at])
        dz = mm(g_ref[...], strip_rows(w4_ref, e_strips, at.start, at.stop), 1, 1)
        dgate = (dz * u).astype(BF)
        u_ref[:, at] = u.astype(BF)
        dzs_ref[:, at] = (dz * s).astype(BF)
        dgate_ref[:, at] = dgate
        sum_ref[:, at] += col_sum(dgate)
    mine_ref[...] = mm(strip_columns(w3m_ref, strips, 0, total, order), dgate_ref[...], 1, 1)
    other = mm(strip_columns(w3o_ref, strips, 0, total, order), dgate_ref[...], 1, 1)
    other_ref[...] = other.astype(BF)


def early_call(core, x, g, b1, weights, order):
    tokens, width = x.shape
    cols = b1.shape[1]
    chans = weights[2][1][2] * weights[2][1][3] * len(order) // cols
    wide, tall = (TILE, cols), (chans, TILE)
    return call(
        functools.partial(early_kernel, order=order),
        tokens // TILE,
        core,
        [
            (x, (TILE, width), row_tile),
            (g, (TILE, width), row_tile),
            (b1, (1, cols), fixed),
            *weights,
        ],
        [((tokens, cols), BF, wide, row_tile)] * 3
        + [
            ((chans, tokens), F32, tall, col_tile),
            ((chans, tokens), BF, tall, turned_tile),
            ((1, cols), F32, (1, cols), fixed),
        ],
        "early",
        40,
    )


def late_kernel(
    _, ym_ref, yo_ref, b3_ref, u_ref, dzs_ref, w1_ref, w4_ref, w3m_ref, w3o_ref,
    z_ref, dh_ref, om_ref, oo_ref, p_ref, sum_ref, *, order,
):
    m, total = pl.program_id(0), u_ref.shape[1]
    cols, strips = 256, total // w1_ref.shape[3]
    chips = range(w1_ref.shape[0])
    e_strips = om_ref.shape[1] // w4_ref.shape[3]

    @pl.when(m == 0)
    def _():
        sum_ref[...] = jnp.zeros_like(sum_ref)

    y = jnp.concatenate([ym_ref[...], yo_ref[...]], axis=0).T
    for n in range(total // cols):
        at = slice(n * cols, (n + 1) * cols)
        w3 = jnp.concatenate(
            [strip_columns(ref, strips, at.start, at.stop, order) for ref in (w3m_ref, w3o_ref)],
            axis=0,
        )
        gate = mm(y, w3, 1, 0) + b3_ref[:, at]
        z_ref[:, at] = (u_ref[:, at].astype(F32) * gate).astype(BF)
        dh = (dzs_ref[:, at].astype(F32) * gate).astype(BF)
        dh_ref[:, at] = dh
        sum_ref[:, at] += col_sum(dh)
    p_ref[...] = mm(dh_ref[...], strip_columns(w1_ref, strips, 0, total, chips), 1, 1).astype(BF)
    out = mm(z_ref[...], strip_rows(w4_ref, e_strips, 0, total), 1, 0)

    @pl.when(m < pl.num_programs(0) // 2)
    def _():
        om_ref[...] = out

    @pl.when(m >= pl.num_programs(0) // 2)
    def _():
        oo_ref[...] = out.astype(BF)


def late_call(core, y_mine, y_other, b3, u, dzs, width, weights, order):
    tokens, cols = u.shape
    wide, tall = (TILE, cols), (y_mine.shape[0], TILE)
    rows = (TILE, width)
    return call(
        functools.partial(late_kernel, order=order),
        tokens // TILE,
        core,
        [
            (y_mine, tall, col_tile),
            (y_other, tall, turned_tile),
            (b3, (1, cols), fixed),
            (u, wide, row_tile),
            (dzs, wide, row_tile),
            *weights,
        ],
        [
            ((tokens, cols), BF, wide, row_tile),
            ((tokens, cols), BF, wide, row_tile),
            ((tokens // 2, width), F32, rows, first_rows),
            ((tokens // 2, width), BF, rows, last_rows),
            ((tokens, width), BF, rows, row_tile),
            ((1, cols), F32, (1, cols), fixed),
        ],
        "late",
        40,
    )


def tail_kernel(_, dv_ref, s_ref, w_ref, p_ref, tok_ref, dh_ref, pm_ref, po_ref, gain_ref, bias_ref, sum_ref):
    m = pl.program_id(0)

    @pl.when(m == 0)
    def _():
        gain_ref[...] = jnp.zeros_like(gain_ref)
        bias_ref[...] = jnp.zeros_like(bias_ref)
        sum_ref[...] = jnp.zeros_like(sum_ref)

    dh = (dv_ref[...].astype(F32) * s_ref[...].astype(F32)).astype(BF)
    dh_ref[...] = dh
    for k in range(dh.shape[1] // 128):
        sum_ref[...] += dh[:, k * 128 : (k + 1) * 128].astype(F32)
    p = p_ref[...].astype(F32) + mm(dh.T, w_ref[...], 1, 0)
    hat, _ = hat_of(tok_ref[...])
    gain_ref[...] += col_sum(p * hat)
    bias_ref[...] += col_sum(p)

    @pl.when(m < pl.num_programs(0) // 2)
    def _():
        pm_ref[...] = p

    @pl.when(m >= pl.num_programs(0) // 2)
    def _():
        po_ref[...] = p.astype(BF)


def tail_call(core, dv, slope, w_turned, p, tok):
    chans, tokens = dv.shape
    width = p.shape[1]
    rows, cols = (TILE, width), (chans, TILE)
    return call(
        tail_kernel,
        tokens // TILE,
        core,
        [
            (dv, cols, col_tile),
            (slope, cols, col_tile),
            (w_turned, (chans, width), fixed),
            (p, rows, row_tile),
            (tok, rows, row_tile),
        ],
        [
            ((chans, tokens), BF, cols, col_tile),
            ((tokens // 2, width), F32, rows, first_rows),
            ((tokens // 2, width), BF, rows, last_rows),
            ((1, width), F32, (1, width), fixed),
            ((1, width), F32, (1, width), fixed),
            ((chans, 128), F32, (chans, 128), fixed),
        ],
        "tail",
    )


def input_kernel(_, mine_ref, got_ref, tok_ref, g_ref, gain_ref, out_ref):
    hat, inv_std = hat_of(tok_ref[...])
    grad = (mine_ref[...] + got_ref[...].astype(F32)) * gain_ref[...]
    out_ref[...] = (
        g_ref[...].astype(F32)
        + inv_std
        * (
            grad
            - jnp.mean(grad, axis=-1, keepdims=True)
            - hat * jnp.mean(grad * hat, axis=-1, keepdims=True)
        )
    ).astype(BF)


def input_call(core, mine, got, tok, g, gain):
    tokens, width = mine.shape
    rows = (256, width)
    return call(
        input_kernel,
        tokens // 256,
        core,
        [(x, rows, row_tile) for x in (mine, got, tok, g)] + [(gain, (1, width), fixed)],
        [((tokens, width), BF, rows, row_tile)],
        "input_grad",
    )[0]

def keep_and_send(bit_ref, out, runs, keep_ref, send_ref):
    low, high = (
        jnp.concatenate(
            [out[k * runs : (k + 1) * runs] for k in range(half, out.shape[0] // runs, 2)], axis=0
        )
        for half in range(2)
    )
    one = bit_ref[0] == 1

    @pl.when(one)
    def _():
        keep_ref[...] = high
        send_ref[...] = low.astype(BF)

    @pl.when(jnp.logical_not(one))
    def _():
        keep_ref[...] = low
        send_ref[...] = high.astype(BF)


def grad_kernel(bit_ref, a_ref, b_ref, keep_ref, send_ref, *, runs):
    keep_and_send(bit_ref, mm(a_ref[...], b_ref[...], 0, 0), runs, keep_ref, send_ref)


def grad_call(bit, a, b, runs, tile, name):
    rows, cols = a.shape[1], b.shape[1]
    half = (tile // 2, cols)
    return call(
        functools.partial(grad_kernel, runs=runs),
        rows // tile,
        bit,
        [(a, (a.shape[0], tile), col_tile), (b, b.shape, fixed)],
        [((rows // 2, cols), F32, half, row_tile), ((rows // 2, cols), BF, half, row_tile)],
        name,
        32,
    )


def mixed_grad_kernel(bit_ref, ym_ref, yo_ref, b_ref, keep_ref, send_ref, *, runs):
    half = b_ref.shape[0] // 2
    out = jnp.concatenate(
        [
            mm(ym_ref[...], b_ref[...], 1, 0),
            mm(yo_ref[:, half:], b_ref[:half], 1, 0) + mm(yo_ref[:, :half], b_ref[half:], 1, 0),
        ],
        axis=0,
    )
    keep_and_send(bit_ref, out, runs, keep_ref, send_ref)


def mixed_grad_call(bit, y_mine, y_other, b, runs, name):
    rows, cols, tile = 2 * y_mine.shape[0], b.shape[1], 512
    half = (rows // 2, tile)
    return call(
        functools.partial(mixed_grad_kernel, runs=runs),
        cols // tile,
        bit,
        [(y_mine, y_mine.shape, fixed), (y_other, y_other.shape, fixed), (b, (b.shape[0], tile), col_tile)],
        [((rows // 2, cols), F32, half, col_tile), ((rows // 2, cols), BF, half, col_tile)],
        name,
        32,
    )


def after(x, *others):
    return lax.optimization_barrier((x,) + others)[0]


def swap_cores(x):
    return lax.ppermute(x, "fsdp", SWAP)


def across(x, size, bit):
    return lax.ppermute(x, "dp", [(i, i ^ (1 << bit)) for i in range(size)])


def bit_of(bit):
    return (lax.axis_index("dp") >> bit) & 1


def gather_bits(x, size, order, layout):
    have = []
    for bit in order:
        other = across(x, size, bit)
        mine = bit_of(bit) == 1
        have = [b for b in layout if b in have or b == bit]
        x = jnp.stack(
            [jnp.where(mine, other, x), jnp.where(mine, x, other)], axis=have.index(bit)
        )
    return x


def scatter_bits(x, size, order, layout, send_type):
    have = list(layout)
    for bit in order:
        axis = have.index(bit)
        mine = bit_of(bit)
        theirs = lax.dynamic_index_in_dim(x, 1 - mine, axis, keepdims=False)
        kept = lax.dynamic_index_in_dim(x, mine, axis, keepdims=False)
        x = kept.astype(F32) + across(theirs.astype(send_type), size, bit).astype(F32)
        have.remove(bit)
    return x


def per_device(
    size,
    tokens,
    cotangent,
    lengths,
    norm_gain,
    norm_bias,
    w_one,
    b_one,
    w_two,
    b_two,
    w_three,
    b_three,
    w_four,
    b_four,
    log_rate,
    ssm_coeff,
    ssm_skip,
):
    bits = size.bit_length() - 1
    tok_dev, width = tokens.shape
    rows_e, rows_f, rows_h = w_one.shape[0], w_four.shape[0], w_three.shape[0]
    f_half, h_half = size * rows_f, size * rows_h
    buckets = lengths.shape[0]
    group = size // buckets
    group_bits = group.bit_length() - 1
    chans = buckets * rows_h
    tok_chip = 2 * tok_dev
    per_dev = tok_dev // QBLK
    nstate = log_rate.shape[1]
    natural = list(range(bits))[::-1]
    by_owner = natural[bits - group_bits :] + natural[: bits - group_bits]
    top = natural[: bits - group_bits]
    order_a = list(range(2, bits)) + [0, 1]
    order_b = list(range(2, bits)) + [1, 0]
    core = lax.axis_index("fsdp")
    first = core == 0
    chip = lax.axis_index("dp")
    core_at = jnp.reshape(core, (1,)).astype(jnp.int32)
    everyone = ("dp", "fsdp")

    def natural_pair(mine, other, axis=0):
        return jnp.stack(
            [jnp.where(first, mine, other), jnp.where(first, other, mine)], axis=axis
        )

    def mine_other(parts, axis):
        a = lax.index_in_dim(parts, 0, axis, keepdims=False)
        b = lax.index_in_dim(parts, 1, axis, keepdims=False)
        return jnp.where(first, a, b), jnp.where(first, b, a)

    tok_pair = jnp.concatenate([tokens, swap_cores(tokens)], axis=0)
    cot_pair = jnp.concatenate([cotangent, swap_cores(cotangent)], axis=0)

    two_parts = jnp.moveaxis(
        w_two.reshape(rows_e, buckets, group, 2, rows_h), (3, 2, 1), (0, 2, 3)
    ).reshape(2, rows_e, h_half)
    vec = jnp.concatenate([norm_gain, norm_bias, b_four, b_one, b_three, b_two])
    vec_len = vec.shape[0]
    vec_rows = -(-vec_len // h_half)
    vec = jnp.pad(vec, (0, vec_rows * h_half - vec_len)).reshape(1, vec_rows, h_half)
    small = jnp.concatenate(
        [two_parts, jnp.broadcast_to(vec, (2, vec_rows, h_half))], axis=1
    )
    small = jnp.broadcast_to(small[None], (size, 2) + small.shape[1:])
    small = lax.all_to_all(
        small.reshape((2 * size,) + small.shape[2:]), everyone, split_axis=0, concat_axis=0
    )
    two_turned = small[:, :rows_e].reshape(width, h_half).T
    vecs = small[:, rows_e:].reshape(2 * size, -1)[:, :vec_len].astype(F32)
    gain_f = vecs[:, :rows_e].reshape(1, width)
    nbias_f = vecs[:, rows_e : 2 * rows_e].reshape(1, width)
    bfour_f = vecs[:, 2 * rows_e : 3 * rows_e].reshape(1, width)
    own_vecs, _ = mine_other(vecs.reshape(size, 2, vec_len)[:, :, 3 * rows_e :], 1)
    bone_f = own_vecs[:, :rows_f].reshape(1, f_half)
    bthree_f = own_vecs[:, rows_f : 2 * rows_f].reshape(1, f_half)
    btwo_f = (
        own_vecs[:, 2 * rows_f :].reshape(buckets, group, rows_h).swapaxes(0, 1).reshape(h_half, 1)
    )

    strip = 512
    f_strips, e_strips = f_half // strip, width // strip

    def by_half(x):
        rows = x.shape[0]
        parts = jnp.moveaxis(x.reshape(rows, size, 2, rows_f), 2, 0).reshape(2, rows, f_half)
        parts = jnp.moveaxis(parts.reshape(2, rows, f_strips, strip), 2, 1)
        return parts.reshape(2 * f_strips * rows, strip)

    packed = jnp.concatenate(
        [w_four[:, k * strip : (k + 1) * strip] for k in range(e_strips)]
        + [by_half(w_one), by_half(w_three)],
        axis=0,
    )
    gathered = lax.all_gather(packed, everyone, axis=0)
    four_end = e_strips * rows_f
    one_end = four_end + 2 * f_strips * rows_e
    gathered = gathered.reshape(size, 2, -1, strip)
    one_rows, three_rows = f_strips * rows_e, f_strips * rows_h

    def block(chips, cores, rows):
        return (chips, cores, rows, strip)

    if rows_h % 16 == 0 and four_end % one_rows == 0 and one_end % three_rows == 0:
        one_at, three_at = four_end // one_rows, one_end // three_rows
        order = [b * group + j for j in range(group) for b in range(buckets)]
        weights = [
            (gathered, block(size, 2, one_rows), lambda m, c: (0, 0, one_at + c[0], 0)),
            (gathered, block(size, 1, four_end), lambda m, c: (0, c[0], 0, 0)),
            (gathered, block(size, 1, three_rows), lambda m, c: (0, c[0], three_at + c[0], 0)),
            (gathered, block(size, 1, three_rows), lambda m, c: (0, 1 - c[0], three_at + c[0], 0)),
        ]
    else:
        order = [0]
        four_half = gathered[:, :, :four_end].reshape(size, 2, e_strips, rows_f, strip)
        four_half = lax.dynamic_index_in_dim(four_half, core, 1, keepdims=False).swapaxes(0, 1)
        one_half = gathered[:, :, four_end:one_end].reshape(2 * size, 2, f_strips, rows_e, strip)
        one_half = lax.dynamic_index_in_dim(one_half, core, 1, keepdims=False).swapaxes(0, 1)
        three_half = gathered[:, :, one_end:].reshape(
            buckets, group, 2, 2, f_strips, rows_h, strip
        )
        three_half = lax.dynamic_index_in_dim(three_half, core, 3, keepdims=False)
        three_half = jnp.transpose(three_half, (2, 3, 1, 0, 4, 5))
        three_half = mine_other(three_half, 0)
        weights = [
            (x.reshape(1, 1, -1, strip), block(1, 1, x.size // strip), lambda m, c: (0, 0, 0, 0))
            for x in (one_half, four_half, *three_half)
        ]

    params = gather_bits(
        jnp.concatenate(
            [log_rate, ssm_coeff, jnp.broadcast_to(ssm_skip[:, None], (rows_h, 128))], axis=1
        ),
        size,
        sorted(top),
        top,
    ).reshape(chans, 1, -1)
    mix_params = (
        params[..., :nstate],
        params[..., nstate : 2 * nstate],
        params[..., 2 * nstate :],
    )
    tables = mixer_tables(*mix_params[:2])
    groups = [[b * group + j for j in range(group)] for b in range(buckets)]

    def exchange(x):
        return lax.all_to_all(x, "dp", split_axis=0, concat_axis=0, axis_index_groups=groups)

    def to_owner(x):
        return exchange(x.reshape(group, chans, tok_chip))

    def from_owner(x):
        return exchange(x).reshape(h_half, tok_chip)

    def swap_turned(x):
        got = swap_cores(x)
        return jnp.concatenate([got[:, tok_dev:], got[:, :tok_dev]], axis=1)

    device = 2 * chip + core
    lane = jnp.arange(tok_dev, dtype=jnp.int32)
    place = jnp.concatenate([device * tok_dev + lane, (device ^ 1) * tok_dev + lane])
    bucket_range = jnp.arange(buckets, dtype=jnp.int32)
    limit = jnp.sum(
        jnp.where((place // SEQ)[:, None] == bucket_range[None, :], lengths[None, :], 0), axis=1
    )
    live = (place % SEQ < limit).astype(F32)[:, None]

    normed, out_grad, reduced_t, two_slope, out_sum = norm_call(
        core_at,
        tok_pair,
        cot_pair,
        jnp.broadcast_to(live, (tok_chip, 128)),
        gain_f,
        nbias_f,
        two_turned,
        jnp.broadcast_to(btwo_f, (h_half, 128)),
    )
    v_seq = to_owner(reduced_t)
    y_seq, entering = mixer_forward(core_at, v_seq, tables, mix_params)
    y_own = from_owner(y_seq)
    y_other = swap_cores(y_own)

    def small_pack(grad_two, gain_sum, nbias_sum, out_sum, one_sum, gate_sum, two_sum):
        def by_device(x):
            return x.reshape(2 * size, -1)

        def by_core(x):
            zero = jnp.zeros_like(x)
            return by_device(natural_pair(x, zero, axis=1))

        grad_btwo = (
            jnp.sum(two_sum, axis=1).reshape(group, buckets, rows_h).swapaxes(0, 1).reshape(size, rows_h)
        )
        vec_grads = jnp.concatenate(
            [
                by_device(gain_sum),
                by_device(nbias_sum),
                by_device(out_sum),
                by_core(one_sum.reshape(size, rows_f)),
                by_core(gate_sum.reshape(size, rows_f)),
                by_core(grad_btwo),
            ],
            axis=1,
        )
        vec_grads = jnp.pad(vec_grads, ((0, 0), (0, vec_rows * h_half - vec_len)))
        return jnp.concatenate(
            [
                grad_two.reshape(2 * size, rows_e, h_half).astype(BF),
                vec_grads.reshape(2 * size, vec_rows, h_half).astype(BF),
            ],
            axis=1,
        )

    act_one, dz_slope, gate_grad, dy_mine, dy_other, gate_sum = early_call(
        core_at, normed, out_grad, bone_f, weights, order
    )
    dy_own = (dy_mine + swap_cores(dy_other).astype(F32)).astype(BF)
    dy_seq = to_owner(dy_own)

    back_a, back_b = order_a[::-1], order_b[::-1]

    def halve(x, have, bit):
        axis, mine = have.index(bit), bit_of(bit)
        theirs = lax.dynamic_index_in_dim(x, 1 - mine, axis, keepdims=False).astype(BF)
        kept = lax.dynamic_index_in_dim(x, mine, axis, keepdims=False)
        return kept, across(theirs, size, bit), [b for b in have if b != bit]

    def join(kept, got, *others):
        return kept.astype(F32) + after(got, *others).astype(F32)

    def begin(keep_send, have, bit, rest):
        have = [b for b in have if b != bit]
        keep, send = (x.reshape((2,) * len(have) + rest) for x in keep_send)
        return keep, across(send, size, bit), have

    def bit_at(bit):
        return jnp.reshape(bit_of(bit), (1,)).astype(jnp.int32)

    product, one_grad, out_mine, out_other, one_back, one_sum = late_call(
        core_at, after(y_own, dy_own), y_other, bthree_f, act_one, dz_slope, width, weights, order
    )
    out_got = swap_cores(out_other)
    grad_four = grad_call(
        bit_at(back_a[0]), after(product, dy_seq), out_grad, rows_f << back_a[0], 384, "grad_four"
    )
    four = begin(grad_four, natural, back_a[0], (rows_f, width))

    dv_seq, grad_rate, grad_coeff, grad_skip = mixer_backward(
        core_at, v_seq, after(dy_seq, grad_four[0]), entering, tables, mix_params
    )
    dv_own = from_owner(dv_seq)
    grad_one = grad_call(
        bit_at(back_b[0]), normed, after(one_grad, dv_seq), 2 * rows_e << back_b[0], 256, "grad_one"
    )
    one = begin(grad_one, natural, back_b[0], (2 * rows_e, f_half))
    grad_three = mixed_grad_call(
        bit_at(back_a[0]),
        y_own,
        y_other,
        after(gate_grad, grad_one[0]),
        buckets * rows_h << back_a[0],
        "grad_three",
    )
    three_bits = [bits] + by_owner
    three = begin(grad_three, three_bits, back_a[0], (rows_h, f_half))
    four = halve(join(four[0], four[1], grad_three[0]), four[2], back_a[1])

    two_grad_t, back_mine, back_other, gain_sum, nbias_sum, two_sum = tail_call(
        core_at,         after(dv_own, four[0]), two_slope, two_turned, one_back, tok_pair
    )
    grad_two = mm(normed, two_grad_t, 0, 1)
    mix_grads = jnp.concatenate([grad_rate[:, 0], grad_coeff[:, 0], grad_skip[:, 0]], axis=1)
    mix_grads = scatter_bits(
        mix_grads.reshape((2,) * len(top) + (rows_h, -1)), size, sorted(top)[::-1], top, F32
    )
    back_got = swap_cores(back_other)
    small_grads = small_pack(
        grad_two, gain_sum, nbias_sum, out_sum, one_sum, gate_sum, two_sum
    )
    small_got = lax.all_to_all(small_grads, everyone, split_axis=0, concat_axis=0)
    branch = out_mine + after(out_got, two_grad_t).astype(F32)
    mixed = (live[:tok_dev] * (tokens.astype(F32) + branch + bfour_f)).astype(BF)
    input_grad = input_call(core_at, back_mine, back_got, tokens, out_grad[:tok_dev], gain_f)

    def merge_f(mine, other):
        rows = mine.shape[0]
        parts = (mine.reshape(rows, size, rows_f), other.reshape(rows, size, rows_f))
        return natural_pair(*parts, axis=2).reshape(rows, 2 * f_half)

    def finish(state, order):
        kept, got, have = state
        for bit in order:
            kept, got, have = halve(join(kept, got, two_grad_t), have, bit)
        return join(kept, got, two_grad_t)

    sum_four = finish(four, back_a[2:])
    sum_one = finish(one, back_b[1:])
    one_keep, one_send = mine_other(sum_one.reshape(2, rows_e, f_half), 0)
    sum_one = merge_f(one_keep, swap_cores(one_send))
    sum_three = finish(three, back_a[1:])
    sum_three = merge_f(sum_three[0], swap_cores(sum_three[1]))

    small_sum = jnp.sum(
        small_got.reshape(size, 2, rows_e + vec_rows, h_half).astype(F32), axis=0
    )
    sum_two = jnp.transpose(
        small_sum[:, :rows_e].reshape(2, rows_e, group, buckets, rows_h), (1, 3, 2, 0, 4)
    ).reshape(rows_e, 2 * h_half)
    vec_sum = jnp.sum(small_sum[:, rows_e:], axis=0).reshape(-1)
    ends = [rows_e, 2 * rows_e, 3 * rows_e, 3 * rows_e + rows_f, 3 * rows_e + 2 * rows_f, vec_len]
    sum_gain, sum_nbias, sum_bfour, sum_bone, sum_bthree, sum_btwo = (
        vec_sum[a:b] for a, b in zip([0] + ends, ends)
    )

    return (
        mixed,
        input_grad,
        sum_gain,
        sum_nbias,
        sum_one,
        sum_bone,
        sum_two,
        sum_btwo,
        sum_three,
        sum_bthree,
        sum_four,
        sum_bfour,
        mix_grads[:, :nstate],
        mix_grads[:, nstate : 2 * nstate],
        mix_grads[:, 2 * nstate],
    )


def solution(mesh):
    both = ("dp", "fsdp")
    rows, vector = P(both, None), P(both)
    in_specs = (
        rows, rows, P(), vector, vector, rows, vector, rows, vector, rows, vector, rows, vector,
        rows, rows, vector,
    )
    out_specs = (
        rows, rows, vector, vector, rows, vector, rows, vector, rows, vector, rows, vector,
        rows, rows, vector,
    )
    return jax.shard_map(
        functools.partial(per_device, mesh.shape["dp"]),
        mesh=mesh,
        in_specs=in_specs,
        out_specs=out_specs,
        check_vma=False,
    )
```

```python
import functools

import jax
import jax.numpy as jnp
from jax import lax
from jax.experimental import pallas as pl
from jax.experimental.pallas import tpu as pltpu
from jax.sharding import PartitionSpec as P

SEQ = 16384
QBLK = 256
F32 = jnp.float32
BF = jnp.bfloat16
SWAP = [(0, 1), (1, 0)]
ROOM = 60
TOOK = dict(
    norm=10, mixer_tables=12, mixer_forward=13, early=28, gate=13, grad_four=11, grad_one=12,
    mixer_backward=20, grad_three=8, out=20, tail=1, input_grad=7,
)


def costing(name):
    return pl.CostEstimate(flops=int(TOOK[name] * 3.3e+06 * 300), bytes_accessed=int(TOOK[name] * 3.3e+06), transcendentals=0)


def mm(left, right, left_dim, right_dim):
    return lax.dot_general(
        left, right, (((left_dim,), (right_dim,)), ((), ())), preferred_element_type=F32
    )


def split(value):
    high = value.astype(BF)
    return high, (value - high.astype(F32)).astype(BF)


def iotas(rows, cols):
    return (
        lax.broadcasted_iota(jnp.int32, (rows, cols), 0),
        lax.broadcasted_iota(jnp.int32, (rows, cols), 1),
    )


def shift_rows(x, k, backward):
    n = x.shape[0]
    row = iotas(*x.shape)[0]
    if backward:
        return jnp.where(row < n - k, pltpu.roll(x, n - k, 0), 0.0)
    return jnp.where(row >= k, pltpu.roll(x, k, 0), 0.0)


def states(x, rate, group, backward):
    blocks = x.shape[0] // group
    order = list(range(blocks))[:: -1 if backward else 1]
    decay = jnp.exp(-rate * float(QBLK))
    local, state = {}, None
    for b in order:
        local[b] = state
        here = x[b * group : (b + 1) * group]
        state = here if state is None else state * decay + here
    k = 1
    while k < group:
        state = state + shift_rows(state, k, backward) * jnp.exp(-rate * float(QBLK * blocks * k))
        k *= 2
    carry = shift_rows(state, 1, backward)
    out = {}
    for step, b in enumerate(order):
        far = carry * jnp.exp(-rate * float(QBLK * step)) if step else carry
        out[b] = far if local[b] is None else far + local[b]
    return jnp.concatenate([out[b] for b in range(blocks)], axis=0)


def flip_matrix():
    i, j = iotas(QBLK, QBLK)
    return jnp.where(i + j == QBLK - 1, 1.0, 0.0).astype(BF)


def base_of(rate):
    return jnp.where(rate * float(QBLK) < 1.0, 1.0, 0.0)


def row_sums(x):
    return jnp.sum(x.astype(F32), axis=1, keepdims=True)


def through(rows, table, base):
    return mm(rows, table, 1, 0) + row_sums(rows) * base


def table_kernel(lr_ref, co_ref, d_ref, dt_ref, t_ref):
    i, j = iotas(QBLK, QBLK)
    for c in range(lr_ref.shape[0]):
        rate, coeff = jnp.exp(lr_ref[c]), co_ref[c]
        row = lax.broadcasted_iota(jnp.int32, (8, rate.shape[1]), 0).astype(F32)
        table = jnp.exp(-rate * row)
        step = 8
        while step < QBLK:
            table = jnp.concatenate([table, table * jnp.exp(-rate * float(step))], axis=0)
            step *= 2
        lowered = table - base_of(rate)
        d_ref[c] = lowered.astype(BF)
        turned = lowered.T
        dt_ref[c] = turned.astype(BF)
        high, low = split(jnp.broadcast_to(coeff, (8, coeff.shape[1])))
        t_high, t_low = split(turned)
        kern = (
            mm(high, t_high, 1, 0) + mm(low, t_high, 1, 0) + mm(high, t_low, 1, 0)
        )[0:1] + row_sums(coeff * base_of(rate))
        rolled = pltpu.roll(jnp.broadcast_to(kern, (QBLK, QBLK)), 0, 1, stride=1, stride_axis=0)
        t_ref[c] = jnp.where(j >= i, rolled, 0.0).astype(BF)


def far_rows(entering, scale, turned, base):
    rows = entering.shape[0]
    scaled = entering * scale
    both = mm(jnp.concatenate(split(scaled), axis=0), turned, 1, 0)
    return both[:rows] + both[rows:] + row_sums(scaled * base)


def lanes_of(b, turn, total):
    start = b * QBLK + turn * (total // 2)
    start = jnp.where(start >= total, start - total, start)
    return pl.ds(pl.multiple_of(start, QBLK), QBLK)


def take_rows(x_ref, rows_ref, turn):
    group, _, total = x_ref.shape
    for b in range(0, total // QBLK, 2):
        pair = [
            jnp.swapaxes(x_ref[:, :, lanes_of(b + k, turn, total)].astype(F32), 0, 1)
            for k in range(2)
        ]
        rows_ref[:, b * group : (b + 2) * group, :] = jnp.concatenate(pair, axis=1).astype(BF)


def give_rows(rows_ref, x_ref, turn):
    group, _, total = x_ref.shape
    for b in range(0, total // QBLK, 2):
        pair = rows_ref[:, b * group : (b + 2) * group, :].astype(F32)
        for k in range(2):
            x_ref[:, :, lanes_of(b + k, turn, total)] = jnp.swapaxes(
                pair[:, k * group : (k + 1) * group], 0, 1
            ).astype(BF)


def forward_kernel(turn_ref, v_ref, d_ref, dt_ref, t_ref, lr_ref, co_ref, sk_ref, y_ref, en_ref, rows_ref, back_ref):
    per, group, turn = d_ref.shape[0], v_ref.shape[0], turn_ref[0]
    part, parts = pl.program_id(1), pl.num_programs(1)
    count = rows_ref.shape[1]

    @pl.when(part == 0)
    def _():
        take_rows(v_ref, rows_ref, turn)

    mine = rows_ref[pl.ds(part * per, per)]
    flipped = mm(mine.reshape(per * count, QBLK), flip_matrix(), 1, 0).astype(BF)
    for c in range(per):
        v = mine[c]
        rate = jnp.exp(lr_ref[c])
        base = base_of(rate)
        ends = through(flipped[c * count : (c + 1) * count], d_ref[c], base)
        entering = states(ends, rate, group, False)
        en_ref[c] = entering
        far = far_rows(entering, co_ref[c] * jnp.exp(-rate), dt_ref[c], base)
        back_ref[part * per + c] = (
            far + mm(v, t_ref[c], 1, 0) + sk_ref[c][:, :1] * v.astype(F32)
        ).astype(BF)

    @pl.when(part == parts - 1)
    def _():
        give_rows(back_ref, y_ref, turn)


def backward_kernel(
    turn_ref, v_ref, dy_ref, en_ref, d_ref, dt_ref, t_ref, lr_ref, co_ref, sk_ref,
    dv_ref, gr_ref, gc_ref, gs_ref, v_rows_ref, dy_rows_ref, back_ref,
):
    per, group, turn = d_ref.shape[0], v_ref.shape[0], turn_ref[0]
    part, parts = pl.program_id(1), pl.num_programs(1)
    count = v_rows_ref.shape[1]
    rows = per * count

    @pl.when(part == 0)
    def _():
        take_rows(v_ref, v_rows_ref, turn)
        take_rows(dy_ref, dy_rows_ref, turn)

    flip = flip_matrix()
    v_all = v_rows_ref[pl.ds(part * per, per)].reshape(rows, QBLK)
    dy_all = dy_rows_ref[pl.ds(part * per, per)].reshape(rows, QBLK)
    flipped = mm(jnp.concatenate([v_all, dy_all], axis=0), flip, 1, 0)
    lane = lax.broadcasted_iota(jnp.int32, (rows, QBLK), 1).astype(F32)
    v_lag = (flipped[:rows] * lane).astype(BF)
    dy_lag = (dy_all.astype(F32) * lane).astype(BF)
    flipped = flipped.astype(BF)
    i, j = iotas(QBLK, QBLK)
    lag = lax.broadcasted_iota(jnp.int32, (1, QBLK), 1).astype(F32)
    back = []
    for c in range(per):
        here = slice(c * count, (c + 1) * count)
        dy = dy_all[here]
        v_flip, dy_flip = flipped[here], flipped[rows + c * count : rows + (c + 1) * count]
        rate, coeff = jnp.exp(lr_ref[c]), co_ref[c]
        base = base_of(rate)
        pairs = pltpu.roll(mm(v_flip, dy, 0, 0), 1, 1, stride=1, stride_axis=0)
        near = jnp.sum(jnp.where(j <= i, pairs, 0.0), axis=0, keepdims=True)
        near_rows = jnp.concatenate(
            split(
                jnp.concatenate(
                    [jnp.broadcast_to(near, (8, QBLK)), jnp.broadcast_to(near * lag, (8, QBLK))],
                    axis=0,
                )
            ),
            axis=0,
        )
        sums = through(
            jnp.concatenate([dy, dy_lag[here], v_lag[here], near_rows], axis=0), d_ref[c], base
        )
        starts, starts_lag, ends_lag = (sums[k * count : (k + 1) * count] for k in range(3))
        inner = sums[3 * count : 3 * count + 16] + sums[3 * count + 16 :]
        leaving = states(starts, rate, group, True)
        entering = en_ref[c]
        one = jnp.exp(-rate)
        far = far_rows(leaving, coeff * one, dt_ref[c], base)
        back.append(
            (
                far + mm(dy_flip, t_ref[c], 1, 0) + sk_ref[c][:, :1] * dy_flip.astype(F32)
            ).astype(BF)
        )
        whole = jnp.exp(-rate * float(QBLK))
        outer = jnp.sum(entering * starts, axis=0, keepdims=True)
        moment = jnp.sum(
            ends_lag * leaving + entering * (starts_lag + (float(QBLK) * whole) * leaving),
            axis=0,
            keepdims=True,
        )
        gc_ref[c] = inner[0:1] + one * outer
        gr_ref[c] = -(coeff * rate) * (inner[8:9] + one * (moment + outer))
        gs_ref[c] = jnp.broadcast_to(near[:, :1], (1, 128))
    turned = mm(jnp.concatenate(back, axis=0), flip, 1, 0).astype(BF)
    back_ref[pl.ds(part * per, per)] = turned.reshape(per, count, QBLK)

    @pl.when(part == parts - 1)
    def _():
        give_rows(back_ref, dv_ref, turn)


def mixer_tables(log_rate, coeff):
    chans, _, n = log_rate.shape
    per = 4

    def spec(rows, cols):
        return pl.BlockSpec((per, rows, cols), lambda i: (i, 0, 0))

    shapes = [(QBLK, n), (n, QBLK), (QBLK, QBLK)]
    return pl.pallas_call(
        table_kernel,
        grid=(chans // per,),
        in_specs=[spec(1, n)] * 2,
        out_specs=[spec(*shape) for shape in shapes],
        out_shape=[jax.ShapeDtypeStruct((chans,) + shape, BF) for shape in shapes],
        compiler_params=pltpu.CompilerParams(vmem_limit_bytes=ROOM * 2**20),
        cost_estimate=costing("mixer_tables"),
        name="mixer_tables",
    )(log_rate, coeff)


def mixer_call(kernel, turn, tokens_in, by_channel, outs, name):
    group, chans, total = tokens_in[0].shape
    tall, per = 16, 8
    parts = tall // per
    count = group * (total // QBLK)

    def spec(shape):
        return pl.BlockSpec((per,) + tuple(shape[1:]), lambda i, j, *_: (i * parts + j, 0, 0))

    wide = pl.BlockSpec((group, tall, total), lambda i, j, *_: (0, i, 0))
    return pl.pallas_call(
        kernel,
        grid_spec=pltpu.PrefetchScalarGridSpec(
            num_scalar_prefetch=1,
            grid=(chans // tall, parts),
            in_specs=[wide] * len(tokens_in) + [spec(x.shape) for x in by_channel],
            out_specs=[wide] + [spec(shape) for shape, _ in outs],
            scratch_shapes=[pltpu.VMEM((tall, count, QBLK), BF)] * (len(tokens_in) + 1),
        ),
        out_shape=[jax.ShapeDtypeStruct((group, chans, total), BF)]
        + [jax.ShapeDtypeStruct(shape, kind) for shape, kind in outs],
        compiler_params=pltpu.CompilerParams(vmem_limit_bytes=ROOM * 2**20),
        cost_estimate=costing(name),
        name=name,
    )(turn, *tokens_in, *by_channel)


def mixer_forward(turn, v, tables, params):
    group, chans, total = v.shape
    n = params[0].shape[2]
    states_of = (chans, group * (total // QBLK), n)
    return mixer_call(
        forward_kernel, turn, [v], [*tables, *params], [(states_of, F32)], "mixer_forward"
    )


def mixer_backward(turn, v, dy, entering, tables, params):
    chans, n = v.shape[1], params[0].shape[2]
    return mixer_call(
        backward_kernel,
        turn,
        [v, dy],
        [entering, *tables, *params],
        [((chans, 1, n), F32), ((chans, 1, n), F32), ((chans, 1, 128), F32)],
        "mixer_backward",
    )


TILE = 512


def call(kernel, grid, core, ins, outs, name, room, scratch=()):
    return pl.pallas_call(
        kernel,
        grid_spec=pltpu.PrefetchScalarGridSpec(
            num_scalar_prefetch=1,
            grid=(grid,),
            in_specs=[
                pl.BlockSpec(block, index, pipeline_mode=None if index in MOVING else pl.Buffered(1))
                for _, block, index in ins
            ],
            out_specs=[pl.BlockSpec(block, index) for _, _, block, index in outs],
            scratch_shapes=list(scratch),
        ),
        out_shape=[jax.ShapeDtypeStruct(shape, kind) for shape, kind, _, _ in outs],
        compiler_params=pltpu.CompilerParams(vmem_limit_bytes=room * 2**20),
        cost_estimate=costing(name),
        name=name,
    )(core, *[array for array, _, _ in ins])


def row_tile(m, _):
    return (m, 0)


def col_tile(m, _):
    return (0, m)


def turned_tile(m, _):
    half = pl.num_programs(0) // 2
    return (0, jnp.where(m < half, m + half, m - half))


def fixed(m, _):
    return (0, 0)


MOVING = (row_tile, col_tile, turned_tile)


def first_rows(m, _):
    return (jnp.minimum(m, pl.num_programs(0) // 2 - 1), 0)


def last_rows(m, _):
    return (jnp.maximum(m - pl.num_programs(0) // 2, 0), 0)


def strips_of(start, stop, strip):
    while start < stop:
        k = start // strip
        end = min(stop, (k + 1) * strip)
        yield k, slice(start - k * strip, end - k * strip)
        start = end


def strip_columns(ref, total, start, stop, order):
    rows = ref.shape[2] // (total // ref.shape[3])
    return jnp.concatenate(
        [
            jnp.concatenate(
                [
                    ref[chip, core, k * rows : (k + 1) * rows, lanes]
                    for chip in order
                    for core in range(ref.shape[1])
                ],
                axis=0,
            )
            for k, lanes in strips_of(start, stop, ref.shape[3])
        ],
        axis=1,
    )


def strip_rows(ref, strips, start, stop):
    rows = ref.shape[2] // strips
    return jnp.concatenate(
        [
            jnp.concatenate(
                [
                    ref[chip, 0, k * rows + part.start : k * rows + part.stop, :]
                    for chip, part in strips_of(start, stop, rows)
                ],
                axis=0,
            )
            for k in range(strips)
        ],
        axis=1,
    )


def col_sum(x):
    return jnp.sum(x.astype(F32), axis=0, keepdims=True)


def hat_of(x):
    x = x.astype(F32)
    centered = x - jnp.mean(x, axis=-1, keepdims=True)
    inv_std = lax.rsqrt(jnp.mean(centered * centered, axis=-1, keepdims=True) + 1e-05)
    return centered * inv_std, inv_std


def slope_and_gelu(h):
    phi = 0.5 + 0.5 * lax.erf(h * 0.7071067811865476)
    return h * phi, phi + h * jnp.exp(-0.5 * h * h) * 0.3989422804014327


def norm_kernel(
    _, tok_ref, cot_ref, live_ref, gain_ref, bias_ref, w_ref, b_ref, n_ref, g_ref, v_ref, s_ref, sum_ref
):
    m = pl.program_id(0)

    @pl.when(m == 0)
    def _():
        sum_ref[...] = jnp.zeros_like(sum_ref)

    hat, _ = hat_of(tok_ref[...])
    normed = (hat * gain_ref[...] + bias_ref[...]).astype(BF)
    n_ref[...] = normed
    g = jnp.where(live_ref[...][:, :1] > 0.0, cot_ref[...], jnp.zeros((), BF))
    g_ref[...] = g

    @pl.when(m < pl.num_programs(0) // 2)
    def _():
        sum_ref[...] += col_sum(g)

    v, s = slope_and_gelu(mm(w_ref[...], normed, 1, 1) + b_ref[...][:, :1])
    v_ref[...] = v.astype(BF)
    s_ref[...] = s.astype(BF)


def norm_call(core, tok, cot, live, gain, bias, w_turned, b):
    tokens, width = tok.shape
    chans = w_turned.shape[0]
    rows, cols = (TILE, width), (chans, TILE)
    return call(
        norm_kernel,
        tokens // TILE,
        core,
        [
            (tok, rows, row_tile),
            (cot, rows, row_tile),
            (live, (TILE, 128), row_tile),
            (gain, (1, width), fixed),
            (bias, (1, width), fixed),
            (w_turned, (chans, width), fixed),
            (b, (chans, 128), fixed),
        ],
        [((tokens, width), BF, rows, row_tile)] * 2
        + [((chans, tokens), BF, cols, col_tile)] * 2
        + [((1, width), F32, (1, width), fixed)],
        "norm",
        ROOM,
    )


def early_kernel(
    _, x_ref, g_ref, b1_ref, w1_ref, w4_ref, w3m_ref, w3o_ref,
    u_ref, dzs_ref, dgate_ref, mine_ref, other_ref, sum_ref, *, order,
):
    total = u_ref.shape[1]
    cols, chips = 384, range(w1_ref.shape[0])
    e_strips = g_ref.shape[1] // w4_ref.shape[3]

    @pl.when(pl.program_id(0) == 0)
    def _():
        sum_ref[...] = jnp.zeros_like(sum_ref)

    for n in range(total // cols):
        at = slice(n * cols, (n + 1) * cols)
        w1 = strip_columns(w1_ref, total, at.start, at.stop, chips)
        u, s = slope_and_gelu(mm(x_ref[...], w1, 1, 0) + b1_ref[:, at])
        dz = mm(g_ref[...], strip_rows(w4_ref, e_strips, at.start, at.stop), 1, 1)
        dgate = (dz * u).astype(BF)
        u_ref[:, at] = u.astype(BF)
        dzs_ref[:, at] = (dz * s).astype(BF)
        dgate_ref[:, at] = dgate
        sum_ref[:, at] += col_sum(dgate)
    mine_ref[...] = mm(strip_columns(w3m_ref, total, 0, total, order), dgate_ref[...], 1, 1)
    other = mm(strip_columns(w3o_ref, total, 0, total, order), dgate_ref[...], 1, 1)
    other_ref[...] = other.astype(BF)


def early_call(core, x, g, b1, weights, order):
    tokens, width = x.shape
    cols = b1.shape[1]
    chans = weights[2][1][2] * weights[2][1][3] * len(order) // cols
    wide, tall = (TILE, cols), (chans, TILE)
    return call(
        functools.partial(early_kernel, order=order),
        tokens // TILE,
        core,
        [
            (x, (TILE, width), row_tile),
            (g, (TILE, width), row_tile),
            (b1, (1, cols), fixed),
            *weights,
        ],
        [((tokens, cols), BF, wide, row_tile)] * 3
        + [
            ((chans, tokens), F32, tall, col_tile),
            ((chans, tokens), BF, tall, turned_tile),
            ((1, cols), F32, (1, cols), fixed),
        ],
        "early",
        ROOM,
    )


def gate_kernel(
    _, ym_ref, yo_ref, b3_ref, u_ref, dzs_ref, w3m_ref, w3o_ref, z_ref, dh_ref, sum_ref, *, order
):
    total, cols = u_ref.shape[1], 256

    @pl.when(pl.program_id(0) == 0)
    def _():
        sum_ref[...] = jnp.zeros_like(sum_ref)

    y = jnp.concatenate([ym_ref[...], yo_ref[...]], axis=0).T
    for n in range(total // cols):
        at = slice(n * cols, (n + 1) * cols)
        w3 = jnp.concatenate(
            [strip_columns(ref, total, at.start, at.stop, order) for ref in (w3m_ref, w3o_ref)],
            axis=0,
        )
        gate = mm(y, w3, 1, 0) + b3_ref[:, at]
        z_ref[:, at] = (u_ref[:, at].astype(F32) * gate).astype(BF)
        dh = (dzs_ref[:, at].astype(F32) * gate).astype(BF)
        dh_ref[:, at] = dh
        sum_ref[:, at] += col_sum(dh)


def gate_call(core, y_mine, y_other, b3, u, dzs, weights, order):
    tokens, cols = u.shape
    wide, tall = (TILE, cols), (y_mine.shape[0], TILE)
    return call(
        functools.partial(gate_kernel, order=order),
        tokens // TILE,
        core,
        [
            (y_mine, tall, col_tile),
            (y_other, tall, turned_tile),
            (b3, (1, cols), fixed),
            (u, wide, row_tile),
            (dzs, wide, row_tile),
            *weights[2:],
        ],
        [
            ((tokens, cols), BF, wide, row_tile),
            ((tokens, cols), BF, wide, row_tile),
            ((1, cols), F32, (1, cols), fixed),
        ],
        "gate",
        ROOM,
    )


def out_kernel(_, z_ref, dh_ref, w1_ref, w4_ref, om_ref, oo_ref, p_ref):
    m, total = pl.program_id(0), z_ref.shape[1]
    chips = range(w1_ref.shape[0])
    e_strips = om_ref.shape[1] // w4_ref.shape[3]
    p_ref[...] = mm(dh_ref[...], strip_columns(w1_ref, total, 0, total, chips), 1, 1).astype(BF)
    out = mm(z_ref[...], strip_rows(w4_ref, e_strips, 0, total), 1, 0)

    @pl.when(m < pl.num_programs(0) // 2)
    def _():
        om_ref[...] = out

    @pl.when(m >= pl.num_programs(0) // 2)
    def _():
        oo_ref[...] = out.astype(BF)


def out_call(core, z, dh, width, weights):
    tokens, cols = z.shape
    wide, rows = (TILE, cols), (TILE, width)
    return call(
        out_kernel,
        tokens // TILE,
        core,
        [(z, wide, row_tile), (dh, wide, row_tile), *weights[:2]],
        [
            ((tokens // 2, width), F32, rows, first_rows),
            ((tokens // 2, width), BF, rows, last_rows),
            ((tokens, width), BF, rows, row_tile),
        ],
        "out",
        ROOM,
    )


def tail_kernel(
    _, dv_ref, s_ref, w_ref, p_ref, tok_ref, n_ref, grad_ref, pm_ref, po_ref, gain_ref, bias_ref, sum_ref, total_ref
):
    m = pl.program_id(0)

    @pl.when(m == 0)
    def _():
        gain_ref[...] = jnp.zeros_like(gain_ref)
        bias_ref[...] = jnp.zeros_like(bias_ref)
        sum_ref[...] = jnp.zeros_like(sum_ref)
        total_ref[...] = jnp.zeros_like(total_ref)

    dh = (dv_ref[...].astype(F32) * s_ref[...].astype(F32)).astype(BF)
    total_ref[...] += mm(dh, n_ref[...], 1, 0)
    for k in range(dh.shape[1] // 128):
        sum_ref[...] += dh[:, k * 128 : (k + 1) * 128].astype(F32)
    p = p_ref[...].astype(F32) + mm(dh.T, w_ref[...], 1, 0)
    hat, _ = hat_of(tok_ref[...])
    gain_ref[...] += col_sum(p * hat)
    bias_ref[...] += col_sum(p)

    @pl.when(m == pl.num_programs(0) - 1)
    def _():
        grad_ref[...] = total_ref[...].T.astype(BF)

    @pl.when(m < pl.num_programs(0) // 2)
    def _():
        pm_ref[...] = p

    @pl.when(m >= pl.num_programs(0) // 2)
    def _():
        po_ref[...] = p.astype(BF)


def tail_call(core, dv, slope, w_turned, p, tok, normed):
    chans, tokens = dv.shape
    width = p.shape[1]
    rows, cols = (TILE, width), (chans, TILE)
    return call(
        tail_kernel,
        tokens // TILE,
        core,
        [
            (dv, cols, col_tile),
            (slope, cols, col_tile),
            (w_turned, (chans, width), fixed),
            (p, rows, row_tile),
            (tok, rows, row_tile),
            (normed, rows, row_tile),
        ],
        [
            ((width, chans), BF, (width, chans), fixed),
            ((tokens // 2, width), F32, rows, first_rows),
            ((tokens // 2, width), BF, rows, last_rows),
            ((1, width), F32, (1, width), fixed),
            ((1, width), F32, (1, width), fixed),
            ((chans, 128), F32, (chans, 128), fixed),
        ],
        "tail",
        ROOM,
        [pltpu.VMEM((chans, width), F32)],
    )


def input_kernel(_, mine_ref, got_ref, tok_ref, g_ref, gain_ref, out_ref):
    hat, inv_std = hat_of(tok_ref[...])
    grad = (mine_ref[...] + got_ref[...].astype(F32)) * gain_ref[...]
    out_ref[...] = (
        g_ref[...].astype(F32)
        + inv_std
        * (
            grad
            - jnp.mean(grad, axis=-1, keepdims=True)
            - hat * jnp.mean(grad * hat, axis=-1, keepdims=True)
        )
    ).astype(BF)


def input_call(core, mine, got, tok, g, gain):
    tokens, width = mine.shape
    rows = (256, width)
    return call(
        input_kernel,
        tokens // 256,
        core,
        [(x, rows, row_tile) for x in (mine, got, tok, g)] + [(gain, (1, width), fixed)],
        [((tokens, width), BF, rows, row_tile)],
        "input_grad",
        ROOM,
    )[0]

def keep_and_send(here, out_ref, runs, keep_ref, send_refs):
    for k, ref in enumerate((keep_ref, *send_refs)):
        part = jnp.concatenate(
            [
                out_ref[pl.ds(pl.multiple_of((at + (here ^ k)) * runs, runs), runs), :]
                for at in range(0, out_ref.shape[0] // runs, 4)
            ],
            axis=0,
        )
        ref[...] = part.astype(ref.dtype)


def grad_kernel(here_ref, a_ref, b_ref, keep_ref, s1_ref, s2_ref, s3_ref, out_ref, *, runs):
    out_ref[...] = mm(a_ref[...], b_ref[...], 0, 0)
    keep_and_send(here_ref[0], out_ref, runs, keep_ref, (s1_ref, s2_ref, s3_ref))


def grad_call(here, a, b, runs, tile, name):
    rows, cols = a.shape[1], b.shape[1]
    part, shape = (tile // 4, cols), (rows // 4, cols)
    return call(
        functools.partial(grad_kernel, runs=runs),
        rows // tile,
        here,
        [(a, (a.shape[0], tile), col_tile), (b, b.shape, fixed)],
        [(shape, kind, part, row_tile) for kind in (F32, BF, BF, BF)],
        name,
        ROOM,
        [pltpu.VMEM((tile, cols), F32)],
    )


def mixed_grad_kernel(here_ref, ym_ref, yo_ref, b_ref, keep_ref, s1_ref, s2_ref, s3_ref, out_ref, *, runs):
    half, rows = b_ref.shape[0] // 2, ym_ref.shape[0]
    out_ref[:rows] = mm(ym_ref[...], b_ref[...], 1, 0)
    out_ref[rows:] = mm(yo_ref[:, half:], b_ref[:half], 1, 0) + mm(
        yo_ref[:, :half], b_ref[half:], 1, 0
    )
    keep_and_send(here_ref[0], out_ref, runs, keep_ref, (s1_ref, s2_ref, s3_ref))


def mixed_grad_call(here, y_mine, y_other, b, runs, name):
    rows, cols, tile = 2 * y_mine.shape[0], b.shape[1], 512
    part, shape = (rows // 4, tile), (rows // 4, cols)
    return call(
        functools.partial(mixed_grad_kernel, runs=runs),
        cols // tile,
        here,
        [(y_mine, y_mine.shape, fixed), (y_other, y_other.shape, fixed), (b, (b.shape[0], tile), col_tile)],
        [(shape, kind, part, col_tile) for kind in (F32, BF, BF, BF)],
        name,
        ROOM,
        [pltpu.VMEM((rows, tile), F32)],
    )


def after(x, *others):
    return lax.optimization_barrier((x,) + others)[0]


def swap_cores(x):
    return lax.ppermute(x, "fsdp", SWAP)


def across(x, size, flip):
    return lax.ppermute(x, "dp", [(i, i ^ flip) for i in range(size)])


def bit_of(bit):
    return (lax.axis_index("dp") >> bit) & 1


def gather_bits(x, size, order, layout):
    have = []
    for bit in order:
        other = across(x, size, 1 << bit)
        mine = bit_of(bit) == 1
        have = [b for b in layout if b in have or b == bit]
        x = jnp.stack(
            [jnp.where(mine, other, x), jnp.where(mine, x, other)], axis=have.index(bit)
        )
    return x


def scatter_bits(x, size, order, layout, send_type):
    have = list(layout)
    for bit in order:
        axis = have.index(bit)
        mine = bit_of(bit)
        theirs = lax.dynamic_index_in_dim(x, 1 - mine, axis, keepdims=False)
        kept = lax.dynamic_index_in_dim(x, mine, axis, keepdims=False)
        x = kept.astype(F32) + across(theirs.astype(send_type), size, 1 << bit).astype(F32)
        have.remove(bit)
    return x


def per_device(
    size,
    tokens,
    cotangent,
    lengths,
    norm_gain,
    norm_bias,
    w_one,
    b_one,
    w_two,
    b_two,
    w_three,
    b_three,
    w_four,
    b_four,
    log_rate,
    ssm_coeff,
    ssm_skip,
):
    bits = size.bit_length() - 1
    tok_dev, width = tokens.shape
    rows_e, rows_f, rows_h = w_one.shape[0], w_four.shape[0], w_three.shape[0]
    f_half, h_half = size * rows_f, size * rows_h
    buckets = lengths.shape[0]
    group = size // buckets
    group_bits = group.bit_length() - 1
    chans = buckets * rows_h
    tok_chip = 2 * tok_dev
    per_dev = tok_dev // QBLK
    nstate = log_rate.shape[1]
    natural = list(range(bits))[::-1]
    by_owner = natural[bits - group_bits :] + natural[: bits - group_bits]
    top = natural[: bits - group_bits]
    order_a = list(range(2, bits)) + [0, 1]
    order_b = list(range(2, bits)) + [1, 0]
    core = lax.axis_index("fsdp")
    first = core == 0
    chip = lax.axis_index("dp")
    core_at = jnp.reshape(core, (1,)).astype(jnp.int32)
    everyone = ("dp", "fsdp")

    def natural_pair(mine, other, axis=0):
        return jnp.stack(
            [jnp.where(first, mine, other), jnp.where(first, other, mine)], axis=axis
        )

    def mine_other(parts, axis):
        a = lax.index_in_dim(parts, 0, axis, keepdims=False)
        b = lax.index_in_dim(parts, 1, axis, keepdims=False)
        return jnp.where(first, a, b), jnp.where(first, b, a)

    tok_pair = jnp.concatenate([tokens, swap_cores(tokens)], axis=0)
    cot_pair = jnp.concatenate([cotangent, swap_cores(cotangent)], axis=0)

    two_parts = jnp.moveaxis(
        w_two.reshape(rows_e, buckets, group, 2, rows_h), (3, 2, 1), (0, 2, 3)
    ).reshape(2, rows_e, h_half)
    vec = jnp.concatenate([norm_gain, norm_bias, b_four, b_one, b_three, b_two])
    vec_len = vec.shape[0]
    vec_rows = -(-vec_len // h_half)
    vec = jnp.pad(vec, (0, vec_rows * h_half - vec_len)).reshape(1, vec_rows, h_half)
    small = jnp.concatenate(
        [two_parts, jnp.broadcast_to(vec, (2, vec_rows, h_half))], axis=1
    )
    small = jnp.broadcast_to(small[None], (size, 2) + small.shape[1:])
    small = lax.all_to_all(
        small.reshape((2 * size,) + small.shape[2:]), everyone, split_axis=0, concat_axis=0
    )
    two_turned = small[:, :rows_e].reshape(width, h_half).T
    vecs = small[:, rows_e:].reshape(2 * size, -1)[:, :vec_len].astype(F32)
    gain_f = vecs[:, :rows_e].reshape(1, width)
    nbias_f = vecs[:, rows_e : 2 * rows_e].reshape(1, width)
    bfour_f = vecs[:, 2 * rows_e : 3 * rows_e].reshape(1, width)
    own_vecs, _ = mine_other(vecs.reshape(size, 2, vec_len)[:, :, 3 * rows_e :], 1)
    bone_f = own_vecs[:, :rows_f].reshape(1, f_half)
    bthree_f = own_vecs[:, rows_f : 2 * rows_f].reshape(1, f_half)
    btwo_f = (
        own_vecs[:, 2 * rows_f :].reshape(buckets, group, rows_h).swapaxes(0, 1).reshape(h_half, 1)
    )

    strip = 512
    f_strips, e_strips = f_half // strip, width // strip

    def by_half(x):
        rows = x.shape[0]
        parts = jnp.moveaxis(x.reshape(rows, size, 2, rows_f), 2, 0).reshape(2, rows, f_half)
        parts = jnp.moveaxis(parts.reshape(2, rows, f_strips, strip), 2, 1)
        return parts.reshape(2 * f_strips * rows, strip)

    packed = jnp.concatenate(
        [w_four[:, k * strip : (k + 1) * strip] for k in range(e_strips)]
        + [by_half(w_one), by_half(w_three)],
        axis=0,
    )
    gathered = lax.all_gather(packed, everyone, axis=0)
    four_end = e_strips * rows_f
    one_end = four_end + 2 * f_strips * rows_e
    gathered = gathered.reshape(size, 2, -1, strip)
    one_rows, three_rows = f_strips * rows_e, f_strips * rows_h

    def block(chips, cores, rows):
        return (chips, cores, rows, strip)

    if rows_h % 16 == 0 and four_end % one_rows == 0 and one_end % three_rows == 0:
        one_at, three_at = four_end // one_rows, one_end // three_rows
        order = [b * group + j for j in range(group) for b in range(buckets)]
        weights = [
            (gathered, block(size, 2, one_rows), lambda m, c: (0, 0, one_at + c[0], 0)),
            (gathered, block(size, 1, four_end), lambda m, c: (0, c[0], 0, 0)),
            (gathered, block(size, 1, three_rows), lambda m, c: (0, c[0], three_at + c[0], 0)),
            (gathered, block(size, 1, three_rows), lambda m, c: (0, 1 - c[0], three_at + c[0], 0)),
        ]
    else:
        order = [0]
        four_half = gathered[:, :, :four_end].reshape(size, 2, e_strips, rows_f, strip)
        four_half = lax.dynamic_index_in_dim(four_half, core, 1, keepdims=False).swapaxes(0, 1)
        one_half = gathered[:, :, four_end:one_end].reshape(2 * size, 2, f_strips, rows_e, strip)
        one_half = lax.dynamic_index_in_dim(one_half, core, 1, keepdims=False).swapaxes(0, 1)
        three_half = gathered[:, :, one_end:].reshape(
            buckets, group, 2, 2, f_strips, rows_h, strip
        )
        three_half = lax.dynamic_index_in_dim(three_half, core, 3, keepdims=False)
        three_half = jnp.transpose(three_half, (2, 3, 1, 0, 4, 5))
        three_half = mine_other(three_half, 0)
        weights = [
            (x.reshape(1, 1, -1, strip), block(1, 1, x.size // strip), lambda m, c: (0, 0, 0, 0))
            for x in (one_half, four_half, *three_half)
        ]

    params = gather_bits(
        jnp.concatenate(
            [log_rate, ssm_coeff, jnp.broadcast_to(ssm_skip[:, None], (rows_h, 128))], axis=1
        ),
        size,
        sorted(top),
        top,
    ).reshape(chans, 1, -1)
    mix_params = (
        params[..., :nstate],
        params[..., nstate : 2 * nstate],
        params[..., 2 * nstate :],
    )
    tables = mixer_tables(*mix_params[:2])
    groups = [[b * group + j for j in range(group)] for b in range(buckets)]

    def exchange(x):
        return lax.all_to_all(x, "dp", split_axis=0, concat_axis=0, axis_index_groups=groups)

    def to_owner(x):
        return exchange(x.reshape(group, chans, tok_chip))

    def from_owner(x):
        return exchange(x).reshape(h_half, tok_chip)

    def swap_turned(x):
        got = swap_cores(x)
        return jnp.concatenate([got[:, tok_dev:], got[:, :tok_dev]], axis=1)

    device = 2 * chip + core
    lane = jnp.arange(tok_dev, dtype=jnp.int32)
    place = jnp.concatenate([device * tok_dev + lane, (device ^ 1) * tok_dev + lane])
    bucket_range = jnp.arange(buckets, dtype=jnp.int32)
    limit = jnp.sum(
        jnp.where((place // SEQ)[:, None] == bucket_range[None, :], lengths[None, :], 0), axis=1
    )
    live = (place % SEQ < limit).astype(F32)[:, None]

    normed, out_grad, reduced_t, two_slope, out_sum = norm_call(
        core_at,
        tok_pair,
        cot_pair,
        jnp.broadcast_to(live, (tok_chip, 128)),
        gain_f,
        nbias_f,
        two_turned,
        jnp.broadcast_to(btwo_f, (h_half, 128)),
    )
    v_seq = to_owner(reduced_t)
    y_seq, entering = mixer_forward(core_at, v_seq, tables, mix_params)
    y_own = from_owner(y_seq)
    y_other = swap_cores(y_own)

    def small_pack(grad_two, gain_sum, nbias_sum, out_sum, one_sum, gate_sum, two_sum):
        def by_device(x):
            return x.reshape(2 * size, -1)

        def by_core(x):
            zero = jnp.zeros_like(x)
            return by_device(natural_pair(x, zero, axis=1))

        grad_btwo = (
            jnp.sum(two_sum, axis=1).reshape(group, buckets, rows_h).swapaxes(0, 1).reshape(size, rows_h)
        )
        vec_grads = jnp.concatenate(
            [
                by_device(gain_sum),
                by_device(nbias_sum),
                by_device(out_sum),
                by_core(one_sum.reshape(size, rows_f)),
                by_core(gate_sum.reshape(size, rows_f)),
                by_core(grad_btwo),
            ],
            axis=1,
        )
        vec_grads = jnp.pad(vec_grads, ((0, 0), (0, vec_rows * h_half - vec_len)))
        return jnp.concatenate(
            [
                grad_two.reshape(2 * size, rows_e, h_half).astype(BF),
                vec_grads.reshape(2 * size, vec_rows, h_half).astype(BF),
            ],
            axis=1,
        )

    act_one, dz_slope, gate_grad, dy_mine, dy_other, gate_sum = early_call(
        core_at, normed, out_grad, bone_f, weights, order
    )
    dy_own = (dy_mine + swap_cores(dy_other).astype(F32)).astype(BF)
    dy_seq = to_owner(dy_own)


    def send_off(sends, low):
        came = {k: across(sends[k - 1], size, k << low) for k in (3, 1, 2)}
        return [came[k] for k in (1, 2, 3)]

    def begin(outputs, have, rest):
        keep, *parts = (x.reshape((2,) * len(have) + rest) for x in outputs)
        return keep, send_off(parts, 0), have

    def split_off(state, low, *others):
        kept, came, have = state
        high = low + 1
        axis = min(have.index(high), have.index(low))
        swapped = have.index(low) < have.index(high)
        shape = kept.shape[:axis] + (4,) + kept.shape[axis + 2 :]
        terms = [kept.reshape(shape)] + [after(x, *others).reshape(shape) for x in came]
        here = (chip >> low) & 3

        def part(k):
            index = here ^ k
            index = ((index & 1) << 1) | (index >> 1) if swapped else index
            return sum(
                lax.dynamic_index_in_dim(x, index, axis, keepdims=False).astype(F32) for x in terms
            )

        return part(0), [part(k).astype(BF) for k in (1, 2, 3)], [b for b in have if b >> 1 != low >> 1]

    def go_on(state, low):
        kept, parts, have = state
        return kept, send_off(parts, low), have

    def to_last(state):
        for low in range(2, bits - 2, 2):
            state = go_on(split_off(state, low), low)
        return state

    def total(state, *others):
        kept, came, _ = state
        return sum((after(x, *others).astype(F32) for x in came), kept)

    here = jnp.reshape(chip & 3, (1,)).astype(jnp.int32)
    last = bits - 2
    far = size // 4
    far_groups = [[4 * g + k for g in range(far)] for k in range(4)]

    product, one_grad, one_sum = gate_call(
        core_at, after(y_own, dy_own), y_other, bthree_f, act_one, dz_slope, weights, order
    )
    grad_four = grad_call(here, product, out_grad, rows_f, 384, "grad_four")
    four = begin(grad_four, natural[:-2], (rows_f, width))
    dv_seq, grad_rate, grad_coeff, grad_skip = mixer_backward(
        core_at, v_seq, after(dy_seq, grad_four[0]), entering, tables, mix_params
    )
    dv_own = from_owner(dv_seq)
    grad_three = mixed_grad_call(
        here, y_own, y_other, after(gate_grad, dv_seq), buckets * rows_h, "grad_three"
    )
    grad_one = grad_call(
        here, normed, after(one_grad, grad_three[0]), 2 * rows_e, 256, "grad_one"
    )

    def stacked(one, three):
        three = three.reshape(2, group // 4, buckets, rows_h, f_half)
        three = jnp.moveaxis(three, (2, 1), (0, 1)).reshape(far, 2 * rows_h, f_half)
        return jnp.concatenate([one.reshape(far, 2 * rows_e, f_half), three], axis=1)

    rest = begin(
        [stacked(x, y) for x, y in zip(grad_one, grad_three)],
        natural[:-2],
        (2 * rows_e + 2 * rows_h, f_half),
    )
    four_parts = total(four, grad_one[0]).astype(BF).reshape(far, rows_f, width)
    four_got = lax.all_to_all(
        after(four_parts, dv_own), "dp", split_axis=0, concat_axis=0, axis_index_groups=far_groups
    )
    out_mine, out_other, one_back = out_call(
        core_at, product, after(one_grad, grad_one[0], dv_own, four_parts), width, weights
    )
    out_got = swap_cores(out_other)
    sum_four = jnp.sum(after(four_got, one_back).astype(F32), axis=0)

    grad_two, back_mine, back_other, gain_sum, nbias_sum, two_sum = tail_call(
        core_at,
        after(dv_own, sum_four),
        two_slope,
        two_turned,
        one_back,
        tok_pair,
        normed,
    )
    mix_grads = jnp.concatenate([grad_rate[:, 0], grad_coeff[:, 0], grad_skip[:, 0]], axis=1)
    mix_grads = scatter_bits(
        mix_grads.reshape((2,) * len(top) + (rows_h, -1)), size, sorted(top)[::-1], top, F32
    )
    back_got = swap_cores(back_other)
    rest = split_off(to_last(rest), last, grad_two)
    rest_sent = rest[1]
    rest = go_on(rest, last)
    small_grads = small_pack(after(grad_two, *rest_sent), gain_sum, nbias_sum, out_sum, one_sum, gate_sum, two_sum)
    small_got = lax.all_to_all(
        small_grads, everyone, split_axis=0, concat_axis=0
    )
    input_grad = input_call(
        core_at, back_mine, after(back_got, small_grads), tokens, out_grad, gain_f
    )


    def merge_f(mine, other):
        rows = mine.shape[0]
        parts = (mine.reshape(rows, size, rows_f), other.reshape(rows, size, rows_f))
        return natural_pair(*parts, axis=2).reshape(rows, 2 * f_half)

    branch = out_mine + after(out_got, small_grads).astype(F32)
    mixed = (live[:tok_dev] * (tokens.astype(F32) + branch + bfour_f)).astype(BF)
    rest_sum = total(rest, input_grad, mixed)
    one_mine, one_other = mine_other(rest_sum[: 2 * rows_e].reshape(2, rows_e, f_half), 0)
    three_sum = rest_sum[2 * rows_e :]
    rest_got = swap_cores(jnp.concatenate([one_other, three_sum[rows_h:]], axis=0))
    merged = merge_f(jnp.concatenate([one_mine, three_sum[:rows_h]], axis=0), rest_got)
    sum_one, sum_three = merged[:rows_e], merged[rows_e:]

    small_sum = jnp.sum(
        after(small_got, input_grad).reshape(size, 2, rows_e + vec_rows, h_half).astype(F32), axis=0
    )
    sum_two = jnp.transpose(
        small_sum[:, :rows_e].reshape(2, rows_e, group, buckets, rows_h), (1, 3, 2, 0, 4)
    ).reshape(rows_e, 2 * h_half)
    vec_sum = jnp.sum(small_sum[:, rows_e:], axis=0).reshape(-1)
    ends = [rows_e, 2 * rows_e, 3 * rows_e, 3 * rows_e + rows_f, 3 * rows_e + 2 * rows_f, vec_len]
    sum_gain, sum_nbias, sum_bfour, sum_bone, sum_bthree, sum_btwo = (
        vec_sum[a:b] for a, b in zip([0] + ends, ends)
    )

    return (
        mixed,
        input_grad,
        sum_gain,
        sum_nbias,
        sum_one,
        sum_bone,
        sum_two,
        sum_btwo,
        sum_three,
        sum_bthree,
        sum_four,
        sum_bfour,
        mix_grads[:, :nstate],
        mix_grads[:, nstate : 2 * nstate],
        mix_grads[:, 2 * nstate],
    )


def solution(mesh):
    both = ("dp", "fsdp")
    rows, vector = P(both, None), P(both)
    in_specs = (
        rows, rows, P(), vector, vector, rows, vector, rows, vector, rows, vector, rows, vector,
        rows, rows, vector,
    )
    out_specs = (
        rows, rows, vector, vector, rows, vector, rows, vector, rows, vector, rows, vector,
        rows, rows, vector,
    )
    return jax.shard_map(
        functools.partial(per_device, mesh.shape["dp"]),
        mesh=mesh,
        in_specs=in_specs,
        out_specs=out_specs,
        check_vma=False,
    )
```

```python
import functools

import jax
import jax.numpy as jnp
from jax import lax
from jax.experimental import pallas as pl
from jax.experimental.pallas import tpu as pltpu
from jax.sharding import PartitionSpec as P

SEQ = 16384
QBLK = 256
F32 = jnp.float32
BF = jnp.bfloat16
SWAP = [(0, 1), (1, 0)]
ROOM = 52
TOOK = dict(
    norm=10, mixer_tables=12, mixer_forward=13, early=24, gate=13, grad_four=11, grad_one=12,
    mixer_backward=20, grad_three=8, out=20, tail=1, input_grad=7,
)


def costing(name):
    return pl.CostEstimate(flops=int(TOOK[name] * 3.3e+06 * 300), bytes_accessed=int(TOOK[name] * 3.3e+06), transcendentals=0)


def mm(left, right, left_dim, right_dim):
    return lax.dot_general(
        left, right, (((left_dim,), (right_dim,)), ((), ())), preferred_element_type=F32
    )


def split(value):
    high = value.astype(BF)
    return high, (value - high.astype(F32)).astype(BF)


def iotas(rows, cols):
    return (
        lax.broadcasted_iota(jnp.int32, (rows, cols), 0),
        lax.broadcasted_iota(jnp.int32, (rows, cols), 1),
    )


def shift_rows(x, k, backward):
    n = x.shape[0]
    row = iotas(*x.shape)[0]
    if backward:
        return jnp.where(row < n - k, pltpu.roll(x, n - k, 0), 0.0)
    return jnp.where(row >= k, pltpu.roll(x, k, 0), 0.0)


def states(x, rate, group, backward):
    blocks = x.shape[0] // group
    order = list(range(blocks))[:: -1 if backward else 1]
    decay = jnp.exp(-rate * float(QBLK))
    local, state = {}, None
    for b in order:
        local[b] = state
        here = x[b * group : (b + 1) * group]
        state = here if state is None else state * decay + here
    k = 1
    while k < group:
        state = state + shift_rows(state, k, backward) * jnp.exp(-rate * float(QBLK * blocks * k))
        k *= 2
    carry = shift_rows(state, 1, backward)
    out = {}
    for step, b in enumerate(order):
        far = carry * jnp.exp(-rate * float(QBLK * step)) if step else carry
        out[b] = far if local[b] is None else far + local[b]
    return jnp.concatenate([out[b] for b in range(blocks)], axis=0)


def flip_matrix():
    i, j = iotas(QBLK, QBLK)
    return jnp.where(i + j == QBLK - 1, 1.0, 0.0).astype(BF)


def base_of(rate):
    return jnp.where(rate * float(QBLK) < 1.0, 1.0, 0.0)


def row_sums(x):
    return jnp.sum(x.astype(F32), axis=1, keepdims=True)


def through(rows, table, base):
    return mm(rows, table, 1, 0) + row_sums(rows) * base


def table_kernel(lr_ref, co_ref, d_ref, dt_ref, t_ref):
    i, j = iotas(QBLK, QBLK)
    for c in range(lr_ref.shape[0]):
        rate, coeff = jnp.exp(lr_ref[c]), co_ref[c]
        row = lax.broadcasted_iota(jnp.int32, (8, rate.shape[1]), 0).astype(F32)
        table = jnp.exp(-rate * row)
        step = 8
        while step < QBLK:
            table = jnp.concatenate([table, table * jnp.exp(-rate * float(step))], axis=0)
            step *= 2
        lowered = table - base_of(rate)
        d_ref[c] = lowered.astype(BF)
        turned = lowered.T
        dt_ref[c] = turned.astype(BF)
        high, low = split(jnp.broadcast_to(coeff, (8, coeff.shape[1])))
        t_high, t_low = split(turned)
        kern = (
            mm(high, t_high, 1, 0) + mm(low, t_high, 1, 0) + mm(high, t_low, 1, 0)
        )[0:1] + row_sums(coeff * base_of(rate))
        rolled = pltpu.roll(jnp.broadcast_to(kern, (QBLK, QBLK)), 0, 1, stride=1, stride_axis=0)
        t_ref[c] = jnp.where(j >= i, rolled, 0.0).astype(BF)


def far_rows(entering, scale, turned, base):
    rows = entering.shape[0]
    scaled = entering * scale
    both = mm(jnp.concatenate(split(scaled), axis=0), turned, 1, 0)
    return both[:rows] + both[rows:] + row_sums(scaled * base)


def lanes_of(b, turn, total):
    start = b * QBLK + turn * (total // 2)
    start = jnp.where(start >= total, start - total, start)
    return pl.ds(pl.multiple_of(start, QBLK), QBLK)


def take_rows(x_ref, rows_ref, turn):
    group, _, total = x_ref.shape
    for b in range(0, total // QBLK, 2):
        pair = [
            jnp.swapaxes(x_ref[:, :, lanes_of(b + k, turn, total)].astype(F32), 0, 1)
            for k in range(2)
        ]
        rows_ref[:, b * group : (b + 2) * group, :] = jnp.concatenate(pair, axis=1).astype(BF)


def give_rows(rows_ref, x_ref, turn):
    group, _, total = x_ref.shape
    for b in range(0, total // QBLK, 2):
        pair = rows_ref[:, b * group : (b + 2) * group, :].astype(F32)
        for k in range(2):
            x_ref[:, :, lanes_of(b + k, turn, total)] = jnp.swapaxes(
                pair[:, k * group : (k + 1) * group], 0, 1
            ).astype(BF)


def forward_kernel(turn_ref, v_ref, d_ref, dt_ref, t_ref, lr_ref, co_ref, sk_ref, y_ref, en_ref, rows_ref, back_ref):
    per, group, turn = d_ref.shape[0], v_ref.shape[0], turn_ref[0]
    part, parts = pl.program_id(1), pl.num_programs(1)
    count = rows_ref.shape[1]

    @pl.when(part == 0)
    def _():
        take_rows(v_ref, rows_ref, turn)

    mine = rows_ref[pl.ds(part * per, per)]
    flipped = mm(mine.reshape(per * count, QBLK), flip_matrix(), 1, 0).astype(BF)
    for c in range(per):
        v = mine[c]
        rate = jnp.exp(lr_ref[c])
        base = base_of(rate)
        ends = through(flipped[c * count : (c + 1) * count], d_ref[c], base)
        entering = states(ends, rate, group, False)
        en_ref[c] = entering
        far = far_rows(entering, co_ref[c] * jnp.exp(-rate), dt_ref[c], base)
        back_ref[part * per + c] = (
            far + mm(v, t_ref[c], 1, 0) + sk_ref[c][:, :1] * v.astype(F32)
        ).astype(BF)

    @pl.when(part == parts - 1)
    def _():
        give_rows(back_ref, y_ref, turn)


def backward_kernel(
    turn_ref, v_ref, dy_ref, en_ref, d_ref, dt_ref, t_ref, lr_ref, co_ref, sk_ref,
    dv_ref, gr_ref, gc_ref, gs_ref, v_rows_ref, dy_rows_ref, back_ref,
):
    per, group, turn = d_ref.shape[0], v_ref.shape[0], turn_ref[0]
    part, parts = pl.program_id(1), pl.num_programs(1)
    count = v_rows_ref.shape[1]
    rows = per * count

    @pl.when(part == 0)
    def _():
        take_rows(v_ref, v_rows_ref, turn)
        take_rows(dy_ref, dy_rows_ref, turn)

    flip = flip_matrix()
    v_all = v_rows_ref[pl.ds(part * per, per)].reshape(rows, QBLK)
    dy_all = dy_rows_ref[pl.ds(part * per, per)].reshape(rows, QBLK)
    flipped = mm(jnp.concatenate([v_all, dy_all], axis=0), flip, 1, 0)
    lane = lax.broadcasted_iota(jnp.int32, (rows, QBLK), 1).astype(F32)
    v_lag = (flipped[:rows] * lane).astype(BF)
    dy_lag = (dy_all.astype(F32) * lane).astype(BF)
    flipped = flipped.astype(BF)
    i, j = iotas(QBLK, QBLK)
    lag = lax.broadcasted_iota(jnp.int32, (1, QBLK), 1).astype(F32)
    back = []
    for c in range(per):
        here = slice(c * count, (c + 1) * count)
        dy = dy_all[here]
        v_flip, dy_flip = flipped[here], flipped[rows + c * count : rows + (c + 1) * count]
        rate, coeff = jnp.exp(lr_ref[c]), co_ref[c]
        base = base_of(rate)
        pairs = pltpu.roll(mm(v_flip, dy, 0, 0), 1, 1, stride=1, stride_axis=0)
        near = jnp.sum(jnp.where(j <= i, pairs, 0.0), axis=0, keepdims=True)
        near_rows = jnp.concatenate(
            split(
                jnp.concatenate(
                    [jnp.broadcast_to(near, (8, QBLK)), jnp.broadcast_to(near * lag, (8, QBLK))],
                    axis=0,
                )
            ),
            axis=0,
        )
        sums = through(
            jnp.concatenate([dy, dy_lag[here], v_lag[here], near_rows], axis=0), d_ref[c], base
        )
        starts, starts_lag, ends_lag = (sums[k * count : (k + 1) * count] for k in range(3))
        inner = sums[3 * count : 3 * count + 16] + sums[3 * count + 16 :]
        leaving = states(starts, rate, group, True)
        entering = en_ref[c]
        one = jnp.exp(-rate)
        far = far_rows(leaving, coeff * one, dt_ref[c], base)
        back.append(
            (
                far + mm(dy_flip, t_ref[c], 1, 0) + sk_ref[c][:, :1] * dy_flip.astype(F32)
            ).astype(BF)
        )
        whole = jnp.exp(-rate * float(QBLK))
        outer = jnp.sum(entering * starts, axis=0, keepdims=True)
        moment = jnp.sum(
            ends_lag * leaving + entering * (starts_lag + (float(QBLK) * whole) * leaving),
            axis=0,
            keepdims=True,
        )
        gc_ref[c] = inner[0:1] + one * outer
        gr_ref[c] = -(coeff * rate) * (inner[8:9] + one * (moment + outer))
        gs_ref[c] = jnp.broadcast_to(near[:, :1], (1, 128))
    turned = mm(jnp.concatenate(back, axis=0), flip, 1, 0).astype(BF)
    back_ref[pl.ds(part * per, per)] = turned.reshape(per, count, QBLK)

    @pl.when(part == parts - 1)
    def _():
        give_rows(back_ref, dv_ref, turn)


def mixer_tables(log_rate, coeff):
    chans, _, n = log_rate.shape
    per = 4

    def spec(rows, cols):
        return pl.BlockSpec((per, rows, cols), lambda i: (i, 0, 0))

    shapes = [(QBLK, n), (n, QBLK), (QBLK, QBLK)]
    return pl.pallas_call(
        table_kernel,
        grid=(chans // per,),
        in_specs=[spec(1, n)] * 2,
        out_specs=[spec(*shape) for shape in shapes],
        out_shape=[jax.ShapeDtypeStruct((chans,) + shape, BF) for shape in shapes],
        compiler_params=pltpu.CompilerParams(vmem_limit_bytes=ROOM * 2**20),
        cost_estimate=costing("mixer_tables"),
        name="mixer_tables",
    )(log_rate, coeff)


def mixer_call(kernel, turn, tokens_in, by_channel, outs, name):
    group, chans, total = tokens_in[0].shape
    tall, per = 16, 8
    parts = tall // per
    count = group * (total // QBLK)

    def spec(shape):
        return pl.BlockSpec((per,) + tuple(shape[1:]), lambda i, j, *_: (i * parts + j, 0, 0))

    wide = pl.BlockSpec((group, tall, total), lambda i, j, *_: (0, i, 0))
    return pl.pallas_call(
        kernel,
        grid_spec=pltpu.PrefetchScalarGridSpec(
            num_scalar_prefetch=1,
            grid=(chans // tall, parts),
            in_specs=[wide] * len(tokens_in) + [spec(x.shape) for x in by_channel],
            out_specs=[wide] + [spec(shape) for shape, _ in outs],
            scratch_shapes=[pltpu.VMEM((tall, count, QBLK), BF)] * (len(tokens_in) + 1),
        ),
        out_shape=[jax.ShapeDtypeStruct((group, chans, total), BF)]
        + [jax.ShapeDtypeStruct(shape, kind) for shape, kind in outs],
        compiler_params=pltpu.CompilerParams(vmem_limit_bytes=ROOM * 2**20),
        cost_estimate=costing(name),
        name=name,
    )(turn, *tokens_in, *by_channel)


def mixer_forward(turn, v, tables, params):
    group, chans, total = v.shape
    n = params[0].shape[2]
    states_of = (chans, group * (total // QBLK), n)
    return mixer_call(
        forward_kernel, turn, [v], [*tables, *params], [(states_of, F32)], "mixer_forward"
    )


def mixer_backward(turn, v, dy, entering, tables, params):
    chans, n = v.shape[1], params[0].shape[2]
    return mixer_call(
        backward_kernel,
        turn,
        [v, dy],
        [entering, *tables, *params],
        [((chans, 1, n), F32), ((chans, 1, n), F32), ((chans, 1, 128), F32)],
        "mixer_backward",
    )


TILE = 512


def call(kernel, grid, core, ins, outs, name, room, scratch=()):
    return pl.pallas_call(
        kernel,
        grid_spec=pltpu.PrefetchScalarGridSpec(
            num_scalar_prefetch=1,
            grid=(grid,),
            in_specs=[
                pl.BlockSpec(block, index, pipeline_mode=None if index in MOVING else pl.Buffered(1))
                for _, block, index in ins
            ],
            out_specs=[pl.BlockSpec(block, index) for _, _, block, index in outs],
            scratch_shapes=list(scratch),
        ),
        out_shape=[jax.ShapeDtypeStruct(shape, kind) for shape, kind, _, _ in outs],
        compiler_params=pltpu.CompilerParams(vmem_limit_bytes=room * 2**20),
        cost_estimate=costing(name),
        name=name,
    )(core, *[array for array, _, _ in ins])


def row_tile(m, _):
    return (m, 0)


def col_tile(m, _):
    return (0, m)


def turned_tile(m, _):
    half = pl.num_programs(0) // 2
    return (0, jnp.where(m < half, m + half, m - half))


def fixed(m, _):
    return (0, 0)


MOVING = (row_tile, col_tile, turned_tile)


def first_rows(m, _):
    return (jnp.minimum(m, pl.num_programs(0) // 2 - 1), 0)


def last_rows(m, _):
    return (jnp.maximum(m - pl.num_programs(0) // 2, 0), 0)


def strips_of(start, stop, strip):
    while start < stop:
        k = start // strip
        end = min(stop, (k + 1) * strip)
        yield k, slice(start - k * strip, end - k * strip)
        start = end


def strip_columns(ref, total, start, stop, order):
    rows = ref.shape[2] // (total // ref.shape[3])
    return jnp.concatenate(
        [
            jnp.concatenate(
                [
                    ref[chip, core, k * rows : (k + 1) * rows, lanes]
                    for chip in order
                    for core in range(ref.shape[1])
                ],
                axis=0,
            )
            for k, lanes in strips_of(start, stop, ref.shape[3])
        ],
        axis=1,
    )


def strip_rows(ref, strips, start, stop):
    rows = ref.shape[2] // strips
    return jnp.concatenate(
        [
            jnp.concatenate(
                [
                    ref[chip, 0, k * rows + part.start : k * rows + part.stop, :]
                    for chip, part in strips_of(start, stop, rows)
                ],
                axis=0,
            )
            for k in range(strips)
        ],
        axis=1,
    )


def col_sum(x):
    return jnp.sum(x.astype(F32), axis=0, keepdims=True)


def hat_of(x):
    x = x.astype(F32)
    centered = x - jnp.mean(x, axis=-1, keepdims=True)
    inv_std = lax.rsqrt(jnp.mean(centered * centered, axis=-1, keepdims=True) + 1e-05)
    return centered * inv_std, inv_std


def slope_and_gelu(h):
    phi = 0.5 + 0.5 * lax.erf(h * 0.7071067811865476)
    return h * phi, phi + h * jnp.exp(-0.5 * h * h) * 0.3989422804014327


def norm_kernel(
    _, tok_ref, cot_ref, live_ref, gain_ref, bias_ref, w_ref, b_ref, n_ref, g_ref, v_ref, s_ref, sum_ref
):
    m = pl.program_id(0)

    @pl.when(m == 0)
    def _():
        sum_ref[...] = jnp.zeros_like(sum_ref)

    hat, _ = hat_of(tok_ref[...])
    normed = (hat * gain_ref[...] + bias_ref[...]).astype(BF)
    n_ref[...] = normed
    g = jnp.where(live_ref[...][:, :1] > 0.0, cot_ref[...], jnp.zeros((), BF))
    g_ref[...] = g

    @pl.when(m < pl.num_programs(0) // 2)
    def _():
        sum_ref[...] += col_sum(g)

    v, s = slope_and_gelu(mm(w_ref[...], normed, 1, 1) + b_ref[...][:, :1])
    v_ref[...] = v.astype(BF)
    s_ref[...] = s.astype(BF)


def norm_call(core, tok, cot, live, gain, bias, w_turned, b):
    tokens, width = tok.shape
    chans = w_turned.shape[0]
    rows, cols = (TILE, width), (chans, TILE)
    return call(
        norm_kernel,
        tokens // TILE,
        core,
        [
            (tok, rows, row_tile),
            (cot, rows, row_tile),
            (live, (TILE, 128), row_tile),
            (gain, (1, width), fixed),
            (bias, (1, width), fixed),
            (w_turned, (chans, width), fixed),
            (b, (chans, 128), fixed),
        ],
        [((tokens, width), BF, rows, row_tile)] * 2
        + [((chans, tokens), BF, cols, col_tile)] * 2
        + [((1, width), F32, (1, width), fixed)],
        "norm",
        ROOM,
    )


def early_kernel(
    _, x_ref, g_ref, b1_ref, w1_ref, w4_ref, w3m_ref, w3o_ref,
    u_ref, dzs_ref, dgate_ref, mine_ref, other_ref, sum_ref, *, order,
):
    total = u_ref.shape[1]
    cols, chips = 768, range(w1_ref.shape[0])
    e_strips = g_ref.shape[1] // w4_ref.shape[3]

    @pl.when(pl.program_id(0) == 0)
    def _():
        sum_ref[...] = jnp.zeros_like(sum_ref)

    for n in range(total // cols):
        at = slice(n * cols, (n + 1) * cols)
        w1 = strip_columns(w1_ref, total, at.start, at.stop, chips)
        u, s = slope_and_gelu(mm(x_ref[...], w1, 1, 0) + b1_ref[:, at])
        dz = mm(g_ref[...], strip_rows(w4_ref, e_strips, at.start, at.stop), 1, 1)
        dgate = (dz * u).astype(BF)
        u_ref[:, at] = u.astype(BF)
        dzs_ref[:, at] = (dz * s).astype(BF)
        dgate_ref[:, at] = dgate
        sum_ref[:, at] += col_sum(dgate)
    mine_ref[...] = mm(strip_columns(w3m_ref, total, 0, total, order), dgate_ref[...], 1, 1)
    other = mm(strip_columns(w3o_ref, total, 0, total, order), dgate_ref[...], 1, 1)
    other_ref[...] = other.astype(BF)


def early_call(core, x, g, b1, weights, order):
    tokens, width = x.shape
    cols = b1.shape[1]
    chans = weights[2][1][2] * weights[2][1][3] * len(order) // cols
    wide, tall = (TILE, cols), (chans, TILE)
    return call(
        functools.partial(early_kernel, order=order),
        tokens // TILE,
        core,
        [
            (x, (TILE, width), row_tile),
            (g, (TILE, width), row_tile),
            (b1, (1, cols), fixed),
            *weights,
        ],
        [((tokens, cols), BF, wide, row_tile)] * 3
        + [
            ((chans, tokens), F32, tall, col_tile),
            ((chans, tokens), BF, tall, turned_tile),
            ((1, cols), F32, (1, cols), fixed),
        ],
        "early",
        ROOM,
    )


def gate_kernel(
    _, ym_ref, yo_ref, b3_ref, u_ref, dzs_ref, w3m_ref, w3o_ref, z_ref, dh_ref, sum_ref, *, order
):
    total, cols = u_ref.shape[1], 256

    @pl.when(pl.program_id(0) == 0)
    def _():
        sum_ref[...] = jnp.zeros_like(sum_ref)

    y = jnp.concatenate([ym_ref[...], yo_ref[...]], axis=0).T
    for n in range(total // cols):
        at = slice(n * cols, (n + 1) * cols)
        w3 = jnp.concatenate(
            [strip_columns(ref, total, at.start, at.stop, order) for ref in (w3m_ref, w3o_ref)],
            axis=0,
        )
        gate = mm(y, w3, 1, 0) + b3_ref[:, at]
        z_ref[:, at] = (u_ref[:, at].astype(F32) * gate).astype(BF)
        dh = (dzs_ref[:, at].astype(F32) * gate).astype(BF)
        dh_ref[:, at] = dh
        sum_ref[:, at] += col_sum(dh)


def gate_call(core, y_mine, y_other, b3, u, dzs, weights, order):
    tokens, cols = u.shape
    wide, tall = (TILE, cols), (y_mine.shape[0], TILE)
    return call(
        functools.partial(gate_kernel, order=order),
        tokens // TILE,
        core,
        [
            (y_mine, tall, col_tile),
            (y_other, tall, turned_tile),
            (b3, (1, cols), fixed),
            (u, wide, row_tile),
            (dzs, wide, row_tile),
            *weights[2:],
        ],
        [
            ((tokens, cols), BF, wide, row_tile),
            ((tokens, cols), BF, wide, row_tile),
            ((1, cols), F32, (1, cols), fixed),
        ],
        "gate",
        ROOM,
    )


def out_kernel(_, z_ref, dh_ref, w1_ref, w4_ref, om_ref, oo_ref, p_ref):
    m, total = pl.program_id(0), z_ref.shape[1]
    chips = range(w1_ref.shape[0])
    e_strips = om_ref.shape[1] // w4_ref.shape[3]
    p_ref[...] = mm(dh_ref[...], strip_columns(w1_ref, total, 0, total, chips), 1, 1).astype(BF)
    out = mm(z_ref[...], strip_rows(w4_ref, e_strips, 0, total), 1, 0)

    @pl.when(m < pl.num_programs(0) // 2)
    def _():
        om_ref[...] = out

    @pl.when(m >= pl.num_programs(0) // 2)
    def _():
        oo_ref[...] = out.astype(BF)


def out_call(core, z, dh, width, weights):
    tokens, cols = z.shape
    wide, rows = (TILE, cols), (TILE, width)
    return call(
        out_kernel,
        tokens // TILE,
        core,
        [(z, wide, row_tile), (dh, wide, row_tile), *weights[:2]],
        [
            ((tokens // 2, width), F32, rows, first_rows),
            ((tokens // 2, width), BF, rows, last_rows),
            ((tokens, width), BF, rows, row_tile),
        ],
        "out",
        ROOM,
    )


def tail_kernel(
    _, dv_ref, s_ref, w_ref, p_ref, tok_ref, n_ref, grad_ref, pm_ref, po_ref, gain_ref, bias_ref, sum_ref, total_ref
):
    m = pl.program_id(0)

    @pl.when(m == 0)
    def _():
        gain_ref[...] = jnp.zeros_like(gain_ref)
        bias_ref[...] = jnp.zeros_like(bias_ref)
        sum_ref[...] = jnp.zeros_like(sum_ref)
        total_ref[...] = jnp.zeros_like(total_ref)

    dh = (dv_ref[...].astype(F32) * s_ref[...].astype(F32)).astype(BF)
    total_ref[...] += mm(dh, n_ref[...], 1, 0)
    for k in range(dh.shape[1] // 128):
        sum_ref[...] += dh[:, k * 128 : (k + 1) * 128].astype(F32)
    p = p_ref[...].astype(F32) + mm(dh.T, w_ref[...], 1, 0)
    hat, _ = hat_of(tok_ref[...])
    gain_ref[...] += col_sum(p * hat)
    bias_ref[...] += col_sum(p)

    @pl.when(m == pl.num_programs(0) - 1)
    def _():
        grad_ref[...] = total_ref[...].T.astype(BF)

    @pl.when(m < pl.num_programs(0) // 2)
    def _():
        pm_ref[...] = p

    @pl.when(m >= pl.num_programs(0) // 2)
    def _():
        po_ref[...] = p.astype(BF)


def tail_call(core, dv, slope, w_turned, p, tok, normed):
    chans, tokens = dv.shape
    width = p.shape[1]
    rows, cols = (TILE, width), (chans, TILE)
    return call(
        tail_kernel,
        tokens // TILE,
        core,
        [
            (dv, cols, col_tile),
            (slope, cols, col_tile),
            (w_turned, (chans, width), fixed),
            (p, rows, row_tile),
            (tok, rows, row_tile),
            (normed, rows, row_tile),
        ],
        [
            ((width, chans), BF, (width, chans), fixed),
            ((tokens // 2, width), F32, rows, first_rows),
            ((tokens // 2, width), BF, rows, last_rows),
            ((1, width), F32, (1, width), fixed),
            ((1, width), F32, (1, width), fixed),
            ((chans, 128), F32, (chans, 128), fixed),
        ],
        "tail",
        ROOM,
        [pltpu.VMEM((chans, width), F32)],
    )


def input_kernel(_, mine_ref, got_ref, tok_ref, g_ref, gain_ref, out_ref):
    hat, inv_std = hat_of(tok_ref[...])
    grad = (mine_ref[...] + got_ref[...].astype(F32)) * gain_ref[...]
    out_ref[...] = (
        g_ref[...].astype(F32)
        + inv_std
        * (
            grad
            - jnp.mean(grad, axis=-1, keepdims=True)
            - hat * jnp.mean(grad * hat, axis=-1, keepdims=True)
        )
    ).astype(BF)


def input_call(core, mine, got, tok, g, gain):
    tokens, width = mine.shape
    rows = (256, width)
    return call(
        input_kernel,
        tokens // 256,
        core,
        [(x, rows, row_tile) for x in (mine, got, tok, g)] + [(gain, (1, width), fixed)],
        [((tokens, width), BF, rows, row_tile)],
        "input_grad",
        ROOM,
    )[0]

def keep_and_send(here, out_ref, runs, keep_ref, send_refs):
    for k, ref in enumerate((keep_ref, *send_refs)):
        part = jnp.concatenate(
            [
                out_ref[pl.ds(pl.multiple_of((at + (here ^ k)) * runs, runs), runs), :]
                for at in range(0, out_ref.shape[0] // runs, 4)
            ],
            axis=0,
        )
        ref[...] = part.astype(ref.dtype)


def grad_kernel(here_ref, a_ref, b_ref, keep_ref, s1_ref, s2_ref, s3_ref, out_ref, *, runs):
    out_ref[...] = mm(a_ref[...], b_ref[...], 0, 0)
    keep_and_send(here_ref[0], out_ref, runs, keep_ref, (s1_ref, s2_ref, s3_ref))


def grad_call(here, a, b, runs, tile, name):
    rows, cols = a.shape[1], b.shape[1]
    part, shape = (tile // 4, cols), (rows // 4, cols)
    return call(
        functools.partial(grad_kernel, runs=runs),
        rows // tile,
        here,
        [(a, (a.shape[0], tile), col_tile), (b, b.shape, fixed)],
        [(shape, kind, part, row_tile) for kind in (F32, BF, BF, BF)],
        name,
        ROOM,
        [pltpu.VMEM((tile, cols), F32)],
    )


def mixed_grad_kernel(here_ref, ym_ref, yo_ref, b_ref, keep_ref, s1_ref, s2_ref, s3_ref, out_ref, *, runs):
    half, rows = b_ref.shape[0] // 2, ym_ref.shape[0]
    out_ref[:rows] = mm(ym_ref[...], b_ref[...], 1, 0)
    out_ref[rows:] = mm(yo_ref[:, half:], b_ref[:half], 1, 0) + mm(
        yo_ref[:, :half], b_ref[half:], 1, 0
    )
    keep_and_send(here_ref[0], out_ref, runs, keep_ref, (s1_ref, s2_ref, s3_ref))


def mixed_grad_call(here, y_mine, y_other, b, runs, name):
    rows, cols, tile = 2 * y_mine.shape[0], b.shape[1], 512
    part, shape = (rows // 4, tile), (rows // 4, cols)
    return call(
        functools.partial(mixed_grad_kernel, runs=runs),
        cols // tile,
        here,
        [(y_mine, y_mine.shape, fixed), (y_other, y_other.shape, fixed), (b, (b.shape[0], tile), col_tile)],
        [(shape, kind, part, col_tile) for kind in (F32, BF, BF, BF)],
        name,
        ROOM,
        [pltpu.VMEM((rows, tile), F32)],
    )


def after(x, *others):
    return lax.optimization_barrier((x,) + others)[0]


def swap_cores(x):
    return lax.ppermute(x, "fsdp", SWAP)


def across(x, size, flip):
    return lax.ppermute(x, "dp", [(i, i ^ flip) for i in range(size)])


def bit_of(bit):
    return (lax.axis_index("dp") >> bit) & 1


def gather_bits(x, size, order, layout):
    have = []
    for bit in order:
        other = across(x, size, 1 << bit)
        mine = bit_of(bit) == 1
        have = [b for b in layout if b in have or b == bit]
        x = jnp.stack(
            [jnp.where(mine, other, x), jnp.where(mine, x, other)], axis=have.index(bit)
        )
    return x


def scatter_bits(x, size, order, layout, send_type):
    have = list(layout)
    for bit in order:
        axis = have.index(bit)
        mine = bit_of(bit)
        theirs = lax.dynamic_index_in_dim(x, 1 - mine, axis, keepdims=False)
        kept = lax.dynamic_index_in_dim(x, mine, axis, keepdims=False)
        x = kept.astype(F32) + across(theirs.astype(send_type), size, 1 << bit).astype(F32)
        have.remove(bit)
    return x


def per_device(
    size,
    tokens,
    cotangent,
    lengths,
    norm_gain,
    norm_bias,
    w_one,
    b_one,
    w_two,
    b_two,
    w_three,
    b_three,
    w_four,
    b_four,
    log_rate,
    ssm_coeff,
    ssm_skip,
):
    bits = size.bit_length() - 1
    tok_dev, width = tokens.shape
    rows_e, rows_f, rows_h = w_one.shape[0], w_four.shape[0], w_three.shape[0]
    f_half, h_half = size * rows_f, size * rows_h
    buckets = lengths.shape[0]
    group = size // buckets
    group_bits = group.bit_length() - 1
    chans = buckets * rows_h
    tok_chip = 2 * tok_dev
    per_dev = tok_dev // QBLK
    nstate = log_rate.shape[1]
    natural = list(range(bits))[::-1]
    by_owner = natural[bits - group_bits :] + natural[: bits - group_bits]
    top = natural[: bits - group_bits]
    order_a = list(range(2, bits)) + [0, 1]
    order_b = list(range(2, bits)) + [1, 0]
    core = lax.axis_index("fsdp")
    first = core == 0
    chip = lax.axis_index("dp")
    core_at = jnp.reshape(core, (1,)).astype(jnp.int32)
    everyone = ("dp", "fsdp")

    def natural_pair(mine, other, axis=0):
        return jnp.stack(
            [jnp.where(first, mine, other), jnp.where(first, other, mine)], axis=axis
        )

    def mine_other(parts, axis):
        a = lax.index_in_dim(parts, 0, axis, keepdims=False)
        b = lax.index_in_dim(parts, 1, axis, keepdims=False)
        return jnp.where(first, a, b), jnp.where(first, b, a)

    tok_pair = jnp.concatenate([tokens, swap_cores(tokens)], axis=0)
    cot_pair = jnp.concatenate([cotangent, swap_cores(cotangent)], axis=0)

    two_parts = jnp.moveaxis(
        w_two.reshape(rows_e, buckets, group, 2, rows_h), (3, 2, 1), (0, 2, 3)
    ).reshape(2, rows_e, h_half)
    vec = jnp.concatenate([norm_gain, norm_bias, b_four, b_one, b_three, b_two])
    vec_len = vec.shape[0]
    vec_rows = -(-vec_len // h_half)
    vec = jnp.pad(vec, (0, vec_rows * h_half - vec_len)).reshape(1, vec_rows, h_half)
    small = jnp.concatenate(
        [two_parts, jnp.broadcast_to(vec, (2, vec_rows, h_half))], axis=1
    )
    small = jnp.broadcast_to(small[None], (size, 2) + small.shape[1:])
    small = lax.all_to_all(
        small.reshape((2 * size,) + small.shape[2:]), everyone, split_axis=0, concat_axis=0
    )
    two_turned = small[:, :rows_e].reshape(width, h_half).T
    vecs = small[:, rows_e:].reshape(2 * size, -1)[:, :vec_len].astype(F32)
    gain_f = vecs[:, :rows_e].reshape(1, width)
    nbias_f = vecs[:, rows_e : 2 * rows_e].reshape(1, width)
    bfour_f = vecs[:, 2 * rows_e : 3 * rows_e].reshape(1, width)
    own_vecs, _ = mine_other(vecs.reshape(size, 2, vec_len)[:, :, 3 * rows_e :], 1)
    bone_f = own_vecs[:, :rows_f].reshape(1, f_half)
    bthree_f = own_vecs[:, rows_f : 2 * rows_f].reshape(1, f_half)
    btwo_f = (
        own_vecs[:, 2 * rows_f :].reshape(buckets, group, rows_h).swapaxes(0, 1).reshape(h_half, 1)
    )

    strip = 512
    f_strips, e_strips = f_half // strip, width // strip

    def by_half(x):
        rows = x.shape[0]
        parts = jnp.moveaxis(x.reshape(rows, size, 2, rows_f), 2, 0).reshape(2, rows, f_half)
        parts = jnp.moveaxis(parts.reshape(2, rows, f_strips, strip), 2, 1)
        return parts.reshape(2 * f_strips * rows, strip)

    packed = jnp.concatenate(
        [w_four[:, k * strip : (k + 1) * strip] for k in range(e_strips)]
        + [by_half(w_one), by_half(w_three)],
        axis=0,
    )
    gathered = lax.all_gather(packed, everyone, axis=0)
    four_end = e_strips * rows_f
    one_end = four_end + 2 * f_strips * rows_e
    gathered = gathered.reshape(size, 2, -1, strip)
    one_rows, three_rows = f_strips * rows_e, f_strips * rows_h

    def block(chips, cores, rows):
        return (chips, cores, rows, strip)

    if rows_h % 16 == 0 and four_end % one_rows == 0 and one_end % three_rows == 0:
        one_at, three_at = four_end // one_rows, one_end // three_rows
        order = [b * group + j for j in range(group) for b in range(buckets)]
        weights = [
            (gathered, block(size, 2, one_rows), lambda m, c: (0, 0, one_at + c[0], 0)),
            (gathered, block(size, 1, four_end), lambda m, c: (0, c[0], 0, 0)),
            (gathered, block(size, 1, three_rows), lambda m, c: (0, c[0], three_at + c[0], 0)),
            (gathered, block(size, 1, three_rows), lambda m, c: (0, 1 - c[0], three_at + c[0], 0)),
        ]
    else:
        order = [0]
        four_half = gathered[:, :, :four_end].reshape(size, 2, e_strips, rows_f, strip)
        four_half = lax.dynamic_index_in_dim(four_half, core, 1, keepdims=False).swapaxes(0, 1)
        one_half = gathered[:, :, four_end:one_end].reshape(2 * size, 2, f_strips, rows_e, strip)
        one_half = lax.dynamic_index_in_dim(one_half, core, 1, keepdims=False).swapaxes(0, 1)
        three_half = gathered[:, :, one_end:].reshape(
            buckets, group, 2, 2, f_strips, rows_h, strip
        )
        three_half = lax.dynamic_index_in_dim(three_half, core, 3, keepdims=False)
        three_half = jnp.transpose(three_half, (2, 3, 1, 0, 4, 5))
        three_half = mine_other(three_half, 0)
        weights = [
            (x.reshape(1, 1, -1, strip), block(1, 1, x.size // strip), lambda m, c: (0, 0, 0, 0))
            for x in (one_half, four_half, *three_half)
        ]

    params = gather_bits(
        jnp.concatenate(
            [log_rate, ssm_coeff, jnp.broadcast_to(ssm_skip[:, None], (rows_h, 128))], axis=1
        ),
        size,
        sorted(top),
        top,
    ).reshape(chans, 1, -1)
    mix_params = (
        params[..., :nstate],
        params[..., nstate : 2 * nstate],
        params[..., 2 * nstate :],
    )
    tables = mixer_tables(*mix_params[:2])
    groups = [[b * group + j for j in range(group)] for b in range(buckets)]

    def exchange(x):
        return lax.all_to_all(x, "dp", split_axis=0, concat_axis=0, axis_index_groups=groups)

    def to_owner(x):
        return exchange(x.reshape(group, chans, tok_chip))

    def from_owner(x):
        return exchange(x).reshape(h_half, tok_chip)

    def swap_turned(x):
        got = swap_cores(x)
        return jnp.concatenate([got[:, tok_dev:], got[:, :tok_dev]], axis=1)

    device = 2 * chip + core
    lane = jnp.arange(tok_dev, dtype=jnp.int32)
    place = jnp.concatenate([device * tok_dev + lane, (device ^ 1) * tok_dev + lane])
    bucket_range = jnp.arange(buckets, dtype=jnp.int32)
    limit = jnp.sum(
        jnp.where((place // SEQ)[:, None] == bucket_range[None, :], lengths[None, :], 0), axis=1
    )
    live = (place % SEQ < limit).astype(F32)[:, None]

    normed, out_grad, reduced_t, two_slope, out_sum = norm_call(
        core_at,
        tok_pair,
        cot_pair,
        jnp.broadcast_to(live, (tok_chip, 128)),
        gain_f,
        nbias_f,
        two_turned,
        jnp.broadcast_to(btwo_f, (h_half, 128)),
    )
    v_seq = to_owner(reduced_t)
    y_seq, entering = mixer_forward(core_at, v_seq, tables, mix_params)
    y_own = from_owner(y_seq)
    y_other = swap_cores(y_own)

    def small_pack(grad_two, gain_sum, nbias_sum, out_sum, one_sum, gate_sum, two_sum):
        def by_device(x):
            return x.reshape(2 * size, -1)

        def by_core(x):
            zero = jnp.zeros_like(x)
            return by_device(natural_pair(x, zero, axis=1))

        grad_btwo = (
            jnp.sum(two_sum, axis=1).reshape(group, buckets, rows_h).swapaxes(0, 1).reshape(size, rows_h)
        )
        vec_grads = jnp.concatenate(
            [
                by_device(gain_sum),
                by_device(nbias_sum),
                by_device(out_sum),
                by_core(one_sum.reshape(size, rows_f)),
                by_core(gate_sum.reshape(size, rows_f)),
                by_core(grad_btwo),
            ],
            axis=1,
        )
        vec_grads = jnp.pad(vec_grads, ((0, 0), (0, vec_rows * h_half - vec_len)))
        return jnp.concatenate(
            [
                grad_two.reshape(2 * size, rows_e, h_half).astype(BF),
                vec_grads.reshape(2 * size, vec_rows, h_half).astype(BF),
            ],
            axis=1,
        )

    act_one, dz_slope, gate_grad, dy_mine, dy_other, gate_sum = early_call(
        core_at, normed, out_grad, bone_f, weights, order
    )
    dy_own = (dy_mine + swap_cores(dy_other).astype(F32)).astype(BF)
    dy_seq = to_owner(dy_own)


    def send_off(sends, low):
        came = {k: across(sends[k - 1], size, k << low) for k in (3, 1, 2)}
        return [came[k] for k in (1, 2, 3)]

    def begin(outputs, have, rest):
        keep, *parts = (x.reshape((2,) * len(have) + rest) for x in outputs)
        return keep, send_off(parts, 0), have

    def split_off(state, low, *others):
        kept, came, have = state
        high = low + 1
        axis = min(have.index(high), have.index(low))
        swapped = have.index(low) < have.index(high)
        shape = kept.shape[:axis] + (4,) + kept.shape[axis + 2 :]
        terms = [kept.reshape(shape)] + [after(x, *others).reshape(shape) for x in came]
        here = (chip >> low) & 3

        def part(k):
            index = here ^ k
            index = ((index & 1) << 1) | (index >> 1) if swapped else index
            return sum(
                lax.dynamic_index_in_dim(x, index, axis, keepdims=False).astype(F32) for x in terms
            )

        return part(0), [part(k).astype(BF) for k in (1, 2, 3)], [b for b in have if b >> 1 != low >> 1]

    def go_on(state, low):
        kept, parts, have = state
        return kept, send_off(parts, low), have

    def to_last(state):
        for low in range(2, bits - 2, 2):
            state = go_on(split_off(state, low), low)
        return state

    def total(state, *others):
        kept, came, _ = state
        return sum((after(x, *others).astype(F32) for x in came), kept)

    here = jnp.reshape(chip & 3, (1,)).astype(jnp.int32)
    last = bits - 2
    far = size // 4
    far_groups = [[4 * g + k for g in range(far)] for k in range(4)]

    product, one_grad, one_sum = gate_call(
        core_at, after(y_own, dy_own), y_other, bthree_f, act_one, dz_slope, weights, order
    )
    grad_four = grad_call(here, product, out_grad, rows_f, 384, "grad_four")
    four = begin(grad_four, natural[:-2], (rows_f, width))
    dv_seq, grad_rate, grad_coeff, grad_skip = mixer_backward(
        core_at, v_seq, after(dy_seq, grad_four[0]), entering, tables, mix_params
    )
    dv_own = from_owner(dv_seq)
    grad_three = mixed_grad_call(
        here, y_own, y_other, after(gate_grad, dv_seq), buckets * rows_h, "grad_three"
    )
    grad_one = grad_call(
        here, normed, after(one_grad, grad_three[0]), 2 * rows_e, 256, "grad_one"
    )

    def stacked(one, three):
        three = three.reshape(2, group // 4, buckets, rows_h, f_half)
        three = jnp.moveaxis(three, (2, 1), (0, 1)).reshape(far, 2 * rows_h, f_half)
        return jnp.concatenate([one.reshape(far, 2 * rows_e, f_half), three], axis=1)

    rest = begin(
        [stacked(x, y) for x, y in zip(grad_one, grad_three)],
        natural[:-2],
        (2 * rows_e + 2 * rows_h, f_half),
    )
    four_parts = total(four, grad_one[0]).astype(BF).reshape(far, rows_f, width)
    four_got = lax.all_to_all(
        after(four_parts, dv_own), "dp", split_axis=0, concat_axis=0, axis_index_groups=far_groups
    )
    out_mine, out_other, one_back = out_call(
        core_at, product, after(one_grad, grad_one[0], dv_own, four_parts), width, weights
    )
    out_got = swap_cores(out_other)
    sum_four = jnp.sum(after(four_got, one_back).astype(F32), axis=0)

    grad_two, back_mine, back_other, gain_sum, nbias_sum, two_sum = tail_call(
        core_at,
        after(dv_own, sum_four),
        two_slope,
        two_turned,
        one_back,
        tok_pair,
        normed,
    )
    mix_grads = jnp.concatenate([grad_rate[:, 0], grad_coeff[:, 0], grad_skip[:, 0]], axis=1)
    mix_grads = scatter_bits(
        mix_grads.reshape((2,) * len(top) + (rows_h, -1)), size, sorted(top)[::-1], top, F32
    )
    back_got = swap_cores(back_other)
    rest = split_off(to_last(rest), last, grad_two)
    rest_sent = rest[1]
    rest = go_on(rest, last)
    small_grads = small_pack(after(grad_two, *rest_sent), gain_sum, nbias_sum, out_sum, one_sum, gate_sum, two_sum)
    small_got = lax.all_to_all(
        small_grads, everyone, split_axis=0, concat_axis=0
    )
    input_grad = input_call(
        core_at, back_mine, after(back_got, small_grads), tokens, out_grad, gain_f
    )


    def merge_f(mine, other):
        rows = mine.shape[0]
        parts = (mine.reshape(rows, size, rows_f), other.reshape(rows, size, rows_f))
        return natural_pair(*parts, axis=2).reshape(rows, 2 * f_half)

    branch = out_mine + after(out_got, small_grads).astype(F32)
    mixed = (live[:tok_dev] * (tokens.astype(F32) + branch + bfour_f)).astype(BF)
    rest_sum = total(rest, input_grad, mixed)
    one_mine, one_other = mine_other(rest_sum[: 2 * rows_e].reshape(2, rows_e, f_half), 0)
    three_sum = rest_sum[2 * rows_e :]
    rest_got = swap_cores(jnp.concatenate([one_other, three_sum[rows_h:]], axis=0))
    merged = merge_f(jnp.concatenate([one_mine, three_sum[:rows_h]], axis=0), rest_got)
    sum_one, sum_three = merged[:rows_e], merged[rows_e:]

    small_sum = jnp.sum(
        after(small_got, input_grad).reshape(size, 2, rows_e + vec_rows, h_half).astype(F32), axis=0
    )
    sum_two = jnp.transpose(
        small_sum[:, :rows_e].reshape(2, rows_e, group, buckets, rows_h), (1, 3, 2, 0, 4)
    ).reshape(rows_e, 2 * h_half)
    vec_sum = jnp.sum(small_sum[:, rows_e:], axis=0).reshape(-1)
    ends = [rows_e, 2 * rows_e, 3 * rows_e, 3 * rows_e + rows_f, 3 * rows_e + 2 * rows_f, vec_len]
    sum_gain, sum_nbias, sum_bfour, sum_bone, sum_bthree, sum_btwo = (
        vec_sum[a:b] for a, b in zip([0] + ends, ends)
    )

    return (
        mixed,
        input_grad,
        sum_gain,
        sum_nbias,
        sum_one,
        sum_bone,
        sum_two,
        sum_btwo,
        sum_three,
        sum_bthree,
        sum_four,
        sum_bfour,
        mix_grads[:, :nstate],
        mix_grads[:, nstate : 2 * nstate],
        mix_grads[:, 2 * nstate],
    )


def solution(mesh):
    both = ("dp", "fsdp")
    rows, vector = P(both, None), P(both)
    in_specs = (
        rows, rows, P(), vector, vector, rows, vector, rows, vector, rows, vector, rows, vector,
        rows, rows, vector,
    )
    out_specs = (
        rows, rows, vector, vector, rows, vector, rows, vector, rows, vector, rows, vector,
        rows, rows, vector,
    )
    return jax.shard_map(
        functools.partial(per_device, mesh.shape["dp"]),
        mesh=mesh,
        in_specs=in_specs,
        out_specs=out_specs,
        check_vma=False,
    )
```

```python
import functools

import jax
import jax.numpy as jnp
from jax import lax
from jax.experimental import pallas as pl
from jax.experimental.pallas import tpu as pltpu
from jax.sharding import PartitionSpec as P

SEQ = 16384
QBLK = 256
F32 = jnp.float32
BF = jnp.bfloat16
SWAP = [(0, 1), (1, 0)]
ROOM = 52
TOOK = dict(
    norm=10, mixer_tables=12, mixer_forward=13, early=24, gate=13, grad_four=11, grad_one=12,
    mixer_backward=20, grad_three=8, out=20, tail=1, input_grad=7,
)


def costing(name):
    return pl.CostEstimate(flops=int(TOOK[name] * 3.3e+06 * 300), bytes_accessed=int(TOOK[name] * 3.3e+06), transcendentals=0)


def mm(left, right, left_dim, right_dim):
    return lax.dot_general(
        left, right, (((left_dim,), (right_dim,)), ((), ())), preferred_element_type=F32
    )


def split(value):
    high = value.astype(BF)
    return high, (value - high.astype(F32)).astype(BF)


def iotas(rows, cols):
    return (
        lax.broadcasted_iota(jnp.int32, (rows, cols), 0),
        lax.broadcasted_iota(jnp.int32, (rows, cols), 1),
    )


def shift_rows(x, k, backward):
    n = x.shape[0]
    row = iotas(*x.shape)[0]
    if backward:
        return jnp.where(row < n - k, pltpu.roll(x, n - k, 0), 0.0)
    return jnp.where(row >= k, pltpu.roll(x, k, 0), 0.0)


def states(x, rate, group, backward):
    blocks = x.shape[0] // group
    order = list(range(blocks))[:: -1 if backward else 1]
    decay = jnp.exp(-rate * float(QBLK))
    local, state = {}, None
    for b in order:
        local[b] = state
        here = x[b * group : (b + 1) * group]
        state = here if state is None else state * decay + here
    k = 1
    while k < group:
        state = state + shift_rows(state, k, backward) * jnp.exp(-rate * float(QBLK * blocks * k))
        k *= 2
    carry = shift_rows(state, 1, backward)
    out = {}
    for step, b in enumerate(order):
        far = carry * jnp.exp(-rate * float(QBLK * step)) if step else carry
        out[b] = far if local[b] is None else far + local[b]
    return jnp.concatenate([out[b] for b in range(blocks)], axis=0)


def flip_matrix():
    i, j = iotas(QBLK, QBLK)
    return jnp.where(i + j == QBLK - 1, 1.0, 0.0).astype(BF)


def base_of(rate):
    return jnp.where(rate * float(QBLK) < 1.0, 1.0, 0.0)


def row_sums(x):
    return jnp.sum(x.astype(F32), axis=1, keepdims=True)


def through(rows, table, base):
    return mm(rows, table, 1, 0) + row_sums(rows) * base


def table_kernel(lr_ref, co_ref, d_ref, dt_ref, t_ref):
    i, j = iotas(QBLK, QBLK)
    for c in range(lr_ref.shape[0]):
        rate, coeff = jnp.exp(lr_ref[c]), co_ref[c]
        row = lax.broadcasted_iota(jnp.int32, (8, rate.shape[1]), 0).astype(F32)
        table = jnp.exp(-rate * row)
        step = 8
        while step < QBLK:
            table = jnp.concatenate([table, table * jnp.exp(-rate * float(step))], axis=0)
            step *= 2
        lowered = table - base_of(rate)
        d_ref[c] = lowered.astype(BF)
        turned = lowered.T
        dt_ref[c] = turned.astype(BF)
        high, low = split(jnp.broadcast_to(coeff, (8, coeff.shape[1])))
        t_high, t_low = split(turned)
        kern = (
            mm(high, t_high, 1, 0) + mm(low, t_high, 1, 0) + mm(high, t_low, 1, 0)
        )[0:1] + row_sums(coeff * base_of(rate))
        rolled = pltpu.roll(jnp.broadcast_to(kern, (QBLK, QBLK)), 0, 1, stride=1, stride_axis=0)
        t_ref[c] = jnp.where(j >= i, rolled, 0.0).astype(BF)


def far_rows(entering, scale, turned, base):
    rows = entering.shape[0]
    scaled = entering * scale
    both = mm(jnp.concatenate(split(scaled), axis=0), turned, 1, 0)
    return both[:rows] + both[rows:] + row_sums(scaled * base)


def lanes_of(b, turn, total):
    start = b * QBLK + turn * (total // 2)
    start = jnp.where(start >= total, start - total, start)
    return pl.ds(pl.multiple_of(start, QBLK), QBLK)


def take_rows(x_ref, rows_ref, turn):
    group, _, total = x_ref.shape
    for b in range(0, total // QBLK, 2):
        pair = [
            jnp.swapaxes(x_ref[:, :, lanes_of(b + k, turn, total)].astype(F32), 0, 1)
            for k in range(2)
        ]
        rows_ref[:, b * group : (b + 2) * group, :] = jnp.concatenate(pair, axis=1).astype(BF)


def give_rows(rows_ref, x_ref, turn):
    group, _, total = x_ref.shape
    for b in range(0, total // QBLK, 2):
        pair = rows_ref[:, b * group : (b + 2) * group, :].astype(F32)
        for k in range(2):
            x_ref[:, :, lanes_of(b + k, turn, total)] = jnp.swapaxes(
                pair[:, k * group : (k + 1) * group], 0, 1
            ).astype(BF)


def forward_kernel(turn_ref, v_ref, d_ref, dt_ref, t_ref, lr_ref, co_ref, sk_ref, y_ref, en_ref, rows_ref, back_ref):
    per, group, turn = d_ref.shape[0], v_ref.shape[0], turn_ref[0]
    part, parts = pl.program_id(1), pl.num_programs(1)
    count = rows_ref.shape[1]

    @pl.when(part == 0)
    def _():
        take_rows(v_ref, rows_ref, turn)

    mine = rows_ref[pl.ds(part * per, per)]
    flipped = mm(mine.reshape(per * count, QBLK), flip_matrix(), 1, 0).astype(BF)
    for c in range(per):
        v = mine[c]
        rate = jnp.exp(lr_ref[c])
        base = base_of(rate)
        ends = through(flipped[c * count : (c + 1) * count], d_ref[c], base)
        entering = states(ends, rate, group, False)
        en_ref[c] = entering
        far = far_rows(entering, co_ref[c] * jnp.exp(-rate), dt_ref[c], base)
        back_ref[part * per + c] = (
            far + mm(v, t_ref[c], 1, 0) + sk_ref[c][:, :1] * v.astype(F32)
        ).astype(BF)

    @pl.when(part == parts - 1)
    def _():
        give_rows(back_ref, y_ref, turn)


def backward_kernel(
    turn_ref, v_ref, dy_ref, en_ref, d_ref, dt_ref, t_ref, lr_ref, co_ref, sk_ref,
    dv_ref, gr_ref, gc_ref, gs_ref, v_rows_ref, dy_rows_ref, back_ref,
):
    per, group, turn = d_ref.shape[0], v_ref.shape[0], turn_ref[0]
    part, parts = pl.program_id(1), pl.num_programs(1)
    count = v_rows_ref.shape[1]
    rows = per * count

    @pl.when(part == 0)
    def _():
        take_rows(v_ref, v_rows_ref, turn)
        take_rows(dy_ref, dy_rows_ref, turn)

    flip = flip_matrix()
    v_all = v_rows_ref[pl.ds(part * per, per)].reshape(rows, QBLK)
    dy_all = dy_rows_ref[pl.ds(part * per, per)].reshape(rows, QBLK)
    flipped = mm(jnp.concatenate([v_all, dy_all], axis=0), flip, 1, 0)
    lane = lax.broadcasted_iota(jnp.int32, (rows, QBLK), 1).astype(F32)
    v_lag = (flipped[:rows] * lane).astype(BF)
    dy_lag = (dy_all.astype(F32) * lane).astype(BF)
    flipped = flipped.astype(BF)
    i, j = iotas(QBLK, QBLK)
    lag = lax.broadcasted_iota(jnp.int32, (1, QBLK), 1).astype(F32)
    back = []
    for c in range(per):
        here = slice(c * count, (c + 1) * count)
        dy = dy_all[here]
        v_flip, dy_flip = flipped[here], flipped[rows + c * count : rows + (c + 1) * count]
        rate, coeff = jnp.exp(lr_ref[c]), co_ref[c]
        base = base_of(rate)
        pairs = pltpu.roll(mm(v_flip, dy, 0, 0), 1, 1, stride=1, stride_axis=0)
        near = jnp.sum(jnp.where(j <= i, pairs, 0.0), axis=0, keepdims=True)
        near_rows = jnp.concatenate(
            split(
                jnp.concatenate(
                    [jnp.broadcast_to(near, (8, QBLK)), jnp.broadcast_to(near * lag, (8, QBLK))],
                    axis=0,
                )
            ),
            axis=0,
        )
        sums = through(
            jnp.concatenate([dy, dy_lag[here], v_lag[here], near_rows], axis=0), d_ref[c], base
        )
        starts, starts_lag, ends_lag = (sums[k * count : (k + 1) * count] for k in range(3))
        inner = sums[3 * count : 3 * count + 16] + sums[3 * count + 16 :]
        leaving = states(starts, rate, group, True)
        entering = en_ref[c]
        one = jnp.exp(-rate)
        far = far_rows(leaving, coeff * one, dt_ref[c], base)
        back.append(
            (
                far + mm(dy_flip, t_ref[c], 1, 0) + sk_ref[c][:, :1] * dy_flip.astype(F32)
            ).astype(BF)
        )
        whole = jnp.exp(-rate * float(QBLK))
        outer = jnp.sum(entering * starts, axis=0, keepdims=True)
        moment = jnp.sum(
            ends_lag * leaving + entering * (starts_lag + (float(QBLK) * whole) * leaving),
            axis=0,
            keepdims=True,
        )
        gc_ref[c] = inner[0:1] + one * outer
        gr_ref[c] = -(coeff * rate) * (inner[8:9] + one * (moment + outer))
        gs_ref[c] = jnp.broadcast_to(near[:, :1], (1, 128))
    turned = mm(jnp.concatenate(back, axis=0), flip, 1, 0).astype(BF)
    back_ref[pl.ds(part * per, per)] = turned.reshape(per, count, QBLK)

    @pl.when(part == parts - 1)
    def _():
        give_rows(back_ref, dv_ref, turn)


def mixer_tables(log_rate, coeff):
    chans, _, n = log_rate.shape
    per = 4

    def spec(rows, cols):
        return pl.BlockSpec((per, rows, cols), lambda i: (i, 0, 0))

    shapes = [(QBLK, n), (n, QBLK), (QBLK, QBLK)]
    return pl.pallas_call(
        table_kernel,
        grid=(chans // per,),
        in_specs=[spec(1, n)] * 2,
        out_specs=[spec(*shape) for shape in shapes],
        out_shape=[jax.ShapeDtypeStruct((chans,) + shape, BF) for shape in shapes],
        compiler_params=pltpu.CompilerParams(vmem_limit_bytes=ROOM * 2**20),
        cost_estimate=costing("mixer_tables"),
        name="mixer_tables",
    )(log_rate, coeff)


def mixer_call(kernel, turn, tokens_in, by_channel, outs, name):
    group, chans, total = tokens_in[0].shape
    tall, per = 16, 8
    parts = tall // per
    count = group * (total // QBLK)

    def spec(shape):
        return pl.BlockSpec((per,) + tuple(shape[1:]), lambda i, j, *_: (i * parts + j, 0, 0))

    wide = pl.BlockSpec((group, tall, total), lambda i, j, *_: (0, i, 0))
    return pl.pallas_call(
        kernel,
        grid_spec=pltpu.PrefetchScalarGridSpec(
            num_scalar_prefetch=1,
            grid=(chans // tall, parts),
            in_specs=[wide] * len(tokens_in) + [spec(x.shape) for x in by_channel],
            out_specs=[wide] + [spec(shape) for shape, _ in outs],
            scratch_shapes=[pltpu.VMEM((tall, count, QBLK), BF)] * (len(tokens_in) + 1),
        ),
        out_shape=[jax.ShapeDtypeStruct((group, chans, total), BF)]
        + [jax.ShapeDtypeStruct(shape, kind) for shape, kind in outs],
        compiler_params=pltpu.CompilerParams(vmem_limit_bytes=ROOM * 2**20),
        cost_estimate=costing(name),
        name=name,
    )(turn, *tokens_in, *by_channel)


def mixer_forward(turn, v, tables, params):
    group, chans, total = v.shape
    n = params[0].shape[2]
    states_of = (chans, group * (total // QBLK), n)
    return mixer_call(
        forward_kernel, turn, [v], [*tables, *params], [(states_of, F32)], "mixer_forward"
    )


def mixer_backward(turn, v, dy, entering, tables, params):
    chans, n = v.shape[1], params[0].shape[2]
    return mixer_call(
        backward_kernel,
        turn,
        [v, dy],
        [entering, *tables, *params],
        [((chans, 1, n), F32), ((chans, 1, n), F32), ((chans, 1, 128), F32)],
        "mixer_backward",
    )


TILE = 512


def call(kernel, grid, core, ins, outs, name, room, scratch=()):
    return pl.pallas_call(
        kernel,
        grid_spec=pltpu.PrefetchScalarGridSpec(
            num_scalar_prefetch=1,
            grid=(grid,),
            in_specs=[
                pl.BlockSpec(block, index, pipeline_mode=None if index in MOVING else pl.Buffered(1))
                for _, block, index in ins
            ],
            out_specs=[pl.BlockSpec(block, index) for _, _, block, index in outs],
            scratch_shapes=list(scratch),
        ),
        out_shape=[jax.ShapeDtypeStruct(shape, kind) for shape, kind, _, _ in outs],
        compiler_params=pltpu.CompilerParams(vmem_limit_bytes=room * 2**20),
        cost_estimate=costing(name),
        name=name,
    )(core, *[array for array, _, _ in ins])


def row_tile(m, _):
    return (m, 0)


def col_tile(m, _):
    return (0, m)


def turned_tile(m, _):
    half = pl.num_programs(0) // 2
    return (0, jnp.where(m < half, m + half, m - half))


def fixed(m, _):
    return (0, 0)


MOVING = (row_tile, col_tile, turned_tile)


def first_rows(m, _):
    return (jnp.minimum(m, pl.num_programs(0) // 2 - 1), 0)


def last_rows(m, _):
    return (jnp.maximum(m - pl.num_programs(0) // 2, 0), 0)


def strips_of(start, stop, strip):
    while start < stop:
        k = start // strip
        end = min(stop, (k + 1) * strip)
        yield k, slice(start - k * strip, end - k * strip)
        start = end


def strip_columns(ref, total, start, stop, order):
    rows = ref.shape[2] // (total // ref.shape[3])
    return jnp.concatenate(
        [
            jnp.concatenate(
                [
                    ref[chip, core, k * rows : (k + 1) * rows, lanes]
                    for chip in order
                    for core in range(ref.shape[1])
                ],
                axis=0,
            )
            for k, lanes in strips_of(start, stop, ref.shape[3])
        ],
        axis=1,
    )


def strip_rows(ref, strips, start, stop):
    rows = ref.shape[2] // strips
    return jnp.concatenate(
        [
            jnp.concatenate(
                [
                    ref[chip, 0, k * rows + part.start : k * rows + part.stop, :]
                    for chip, part in strips_of(start, stop, rows)
                ],
                axis=0,
            )
            for k in range(strips)
        ],
        axis=1,
    )


def col_sum(x):
    return jnp.sum(x.astype(F32), axis=0, keepdims=True)


def hat_of(x):
    x = x.astype(F32)
    centered = x - jnp.mean(x, axis=-1, keepdims=True)
    inv_std = lax.rsqrt(jnp.mean(centered * centered, axis=-1, keepdims=True) + 1e-05)
    return centered * inv_std, inv_std


def slope_and_gelu(h):
    phi = 0.5 + 0.5 * lax.erf(h * 0.7071067811865476)
    return h * phi, phi + h * jnp.exp(-0.5 * h * h) * 0.3989422804014327


def norm_kernel(
    _, tok_ref, cot_ref, live_ref, gain_ref, bias_ref, w_ref, b_ref, n_ref, g_ref, v_ref, s_ref, sum_ref
):
    m = pl.program_id(0)

    @pl.when(m == 0)
    def _():
        sum_ref[...] = jnp.zeros_like(sum_ref)

    hat, _ = hat_of(tok_ref[...])
    normed = (hat * gain_ref[...] + bias_ref[...]).astype(BF)
    n_ref[...] = normed
    g = jnp.where(live_ref[...][:, :1] > 0.0, cot_ref[...], jnp.zeros((), BF))
    g_ref[...] = g

    @pl.when(m < pl.num_programs(0) // 2)
    def _():
        sum_ref[...] += col_sum(g)

    v, s = slope_and_gelu(mm(w_ref[...], normed, 1, 1) + b_ref[...][:, :1])
    v_ref[...] = v.astype(BF)
    s_ref[...] = s.astype(BF)


def norm_call(core, tok, cot, live, gain, bias, w_turned, b):
    tokens, width = tok.shape
    chans = w_turned.shape[0]
    rows, cols = (TILE, width), (chans, TILE)
    return call(
        norm_kernel,
        tokens // TILE,
        core,
        [
            (tok, rows, row_tile),
            (cot, rows, row_tile),
            (live, (TILE, 128), row_tile),
            (gain, (1, width), fixed),
            (bias, (1, width), fixed),
            (w_turned, (chans, width), fixed),
            (b, (chans, 128), fixed),
        ],
        [((tokens, width), BF, rows, row_tile)] * 2
        + [((chans, tokens), BF, cols, col_tile)] * 2
        + [((1, width), F32, (1, width), fixed)],
        "norm",
        ROOM,
    )


def early_kernel(
    _, x_ref, g_ref, b1_ref, w1_ref, w4_ref, w3m_ref, w3o_ref,
    u_ref, dzs_ref, dgate_ref, mine_ref, other_ref, sum_ref, *, order,
):
    total = u_ref.shape[1]
    cols, chips = 768, range(w1_ref.shape[0])
    e_strips = g_ref.shape[1] // w4_ref.shape[3]

    @pl.when(pl.program_id(0) == 0)
    def _():
        sum_ref[...] = jnp.zeros_like(sum_ref)

    for n in range(total // cols):
        at = slice(n * cols, (n + 1) * cols)
        w1 = strip_columns(w1_ref, total, at.start, at.stop, chips)
        u, s = slope_and_gelu(mm(x_ref[...], w1, 1, 0) + b1_ref[:, at])
        dz = mm(g_ref[...], strip_rows(w4_ref, e_strips, at.start, at.stop), 1, 1)
        dgate = (dz * u).astype(BF)
        u_ref[:, at] = u.astype(BF)
        dzs_ref[:, at] = (dz * s).astype(BF)
        dgate_ref[:, at] = dgate
        sum_ref[:, at] += col_sum(dgate)
    mine_ref[...] = mm(strip_columns(w3m_ref, total, 0, total, order), dgate_ref[...], 1, 1)
    other = mm(strip_columns(w3o_ref, total, 0, total, order), dgate_ref[...], 1, 1)
    other_ref[...] = other.astype(BF)


def early_call(core, x, g, b1, weights, order):
    tokens, width = x.shape
    cols = b1.shape[1]
    chans = weights[2][1][2] * weights[2][1][3] * len(order) // cols
    wide, tall = (TILE, cols), (chans, TILE)
    return call(
        functools.partial(early_kernel, order=order),
        tokens // TILE,
        core,
        [
            (x, (TILE, width), row_tile),
            (g, (TILE, width), row_tile),
            (b1, (1, cols), fixed),
            *weights,
        ],
        [((tokens, cols), BF, wide, row_tile)] * 3
        + [
            ((chans, tokens), F32, tall, col_tile),
            ((chans, tokens), BF, tall, turned_tile),
            ((1, cols), F32, (1, cols), fixed),
        ],
        "early",
        ROOM,
    )


def gate_kernel(
    _, ym_ref, yo_ref, b3_ref, u_ref, dzs_ref, w3m_ref, w3o_ref, z_ref, dh_ref, sum_ref, *, order
):
    total, cols = u_ref.shape[1], 256

    @pl.when(pl.program_id(0) == 0)
    def _():
        sum_ref[...] = jnp.zeros_like(sum_ref)

    y = jnp.concatenate([ym_ref[...], yo_ref[...]], axis=0).T
    for n in range(total // cols):
        at = slice(n * cols, (n + 1) * cols)
        w3 = jnp.concatenate(
            [strip_columns(ref, total, at.start, at.stop, order) for ref in (w3m_ref, w3o_ref)],
            axis=0,
        )
        gate = mm(y, w3, 1, 0) + b3_ref[:, at]
        z_ref[:, at] = (u_ref[:, at].astype(F32) * gate).astype(BF)
        dh = (dzs_ref[:, at].astype(F32) * gate).astype(BF)
        dh_ref[:, at] = dh
        sum_ref[:, at] += col_sum(dh)


def gate_call(core, y_mine, y_other, b3, u, dzs, weights, order):
    tokens, cols = u.shape
    tile = 2 * TILE
    wide, tall = (tile, cols), (y_mine.shape[0], tile)
    return call(
        functools.partial(gate_kernel, order=order),
        tokens // tile,
        core,
        [
            (y_mine, tall, col_tile),
            (y_other, tall, turned_tile),
            (b3, (1, cols), fixed),
            (u, wide, row_tile),
            (dzs, wide, row_tile),
            *weights[2:],
        ],
        [
            ((tokens, cols), BF, wide, row_tile),
            ((tokens, cols), BF, wide, row_tile),
            ((1, cols), F32, (1, cols), fixed),
        ],
        "gate",
        ROOM,
    )


def out_kernel(_, z_ref, dh_ref, w1_ref, w4_ref, om_ref, oo_ref, p_ref):
    m, total = pl.program_id(0), z_ref.shape[1]
    chips = range(w1_ref.shape[0])
    e_strips = om_ref.shape[1] // w4_ref.shape[3]
    p_ref[...] = mm(dh_ref[...], strip_columns(w1_ref, total, 0, total, chips), 1, 1).astype(BF)
    out = mm(z_ref[...], strip_rows(w4_ref, e_strips, 0, total), 1, 0)

    @pl.when(m < pl.num_programs(0) // 2)
    def _():
        om_ref[...] = out

    @pl.when(m >= pl.num_programs(0) // 2)
    def _():
        oo_ref[...] = out.astype(BF)


def out_call(core, z, dh, width, weights):
    tokens, cols = z.shape
    wide, rows = (TILE, cols), (TILE, width)
    return call(
        out_kernel,
        tokens // TILE,
        core,
        [(z, wide, row_tile), (dh, wide, row_tile), *weights[:2]],
        [
            ((tokens // 2, width), F32, rows, first_rows),
            ((tokens // 2, width), BF, rows, last_rows),
            ((tokens, width), BF, rows, row_tile),
        ],
        "out",
        ROOM,
    )


def tail_kernel(
    _, dv_ref, s_ref, w_ref, p_ref, tok_ref, n_ref, grad_ref, pm_ref, po_ref, gain_ref, bias_ref, sum_ref, total_ref
):
    m = pl.program_id(0)

    @pl.when(m == 0)
    def _():
        gain_ref[...] = jnp.zeros_like(gain_ref)
        bias_ref[...] = jnp.zeros_like(bias_ref)
        sum_ref[...] = jnp.zeros_like(sum_ref)
        total_ref[...] = jnp.zeros_like(total_ref)

    dh = (dv_ref[...].astype(F32) * s_ref[...].astype(F32)).astype(BF)
    total_ref[...] += mm(dh, n_ref[...], 1, 0)
    for k in range(dh.shape[1] // 128):
        sum_ref[...] += dh[:, k * 128 : (k + 1) * 128].astype(F32)
    p = p_ref[...].astype(F32) + mm(dh.T, w_ref[...], 1, 0)
    hat, _ = hat_of(tok_ref[...])
    gain_ref[...] += col_sum(p * hat)
    bias_ref[...] += col_sum(p)

    @pl.when(m == pl.num_programs(0) - 1)
    def _():
        grad_ref[...] = total_ref[...].T.astype(BF)

    @pl.when(m < pl.num_programs(0) // 2)
    def _():
        pm_ref[...] = p

    @pl.when(m >= pl.num_programs(0) // 2)
    def _():
        po_ref[...] = p.astype(BF)


def tail_call(core, dv, slope, w_turned, p, tok, normed):
    chans, tokens = dv.shape
    width = p.shape[1]
    rows, cols = (TILE, width), (chans, TILE)
    return call(
        tail_kernel,
        tokens // TILE,
        core,
        [
            (dv, cols, col_tile),
            (slope, cols, col_tile),
            (w_turned, (chans, width), fixed),
            (p, rows, row_tile),
            (tok, rows, row_tile),
            (normed, rows, row_tile),
        ],
        [
            ((width, chans), BF, (width, chans), fixed),
            ((tokens // 2, width), F32, rows, first_rows),
            ((tokens // 2, width), BF, rows, last_rows),
            ((1, width), F32, (1, width), fixed),
            ((1, width), F32, (1, width), fixed),
            ((chans, 128), F32, (chans, 128), fixed),
        ],
        "tail",
        ROOM,
        [pltpu.VMEM((chans, width), F32)],
    )


def input_kernel(_, mine_ref, got_ref, tok_ref, g_ref, gain_ref, out_ref):
    hat, inv_std = hat_of(tok_ref[...])
    grad = (mine_ref[...] + got_ref[...].astype(F32)) * gain_ref[...]
    out_ref[...] = (
        g_ref[...].astype(F32)
        + inv_std
        * (
            grad
            - jnp.mean(grad, axis=-1, keepdims=True)
            - hat * jnp.mean(grad * hat, axis=-1, keepdims=True)
        )
    ).astype(BF)


def input_call(core, mine, got, tok, g, gain):
    tokens, width = mine.shape
    rows = (256, width)
    return call(
        input_kernel,
        tokens // 256,
        core,
        [(x, rows, row_tile) for x in (mine, got, tok, g)] + [(gain, (1, width), fixed)],
        [((tokens, width), BF, rows, row_tile)],
        "input_grad",
        ROOM,
    )[0]

def keep_and_send(here, out_ref, runs, keep_ref, send_refs):
    for k, ref in enumerate((keep_ref, *send_refs)):
        part = jnp.concatenate(
            [
                out_ref[pl.ds(pl.multiple_of((at + (here ^ k)) * runs, runs), runs), :]
                for at in range(0, out_ref.shape[0] // runs, 4)
            ],
            axis=0,
        )
        ref[...] = part.astype(ref.dtype)


def grad_kernel(here_ref, a_ref, b_ref, keep_ref, s1_ref, s2_ref, s3_ref, out_ref, *, runs):
    out_ref[...] = mm(a_ref[...], b_ref[...], 0, 0)
    keep_and_send(here_ref[0], out_ref, runs, keep_ref, (s1_ref, s2_ref, s3_ref))


def grad_call(here, a, b, runs, tile, name):
    rows, cols = a.shape[1], b.shape[1]
    part, shape = (tile // 4, cols), (rows // 4, cols)
    return call(
        functools.partial(grad_kernel, runs=runs),
        rows // tile,
        here,
        [(a, (a.shape[0], tile), col_tile), (b, b.shape, fixed)],
        [(shape, kind, part, row_tile) for kind in (F32, BF, BF, BF)],
        name,
        ROOM,
        [pltpu.VMEM((tile, cols), F32)],
    )


def mixed_grad_kernel(here_ref, ym_ref, yo_ref, b_ref, keep_ref, s1_ref, s2_ref, s3_ref, out_ref, *, runs):
    half, rows = b_ref.shape[0] // 2, ym_ref.shape[0]
    out_ref[:rows] = mm(ym_ref[...], b_ref[...], 1, 0)
    out_ref[rows:] = mm(yo_ref[:, half:], b_ref[:half], 1, 0) + mm(
        yo_ref[:, :half], b_ref[half:], 1, 0
    )
    keep_and_send(here_ref[0], out_ref, runs, keep_ref, (s1_ref, s2_ref, s3_ref))


def mixed_grad_call(here, y_mine, y_other, b, runs, name):
    rows, cols, tile = 2 * y_mine.shape[0], b.shape[1], 512
    part, shape = (rows // 4, tile), (rows // 4, cols)
    return call(
        functools.partial(mixed_grad_kernel, runs=runs),
        cols // tile,
        here,
        [(y_mine, y_mine.shape, fixed), (y_other, y_other.shape, fixed), (b, (b.shape[0], tile), col_tile)],
        [(shape, kind, part, col_tile) for kind in (F32, BF, BF, BF)],
        name,
        ROOM,
        [pltpu.VMEM((rows, tile), F32)],
    )


def after(x, *others):
    return lax.optimization_barrier((x,) + others)[0]


def swap_cores(x):
    return lax.ppermute(x, "fsdp", SWAP)


def across(x, size, flip):
    return lax.ppermute(x, "dp", [(i, i ^ flip) for i in range(size)])


def bit_of(bit):
    return (lax.axis_index("dp") >> bit) & 1


def gather_bits(x, size, order, layout):
    have = []
    for bit in order:
        other = across(x, size, 1 << bit)
        mine = bit_of(bit) == 1
        have = [b for b in layout if b in have or b == bit]
        x = jnp.stack(
            [jnp.where(mine, other, x), jnp.where(mine, x, other)], axis=have.index(bit)
        )
    return x


def scatter_bits(x, size, order, layout, send_type):
    have = list(layout)
    for bit in order:
        axis = have.index(bit)
        mine = bit_of(bit)
        theirs = lax.dynamic_index_in_dim(x, 1 - mine, axis, keepdims=False)
        kept = lax.dynamic_index_in_dim(x, mine, axis, keepdims=False)
        x = kept.astype(F32) + across(theirs.astype(send_type), size, 1 << bit).astype(F32)
        have.remove(bit)
    return x


def per_device(
    size,
    tokens,
    cotangent,
    lengths,
    norm_gain,
    norm_bias,
    w_one,
    b_one,
    w_two,
    b_two,
    w_three,
    b_three,
    w_four,
    b_four,
    log_rate,
    ssm_coeff,
    ssm_skip,
):
    bits = size.bit_length() - 1
    tok_dev, width = tokens.shape
    rows_e, rows_f, rows_h = w_one.shape[0], w_four.shape[0], w_three.shape[0]
    f_half, h_half = size * rows_f, size * rows_h
    buckets = lengths.shape[0]
    group = size // buckets
    group_bits = group.bit_length() - 1
    chans = buckets * rows_h
    tok_chip = 2 * tok_dev
    per_dev = tok_dev // QBLK
    nstate = log_rate.shape[1]
    natural = list(range(bits))[::-1]
    by_owner = natural[bits - group_bits :] + natural[: bits - group_bits]
    top = natural[: bits - group_bits]
    order_a = list(range(2, bits)) + [0, 1]
    order_b = list(range(2, bits)) + [1, 0]
    core = lax.axis_index("fsdp")
    first = core == 0
    chip = lax.axis_index("dp")
    core_at = jnp.reshape(core, (1,)).astype(jnp.int32)
    everyone = ("dp", "fsdp")

    def natural_pair(mine, other, axis=0):
        return jnp.stack(
            [jnp.where(first, mine, other), jnp.where(first, other, mine)], axis=axis
        )

    def mine_other(parts, axis):
        a = lax.index_in_dim(parts, 0, axis, keepdims=False)
        b = lax.index_in_dim(parts, 1, axis, keepdims=False)
        return jnp.where(first, a, b), jnp.where(first, b, a)

    tok_pair = jnp.concatenate([tokens, swap_cores(tokens)], axis=0)
    cot_pair = jnp.concatenate([cotangent, swap_cores(cotangent)], axis=0)

    two_parts = jnp.moveaxis(
        w_two.reshape(rows_e, buckets, group, 2, rows_h), (3, 2, 1), (0, 2, 3)
    ).reshape(2, rows_e, h_half)
    vec = jnp.concatenate([norm_gain, norm_bias, b_four, b_one, b_three, b_two])
    vec_len = vec.shape[0]
    vec_rows = -(-vec_len // h_half)
    vec = jnp.pad(vec, (0, vec_rows * h_half - vec_len)).reshape(1, vec_rows, h_half)
    small = jnp.concatenate(
        [two_parts, jnp.broadcast_to(vec, (2, vec_rows, h_half))], axis=1
    )
    small = jnp.broadcast_to(small[None], (size, 2) + small.shape[1:])
    small = lax.all_to_all(
        small.reshape((2 * size,) + small.shape[2:]), everyone, split_axis=0, concat_axis=0
    )
    two_turned = small[:, :rows_e].reshape(width, h_half).T
    vecs = small[:, rows_e:].reshape(2 * size, -1)[:, :vec_len].astype(F32)
    gain_f = vecs[:, :rows_e].reshape(1, width)
    nbias_f = vecs[:, rows_e : 2 * rows_e].reshape(1, width)
    bfour_f = vecs[:, 2 * rows_e : 3 * rows_e].reshape(1, width)
    own_vecs, _ = mine_other(vecs.reshape(size, 2, vec_len)[:, :, 3 * rows_e :], 1)
    bone_f = own_vecs[:, :rows_f].reshape(1, f_half)
    bthree_f = own_vecs[:, rows_f : 2 * rows_f].reshape(1, f_half)
    btwo_f = (
        own_vecs[:, 2 * rows_f :].reshape(buckets, group, rows_h).swapaxes(0, 1).reshape(h_half, 1)
    )

    strip = 512
    f_strips, e_strips = f_half // strip, width // strip

    def by_half(x):
        rows = x.shape[0]
        parts = jnp.moveaxis(x.reshape(rows, size, 2, rows_f), 2, 0).reshape(2, rows, f_half)
        parts = jnp.moveaxis(parts.reshape(2, rows, f_strips, strip), 2, 1)
        return parts.reshape(2 * f_strips * rows, strip)

    packed = jnp.concatenate(
        [w_four[:, k * strip : (k + 1) * strip] for k in range(e_strips)]
        + [by_half(w_one), by_half(w_three)],
        axis=0,
    )
    gathered = lax.all_gather(packed, everyone, axis=0)
    four_end = e_strips * rows_f
    one_end = four_end + 2 * f_strips * rows_e
    gathered = gathered.reshape(size, 2, -1, strip)
    one_rows, three_rows = f_strips * rows_e, f_strips * rows_h

    def block(chips, cores, rows):
        return (chips, cores, rows, strip)

    if rows_h % 16 == 0 and four_end % one_rows == 0 and one_end % three_rows == 0:
        one_at, three_at = four_end // one_rows, one_end // three_rows
        order = [b * group + j for j in range(group) for b in range(buckets)]
        weights = [
            (gathered, block(size, 2, one_rows), lambda m, c: (0, 0, one_at + c[0], 0)),
            (gathered, block(size, 1, four_end), lambda m, c: (0, c[0], 0, 0)),
            (gathered, block(size, 1, three_rows), lambda m, c: (0, c[0], three_at + c[0], 0)),
            (gathered, block(size, 1, three_rows), lambda m, c: (0, 1 - c[0], three_at + c[0], 0)),
        ]
    else:
        order = [0]
        four_half = gathered[:, :, :four_end].reshape(size, 2, e_strips, rows_f, strip)
        four_half = lax.dynamic_index_in_dim(four_half, core, 1, keepdims=False).swapaxes(0, 1)
        one_half = gathered[:, :, four_end:one_end].reshape(2 * size, 2, f_strips, rows_e, strip)
        one_half = lax.dynamic_index_in_dim(one_half, core, 1, keepdims=False).swapaxes(0, 1)
        three_half = gathered[:, :, one_end:].reshape(
            buckets, group, 2, 2, f_strips, rows_h, strip
        )
        three_half = lax.dynamic_index_in_dim(three_half, core, 3, keepdims=False)
        three_half = jnp.transpose(three_half, (2, 3, 1, 0, 4, 5))
        three_half = mine_other(three_half, 0)
        weights = [
            (x.reshape(1, 1, -1, strip), block(1, 1, x.size // strip), lambda m, c: (0, 0, 0, 0))
            for x in (one_half, four_half, *three_half)
        ]

    params = gather_bits(
        jnp.concatenate(
            [log_rate, ssm_coeff, jnp.broadcast_to(ssm_skip[:, None], (rows_h, 128))], axis=1
        ),
        size,
        sorted(top),
        top,
    ).reshape(chans, 1, -1)
    mix_params = (
        params[..., :nstate],
        params[..., nstate : 2 * nstate],
        params[..., 2 * nstate :],
    )
    tables = mixer_tables(*mix_params[:2])
    groups = [[b * group + j for j in range(group)] for b in range(buckets)]

    def exchange(x):
        return lax.all_to_all(x, "dp", split_axis=0, concat_axis=0, axis_index_groups=groups)

    def to_owner(x):
        return exchange(x.reshape(group, chans, tok_chip))

    def from_owner(x):
        return exchange(x).reshape(h_half, tok_chip)

    def swap_turned(x):
        got = swap_cores(x)
        return jnp.concatenate([got[:, tok_dev:], got[:, :tok_dev]], axis=1)

    device = 2 * chip + core
    lane = jnp.arange(tok_dev, dtype=jnp.int32)
    place = jnp.concatenate([device * tok_dev + lane, (device ^ 1) * tok_dev + lane])
    bucket_range = jnp.arange(buckets, dtype=jnp.int32)
    limit = jnp.sum(
        jnp.where((place // SEQ)[:, None] == bucket_range[None, :], lengths[None, :], 0), axis=1
    )
    live = (place % SEQ < limit).astype(F32)[:, None]

    normed, out_grad, reduced_t, two_slope, out_sum = norm_call(
        core_at,
        tok_pair,
        cot_pair,
        jnp.broadcast_to(live, (tok_chip, 128)),
        gain_f,
        nbias_f,
        two_turned,
        jnp.broadcast_to(btwo_f, (h_half, 128)),
    )
    v_seq = to_owner(reduced_t)
    y_seq, entering = mixer_forward(core_at, v_seq, tables, mix_params)
    y_own = from_owner(y_seq)
    y_other = swap_cores(y_own)

    def small_pack(grad_two, gain_sum, nbias_sum, out_sum, one_sum, gate_sum, two_sum):
        def by_device(x):
            return x.reshape(2 * size, -1)

        def by_core(x):
            zero = jnp.zeros_like(x)
            return by_device(natural_pair(x, zero, axis=1))

        grad_btwo = (
            jnp.sum(two_sum, axis=1).reshape(group, buckets, rows_h).swapaxes(0, 1).reshape(size, rows_h)
        )
        vec_grads = jnp.concatenate(
            [
                by_device(gain_sum),
                by_device(nbias_sum),
                by_device(out_sum),
                by_core(one_sum.reshape(size, rows_f)),
                by_core(gate_sum.reshape(size, rows_f)),
                by_core(grad_btwo),
            ],
            axis=1,
        )
        vec_grads = jnp.pad(vec_grads, ((0, 0), (0, vec_rows * h_half - vec_len)))
        return jnp.concatenate(
            [
                grad_two.reshape(2 * size, rows_e, h_half).astype(BF),
                vec_grads.reshape(2 * size, vec_rows, h_half).astype(BF),
            ],
            axis=1,
        )

    act_one, dz_slope, gate_grad, dy_mine, dy_other, gate_sum = early_call(
        core_at, normed, out_grad, bone_f, weights, order
    )
    dy_own = (dy_mine + swap_cores(dy_other).astype(F32)).astype(BF)
    dy_seq = to_owner(dy_own)


    def send_off(sends, low):
        came = {k: across(sends[k - 1], size, k << low) for k in (3, 1, 2)}
        return [came[k] for k in (1, 2, 3)]

    def begin(outputs, have, rest):
        keep, *parts = (x.reshape((2,) * len(have) + rest) for x in outputs)
        return keep, send_off(parts, 0), have

    def split_off(state, low, *others):
        kept, came, have = state
        high = low + 1
        axis = min(have.index(high), have.index(low))
        swapped = have.index(low) < have.index(high)
        shape = kept.shape[:axis] + (4,) + kept.shape[axis + 2 :]
        terms = [kept.reshape(shape)] + [after(x, *others).reshape(shape) for x in came]
        here = (chip >> low) & 3

        def part(k):
            index = here ^ k
            index = ((index & 1) << 1) | (index >> 1) if swapped else index
            return sum(
                lax.dynamic_index_in_dim(x, index, axis, keepdims=False).astype(F32) for x in terms
            )

        return part(0), [part(k).astype(BF) for k in (1, 2, 3)], [b for b in have if b >> 1 != low >> 1]

    def go_on(state, low):
        kept, parts, have = state
        return kept, send_off(parts, low), have

    def to_last(state):
        for low in range(2, bits - 2, 2):
            state = go_on(split_off(state, low), low)
        return state

    def total(state, *others):
        kept, came, _ = state
        return sum((after(x, *others).astype(F32) for x in came), kept)

    here = jnp.reshape(chip & 3, (1,)).astype(jnp.int32)
    last = bits - 2
    far = size // 4
    far_groups = [[4 * g + k for g in range(far)] for k in range(4)]

    product, one_grad, one_sum = gate_call(
        core_at, after(y_own, dy_own), y_other, bthree_f, act_one, dz_slope, weights, order
    )
    grad_four = grad_call(here, product, out_grad, rows_f, 384, "grad_four")
    four = begin(grad_four, natural[:-2], (rows_f, width))
    dv_seq, grad_rate, grad_coeff, grad_skip = mixer_backward(
        core_at, v_seq, after(dy_seq, grad_four[0]), entering, tables, mix_params
    )
    dv_own = from_owner(dv_seq)
    grad_three = mixed_grad_call(
        here, y_own, y_other, after(gate_grad, dv_seq), buckets * rows_h, "grad_three"
    )
    grad_one = grad_call(
        here, normed, after(one_grad, grad_three[0]), 2 * rows_e, 256, "grad_one"
    )

    def stacked(one, three):
        three = three.reshape(2, group // 4, buckets, rows_h, f_half)
        three = jnp.moveaxis(three, (2, 1), (0, 1)).reshape(far, 2 * rows_h, f_half)
        return jnp.concatenate([one.reshape(far, 2 * rows_e, f_half), three], axis=1)

    rest = begin(
        [stacked(x, y) for x, y in zip(grad_one, grad_three)],
        natural[:-2],
        (2 * rows_e + 2 * rows_h, f_half),
    )
    four_parts = total(four, grad_one[0]).astype(BF).reshape(far, rows_f, width)
    four_got = lax.all_to_all(
        after(four_parts, dv_own), "dp", split_axis=0, concat_axis=0, axis_index_groups=far_groups
    )
    out_mine, out_other, one_back = out_call(
        core_at, product, after(one_grad, grad_one[0], dv_own, four_parts), width, weights
    )
    out_got = swap_cores(out_other)
    sum_four = jnp.sum(after(four_got, one_back).astype(F32), axis=0)

    grad_two, back_mine, back_other, gain_sum, nbias_sum, two_sum = tail_call(
        core_at,
        after(dv_own, sum_four),
        two_slope,
        two_turned,
        one_back,
        tok_pair,
        normed,
    )
    mix_grads = jnp.concatenate([grad_rate[:, 0], grad_coeff[:, 0], grad_skip[:, 0]], axis=1)
    mix_grads = scatter_bits(
        mix_grads.reshape((2,) * len(top) + (rows_h, -1)), size, sorted(top)[::-1], top, F32
    )
    back_got = swap_cores(back_other)
    rest = split_off(to_last(rest), last, grad_two)
    rest_sent = rest[1]
    rest = go_on(rest, last)
    small_grads = small_pack(after(grad_two, *rest_sent), gain_sum, nbias_sum, out_sum, one_sum, gate_sum, two_sum)
    small_got = lax.all_to_all(
        small_grads, everyone, split_axis=0, concat_axis=0
    )
    input_grad = input_call(
        core_at, back_mine, after(back_got, small_grads), tokens, out_grad, gain_f
    )


    def merge_f(mine, other):
        rows = mine.shape[0]
        parts = (mine.reshape(rows, size, rows_f), other.reshape(rows, size, rows_f))
        return natural_pair(*parts, axis=2).reshape(rows, 2 * f_half)

    branch = out_mine + after(out_got, small_grads).astype(F32)
    mixed = (live[:tok_dev] * (tokens.astype(F32) + branch + bfour_f)).astype(BF)
    rest_sum = total(rest, input_grad, mixed)
    one_mine, one_other = mine_other(rest_sum[: 2 * rows_e].reshape(2, rows_e, f_half), 0)
    three_sum = rest_sum[2 * rows_e :]
    rest_got = swap_cores(jnp.concatenate([one_other, three_sum[rows_h:]], axis=0))
    merged = merge_f(jnp.concatenate([one_mine, three_sum[:rows_h]], axis=0), rest_got)
    sum_one, sum_three = merged[:rows_e], merged[rows_e:]

    small_sum = jnp.sum(
        after(small_got, input_grad).reshape(size, 2, rows_e + vec_rows, h_half).astype(F32), axis=0
    )
    sum_two = jnp.transpose(
        small_sum[:, :rows_e].reshape(2, rows_e, group, buckets, rows_h), (1, 3, 2, 0, 4)
    ).reshape(rows_e, 2 * h_half)
    vec_sum = jnp.sum(small_sum[:, rows_e:], axis=0).reshape(-1)
    ends = [rows_e, 2 * rows_e, 3 * rows_e, 3 * rows_e + rows_f, 3 * rows_e + 2 * rows_f, vec_len]
    sum_gain, sum_nbias, sum_bfour, sum_bone, sum_bthree, sum_btwo = (
        vec_sum[a:b] for a, b in zip([0] + ends, ends)
    )

    return (
        mixed,
        input_grad,
        sum_gain,
        sum_nbias,
        sum_one,
        sum_bone,
        sum_two,
        sum_btwo,
        sum_three,
        sum_bthree,
        sum_four,
        sum_bfour,
        mix_grads[:, :nstate],
        mix_grads[:, nstate : 2 * nstate],
        mix_grads[:, 2 * nstate],
    )


def solution(mesh):
    both = ("dp", "fsdp")
    rows, vector = P(both, None), P(both)
    in_specs = (
        rows, rows, P(), vector, vector, rows, vector, rows, vector, rows, vector, rows, vector,
        rows, rows, vector,
    )
    out_specs = (
        rows, rows, vector, vector, rows, vector, rows, vector, rows, vector, rows, vector,
        rows, rows, vector,
    )
    return jax.shard_map(
        functools.partial(per_device, mesh.shape["dp"]),
        mesh=mesh,
        in_specs=in_specs,
        out_specs=out_specs,
        check_vma=False,
    )
```
